512 devices in a mesh: row: 32 (over x, y, core), col: 16 (over z).
Axes of the slice: x: 4, y: 4, z: 16, core: 2. Of those that a mesh axis runs over, the one named last changes fastest.
Arguments:
- user_embed: bfloat16 [16384, 256], P('row')
- item_embed: bfloat16 [16384, 256], P('col')
- positive: int32 [16384], P('row'), may hold values from 0 to 16383
- user_count: int32 [16384], P('row'), may hold values from 1 to 999
- item_count: int32 [16384], P('col'), may hold values from 1 to 999
Outputs:
- user_grad: float32 [16384, 256], P('row')
- item_grad: float32 [16384, 256], P('col')
- mean_loss: float32 [], replicated
The draws below stay inside these ranges and needn't reach their ends.
All inputs are finite; a program needn't handle non-finite values.
Results may differ from the reference program's by a relative error of at most 0.0019.
Values sent between devices are 32-bit elements; how exact they have to be, the bound alone decides.
A program may use at most 64 MiB of HBM per device.

```python
import jax
import jax.numpy as jnp
from jax import lax

D = 256
USERS = 16384
ITEMS = 16384


def base_items(key):
    items = 0.35 * jax.random.normal(key, (ITEMS, D), jnp.float32)
    group_index = jnp.arange(USERS // 64, dtype=jnp.int32)
    targets = 2 * (group_index * 37 % (ITEMS // 2))
    flagged = jnp.zeros((ITEMS,), jnp.int32).at[targets + 1].set(1)
    return jnp.where(flagged[:, None] > 0, 1.006 * jnp.roll(items, 1, axis=0), items)


def aligned_users(key, users, low, spread):
    items = base_items(key)
    user_index = jnp.arange(USERS, dtype=jnp.int32)
    aligned = user_index % 64 < 2
    target = 2 * (user_index // 64 * 37 % (ITEMS // 2))
    pick = jax.random.uniform(jax.random.fold_in(key, 11), (USERS,), jnp.float32)
    level = low + spread * pick
    strength = level / (0.49 * D * 1.003)
    aligned_rows = strength[:, None] * (items[target] + items[target + 1])
    return jnp.where(aligned[:, None], aligned_rows, users)


def draw_item_embed(key, part):
    return base_items(key).astype(jnp.bfloat16)


def draw_user_embed(key, part):
    own_key = jax.random.fold_in(key, 3)
    users = 0.35 * jax.random.normal(own_key, (USERS, D), jnp.float32)
    users = aligned_users(key, users, 150.0, 250.0)
    return users.astype(jnp.bfloat16)


def with_ends(entries, stream_key, low, high):
    extent = entries.shape
    place = [jax.random.randint(jax.random.fold_in(stream_key, axis), (), 0, extent[axis]) for axis in range(len(extent))]
    entries = entries.at[tuple(place)].set(low)
    longest = extent.index(max(extent))
    place[longest] = (place[longest] + 1) % extent[longest]
    return entries.at[tuple(place)].set(high)


def setup_inputs(seed: int = 0) -> dict:
    arg_keys = jax.random.split(jax.random.key(seed), 6)
    return {
        "user_embed": draw_user_embed(jax.random.fold_in(arg_keys[5], 71), 0),
        "item_embed": draw_item_embed(jax.random.fold_in(arg_keys[5], 71), 0),
        "positive": with_ends(jax.random.randint(arg_keys[2], (USERS,), 0, ITEMS), jax.random.fold_in(arg_keys[2], 1), 0, ITEMS - 1).astype(jnp.int32),
        "user_count": with_ends(jax.random.randint(arg_keys[3], (USERS,), 1, 1000), jax.random.fold_in(arg_keys[3], 1), 1, 999).astype(jnp.int32),
        "item_count": with_ends(jax.random.randint(arg_keys[4], (ITEMS,), 1, 1000), jax.random.fold_in(arg_keys[4], 1), 1, 999).astype(jnp.int32),
    }


def reference(user_embed, item_embed, positive, user_count, item_count):
    block_rows = min(1024, USERS)
    count_blocks = USERS // block_rows
    log_item = jnp.log(item_count.astype(jnp.float32))
    log_user = jnp.log(user_count.astype(jnp.float32))
    columns = jnp.arange(ITEMS, dtype=jnp.int32)
    user_blocks = user_embed.reshape(count_blocks, block_rows, D)
    log_blocks = log_user.reshape(count_blocks, block_rows)
    pos_blocks = positive.reshape(count_blocks, block_rows).astype(jnp.int32)

    def scores_of(user_block):
        prod = lax.dot_general(user_block, item_embed, (((1,), (1,)), ((), ())), preferred_element_type=jnp.float32)
        return prod * 2.0

    def first(carry, inputs):
        col_max, col_sum, pos_hits = carry
        user_block, user_log, pos_block = inputs
        scores = scores_of(user_block)
        shifted = scores - log_item[None, :]
        row_max = jnp.max(shifted, axis=1)
        row_sum = jnp.sum(jnp.exp(shifted - row_max[:, None]), axis=1)
        matches = pos_block[:, None] == columns[None, :]
        z_shift = jnp.sum(jnp.where(matches, shifted, 0.0), axis=1)
        z_raw = jnp.sum(jnp.where(matches, scores, 0.0), axis=1)
        col_term = scores - user_log[:, None]
        new_max = jnp.maximum(col_max, jnp.max(col_term, axis=0))
        col_sum = col_sum * jnp.exp(col_max - new_max) + jnp.sum(jnp.exp(col_term - new_max[None, :]), axis=0)
        pos_hits = pos_hits + jnp.sum(matches.astype(jnp.float32), axis=0)
        return (new_max, col_sum, pos_hits), (row_max, row_sum, z_shift, z_raw)

    start = (jnp.full((ITEMS,), -1e30, jnp.float32), jnp.zeros((ITEMS,), jnp.float32), jnp.zeros((ITEMS,), jnp.float32))
    (col_max, col_sum, pos_hits), (row_max, row_sum, z_shift, z_raw) = lax.scan(first, start, (user_blocks, log_blocks, pos_blocks))
    row_lse = row_max + jnp.log(row_sum)
    col_lse = col_max + jnp.log(col_sum)
    total_loss = jnp.sum(row_lse - z_shift - z_raw + log_blocks) + jnp.sum(pos_hits * col_lse)
    mean_loss = total_loss / USERS

    def second(item_acc, inputs):
        user_block, user_log, pos_block, lse_block = inputs
        scores = scores_of(user_block)
        matches = (pos_block[:, None] == columns[None, :]).astype(jnp.float32)
        row_part = jnp.exp(scores - log_item[None, :] - lse_block[:, None])
        col_part = pos_hits[None, :] * jnp.exp(scores - user_log[:, None] - col_lse[None, :])
        coupling = (row_part + col_part - 2.0 * matches).astype(jnp.bfloat16)
        user_part = jnp.dot(coupling, item_embed, preferred_element_type=jnp.float32) * 2.0
        item_part = lax.dot_general(coupling, user_block, (((0,), (0,)), ((), ())), preferred_element_type=jnp.float32) * 2.0
        return item_acc + item_part, user_part

    item_grad, user_parts = lax.scan(second, jnp.zeros((ITEMS, D), jnp.float32), (user_blocks, log_blocks, pos_blocks, row_lse))
    return user_parts.reshape(USERS, D), item_grad, mean_loss
```

```python
import functools

import jax
import jax.numpy as jnp
from jax import lax
from jax.experimental import pallas as pl
from jax.experimental.pallas import tpu as pltpu
from jax.sharding import PartitionSpec as P

MESH = pl.DeviceIdType.MESH
LANES = 128
BLOCK = 128
F32 = jnp.float32


def columns_of(row):
    return jnp.transpose(jnp.broadcast_to(row, (LANES, LANES)))


def fold(block):
    return block.reshape(block.shape[0] // 8, 8, LANES)


def merged_lse(parts):
    top = jnp.max(parts, axis=0)
    return top + jnp.log(jnp.sum(jnp.exp(parts - top[None]), axis=0))


def kernel(
    total_users,
    chips,
    rings,
    user_ref,
    item_ref,
    pos_ref,
    ucnt_ref,
    icnt_ref,
    ug_ref,
    ig_ref,
    loss_ref,
    scores,
    coupling,
    part,
    items,
    log_item,
    lu_col,
    pos_col,
    row_col,
    col_max,
    col_sum,
    hits_acc,
    z_stats,
    c_stats,
    p_stats,
    z_loss,
    plus_in,
    minus_in,
    core_in,
    plane_out,
    plane_in,
    z_sems,
    c_sems,
    p_sems,
    l_sems,
    plus_sems,
    minus_sems,
    gplus_sems,
    gminus_sems,
    x_sems,
):
    rows_here, width = user_ref.shape
    cols_here = item_ref.shape[0]
    tiles = cols_here // LANES
    row_tiles = rows_here // LANES
    half_cols = cols_here // 2
    half_tiles = tiles // 2
    blocks = rows_here // BLOCK
    chunk = rows_here // rings
    piece = half_cols // chips
    half = rings // 2

    mine = lax.axis_index("row")
    ring = lax.axis_index("col")
    chip = mine // 2
    core = mine % 2
    other = 1 - core
    twin = chip * 2 + other

    def z_peer(step):
        return (mine, (ring + step) % rings)

    def chip_peer(step):
        return (((chip + step) % chips) * 2 + core, ring)

    z_steps = sorted(range(1, rings), key=lambda k: -min(k, rings - k))
    chip_steps = list(range(1, chips))

    barrier = pltpu.get_barrier_semaphore()
    for step in z_steps:
        pl.semaphore_signal(barrier, inc=1, device_id=z_peer(step), device_id_type=MESH)
    for step in chip_steps:
        pl.semaphore_signal(barrier, inc=1, device_id=chip_peer(step), device_id_type=MESH)
    pl.semaphore_signal(barrier, inc=1, device_id=(twin, ring), device_id_type=MESH)

    def remote(src, dst, send_sem, recv_sem, device):
        return pltpu.make_async_remote_copy(
            src_ref=src,
            dst_ref=dst,
            send_sem=send_sem,
            recv_sem=recv_sem,
            device_id=device,
            device_id_type=MESH,
        )

    def wait_bytes(ref, sem):
        pltpu.make_async_copy(ref, ref, sem).wait()

    log_item[...] = jnp.log(icnt_ref[...].astype(F32))
    log_user = jnp.log(ucnt_ref[...].astype(F32))
    local_pos = pos_ref[...].astype(F32) - (ring * cols_here).astype(F32)
    for k in range(row_tiles):
        span = pl.ds(k * LANES, LANES)
        lu_col[span, :] = columns_of(log_user[k : k + 1, :])
        pos_col[span, :] = columns_of(local_pos[k : k + 1, :])
    col_max[...] = jnp.full(col_max.shape, -jnp.inf, F32)
    col_sum[...] = jnp.zeros(col_sum.shape, F32)
    hits_acc[...] = jnp.zeros(hits_acc.shape, F32)
    lane = lax.broadcasted_iota(jnp.int32, (BLOCK, LANES), 1).astype(F32)

    def sweep_one(b, z_part):
        span = pl.ds(pl.multiple_of(b * BLOCK, BLOCK), BLOCK)
        scores[span, :] = 2.0 * lax.dot_general(
            user_ref[span, :],
            item_ref[...],
            (((1,), (1,)), ((), ())),
            preferred_element_type=F32,
        )
        lu = lu_col[span, :]
        pos = pos_col[span, :]
        top = None
        for t in range(tiles):
            s = scores[span, t * LANES : (t + 1) * LANES]
            shifted = s - log_item[t : t + 1, :]
            top = shifted if top is None else jnp.maximum(top, shifted)
            col_max[t] = jnp.maximum(col_max[t], jnp.max(fold(s - lu), axis=0))
            match = pos == lane + float(t * LANES)
            hits_acc[t] += jnp.sum(fold(jnp.where(match, 1.0, 0.0)), axis=0)
            z_part = z_part + jnp.sum(fold(jnp.where(match, s + shifted, 0.0)), axis=0)
        row_col[span, :] = jnp.broadcast_to(jnp.max(top, axis=1, keepdims=True), (BLOCK, LANES))
        return z_part

    z_part = lax.fori_loop(0, blocks, sweep_one, jnp.zeros((8, LANES), F32))
    for t in range(tiles):
        col_max[t] = jnp.broadcast_to(jnp.max(col_max[t], axis=0, keepdims=True), (8, LANES))

    z_stats[ring] = jnp.zeros((8, LANES), F32)

    def sweep_two(b, carry):
        span = pl.ds(pl.multiple_of(b * BLOCK, BLOCK), BLOCK)
        lu = lu_col[span, :]
        row_max = row_col[span, :]
        total = jnp.zeros((BLOCK, LANES), F32)
        for t in range(tiles):
            s = scores[span, t * LANES : (t + 1) * LANES]
            total = total + jnp.exp(s - log_item[t : t + 1, :] - row_max)
            col = jnp.exp(fold(s - lu) - col_max[t][None])
            col_sum[t] += jnp.sum(col, axis=0)
        lse = row_max + jnp.log(jnp.sum(total, axis=1, keepdims=True))
        z_stats[ring, pl.ds(b, 1), :] = jnp.transpose(lse)[0:1, :]
        return carry

    lax.fori_loop(0, blocks, sweep_two, 0)
    z_stats[ring, pl.ds(row_tiles, 1), :] = jnp.sum(z_part, axis=0, keepdims=True)
    col_lse_rows = []
    hits_rows = []
    for t in range(tiles):
        total = jnp.sum(col_sum[t], axis=0, keepdims=True)
        col_lse_rows.append(col_max[t, 0:1, :] + jnp.log(total))
        hits_rows.append(jnp.sum(hits_acc[t], axis=0, keepdims=True))
    c_stats[0] = jnp.concatenate(col_lse_rows + hits_rows, axis=0)

    pl.semaphore_wait(barrier, rings - 1 + chips - 1 + 1)
    core_stat = remote(c_stats.at[0], c_stats.at[1], c_sems.at[0], c_sems.at[1], (twin, ring))
    core_stat.start()
    for step in z_steps:
        remote(
            z_stats.at[ring], z_stats.at[ring], z_sems.at[0], z_sems.at[1], z_peer(step)
        ).start()
    core_stat.wait()
    one, two = c_stats[0], c_stats[1]
    p_stats[chip, 0:tiles, :] = merged_lse(jnp.stack([one[:tiles], two[:tiles]]))
    p_stats[chip, tiles : 2 * tiles, :] = one[tiles:] + two[tiles:]
    for step in chip_steps:
        remote(
            p_stats.at[chip], p_stats.at[chip], p_sems.at[0], p_sems.at[1], chip_peer(step)
        ).start()
    wait_bytes(z_stats.at[pl.ds(0, rings - 1)], z_sems.at[1])
    user_stats = z_stats[...]
    row_lse = merged_lse(user_stats[:, :row_tiles])
    for k in range(row_tiles):
        row_col[pl.ds(k * LANES, LANES), :] = columns_of(row_lse[k : k + 1, :])
    user_loss = jnp.sum(row_lse + log_user, axis=0, keepdims=True) - jnp.sum(
        user_stats[:, row_tiles : row_tiles + 1], axis=0
    )
    wait_bytes(p_stats.at[pl.ds(0, chips - 1)], p_sems.at[1])
    item_stats = p_stats[...]
    col_lse = merged_lse(item_stats[:, :tiles])
    pos_hits = jnp.sum(item_stats[:, tiles:], axis=0)
    z_loss[ring] = jnp.broadcast_to(
        jnp.sum(pos_hits * col_lse, axis=0, keepdims=True), (8, LANES)
    )

    def sweep_three(b, carry):
        span = pl.ds(pl.multiple_of(b * BLOCK, BLOCK), BLOCK)
        lu = lu_col[span, :]
        pos = pos_col[span, :]
        row = row_col[span, :]
        for t in range(tiles):
            s = scores[span, t * LANES : (t + 1) * LANES]
            value = jnp.exp(s - log_item[t : t + 1, :] - row) + pos_hits[t : t + 1, :] * jnp.exp(
                s - lu - col_lse[t : t + 1, :]
            )
            match = pos == lane + float(t * LANES)
            value = value - jnp.where(match, 2.0, 0.0)
            place = (t % half_tiles) * LANES
            coupling[t // half_tiles, span, place : place + LANES] = value.astype(jnp.bfloat16)
        part[span, :] = 2.0 * (
            jnp.dot(coupling[0, span, :], item_ref[:half_cols, :], preferred_element_type=F32)
            + jnp.dot(coupling[1, span, :], item_ref[half_cols:, :], preferred_element_type=F32)
        )
        return carry

    lax.fori_loop(0, blocks, sweep_three, 0)

    def chunk_at(index):
        return pl.ds(pl.multiple_of(index % rings * chunk, chunk), chunk)

    up = z_peer(1)
    down = z_peer(rings - 1)

    def reduce_step(step):
        if step < half:
            span = chunk_at(ring + half - step)
            if step == 0:
                src = part.at[span, :]
            else:
                src = plus_in.at[step - 1]
                wait_bytes(src, plus_sems.at[1, step - 1])
                plus_in[step - 1] += part[span, :]
            remote(
                src, plus_in.at[step], plus_sems.at[0, step], plus_sems.at[1, step], up
            ).start()
        if step < half - 1:
            span = chunk_at(ring + rings - (half - 1) + step)
            if step == 0:
                src = part.at[span, :]
            else:
                src = minus_in.at[step - 1]
                wait_bytes(src, minus_sems.at[1, step - 1])
                minus_in[step - 1] += part[span, :]
            remote(
                src, minus_in.at[step], minus_sems.at[0, step], minus_sems.at[1, step], down
            ).start()

    def reduce_end():
        wait_bytes(minus_in.at[half - 2], minus_sems.at[1, half - 2])
        wait_bytes(plus_in.at[half - 1], plus_sems.at[1, half - 1])
        span = chunk_at(ring)
        ug_ref[span, :] = part[span, :] + plus_in[half - 1] + minus_in[half - 2]

    def gather_step(step):
        if step < half:
            if step > 0:
                span = chunk_at(ring + rings - step)
                wait_bytes(ug_ref.at[span, :], gplus_sems.at[1, step - 1])
            span = chunk_at(ring + rings - step)
            here = ug_ref.at[span, :]
            remote(here, here, gplus_sems.at[0, step], gplus_sems.at[1, step], up).start()
        if step < half - 1:
            span = chunk_at(ring + step)
            here = ug_ref.at[span, :]
            if step > 0:
                wait_bytes(here, gminus_sems.at[1, step - 1])
            remote(here, here, gminus_sems.at[0, step], gminus_sems.at[1, step], down).start()

    def gather_end():
        wait_bytes(ug_ref.at[chunk_at(ring + half), :], gplus_sems.at[1, half - 1])
        wait_bytes(ug_ref.at[chunk_at(ring + half - 1), :], gminus_sems.at[1, half - 2])

    def item_part(which):
        items[which, :half_cols, :] = 2.0 * lax.dot_general(
            coupling[which],
            user_ref[...],
            (((0,), (0,)), ((), ())),
            preferred_element_type=F32,
        )

    core_copy = remote(items.at[other], core_in, x_sems.at[0], x_sems.at[1], (twin, ring))

    def core_send():
        item_part(other)
        items[other, half_cols:, :LANES] = jnp.broadcast_to(user_loss, (8, LANES))
        items[other, half_cols:, LANES:] = jnp.zeros((8, width - LANES), F32)
        core_copy.start()

    def loss_send():
        for step in z_steps:
            remote(
                z_loss.at[ring], z_loss.at[ring], l_sems.at[0], l_sems.at[1], z_peer(step)
            ).start()

    def plane_send():
        core_copy.wait_recv()
        pair_loss = core_in[half_cols:, :LANES] + user_loss

        def pack(k, carry):
            span = pl.ds(pl.multiple_of(k * piece, piece), piece)
            plane_out[k, :piece, :] = items[core, span, :] + core_in[span, :]
            plane_out[k, piece:, :LANES] = pair_loss
            plane_out[k, piece:, LANES:] = jnp.zeros((8, width - LANES), F32)
            return carry

        lax.fori_loop(0, chips, pack, 0)
        for step in chip_steps:
            remote(
                plane_out.at[(chip + step) % chips],
                plane_in.at[chip],
                x_sems.at[2],
                x_sems.at[3],
                chip_peer(step),
            ).start()
        plane_in[chip] = plane_out[chip]

    def piece_at(half_index, index):
        return pl.ds(pl.multiple_of(half_index * half_cols + index * piece, piece), piece)

    def plane_sum():
        wait_bytes(plane_in.at[pl.ds(0, chips - 1)], x_sems.at[3])
        total = plane_in[0]
        for k in range(1, chips):
            total = total + plane_in[k]
        here = ig_ref.at[piece_at(core, chip), :]
        here[...] = total[:piece, :]
        for step in chip_steps:
            remote(here, here, x_sems.at[4], x_sems.at[5], chip_peer(step)).start()
        return total[piece : piece + 1, :LANES]

    half_here = ig_ref.at[pl.ds(pl.multiple_of(core * half_cols, half_cols), half_cols), :]
    half_copy = remote(half_here, half_here, x_sems.at[6], x_sems.at[7], (twin, ring))
    others = pl.ds(0, (chips - 1) * piece)

    def half_send():
        wait_bytes(ig_ref.at[others, :], x_sems.at[5])
        half_copy.start()

    def loss_end(users):
        wait_bytes(z_loss.at[pl.ds(0, rings - 1)], l_sems.at[1])
        total = users
        for k in range(rings):
            total = total + z_loss[k, 0:1, :]
        loss_ref[0, 0] = jnp.sum(total) * (1.0 / total_users)

    events = []
    for step in range(half):
        events.append(functools.partial(reduce_step, step))
    events.append(reduce_end)
    for step in range(half):
        events.append(functools.partial(gather_step, step))
    events.append(gather_end)
    state = {}

    def sum_event():
        state["users"] = plane_sum()

    def loss_event():
        loss_end(state["users"])

    last = len(events) - 1
    extra = {}
    for place, event in (
        (0, core_send),
        (1, lambda: item_part(core)),
        (1, loss_send),
        (2, plane_send),
        (half + 1, sum_event),
        (half + 2, loss_event),
        (half + 5, half_send),
    ):
        extra.setdefault(min(place, last - 1), []).append(event)
    for place, event in enumerate(events):
        event()
        for more in extra.get(place, ()):
            more()
    half_copy.wait_recv()

    wait_bytes(z_stats.at[pl.ds(0, rings - 1)], z_sems.at[0])
    wait_bytes(p_stats.at[pl.ds(0, chips - 1)], p_sems.at[0])
    wait_bytes(z_loss.at[pl.ds(0, rings - 1)], l_sems.at[0])
    for step in range(half):
        wait_bytes(plus_in.at[step], plus_sems.at[0, step])
        wait_bytes(plus_in.at[step], gplus_sems.at[0, step])
    for step in range(half - 1):
        wait_bytes(minus_in.at[step], minus_sems.at[0, step])
        wait_bytes(minus_in.at[step], gminus_sems.at[0, step])
    core_copy.wait_send()
    wait_bytes(plane_in.at[pl.ds(0, chips - 1)], x_sems.at[2])
    wait_bytes(ig_ref.at[others, :], x_sems.at[4])
    half_copy.wait_send()


def per_device(total_users, chips, rings, user_embed, item_embed, positive, user_count, item_count):
    rows, width = user_embed.shape
    cols = item_embed.shape[0]
    tiles = cols // LANES
    half = rings // 2
    chunk = rows // rings
    piece = cols // 2 // chips
    vmem = pl.BlockSpec(memory_space=pltpu.VMEM)
    dma = pltpu.SemaphoreType.DMA
    user_grad, item_grad, loss = pl.pallas_call(
        functools.partial(kernel, total_users, chips, rings),
        out_shape=(
            jax.ShapeDtypeStruct((rows, width), F32),
            jax.ShapeDtypeStruct((cols, width), F32),
            jax.ShapeDtypeStruct((1, 1), F32),
        ),
        in_specs=[vmem] * 5,
        out_specs=(vmem, vmem, pl.BlockSpec(memory_space=pltpu.SMEM)),
        scratch_shapes=[
            pltpu.VMEM((rows, cols), F32),
            pltpu.VMEM((2, rows, cols // 2), jnp.bfloat16),
            pltpu.VMEM((rows, width), F32),
            pltpu.VMEM((2, cols // 2 + 8, width), F32),
            pltpu.VMEM((tiles, LANES), F32),
            pltpu.VMEM((rows, LANES), F32),
            pltpu.VMEM((rows, LANES), F32),
            pltpu.VMEM((rows, LANES), F32),
            pltpu.VMEM((tiles, 8, LANES), F32),
            pltpu.VMEM((tiles, 8, LANES), F32),
            pltpu.VMEM((tiles, 8, LANES), F32),
            pltpu.VMEM((rings, 8, LANES), F32),
            pltpu.VMEM((2, 2 * tiles, LANES), F32),
            pltpu.VMEM((chips, 2 * tiles, LANES), F32),
            pltpu.VMEM((rings, 8, LANES), F32),
            pltpu.VMEM((half, chunk, width), F32),
            pltpu.VMEM((half - 1, chunk, width), F32),
            pltpu.VMEM((cols // 2 + 8, width), F32),
            pltpu.VMEM((chips, piece + 8, width), F32),
            pltpu.VMEM((chips, piece + 8, width), F32),
            dma((2,)),
            dma((2,)),
            dma((2,)),
            dma((2,)),
            dma((2, half)),
            dma((2, half - 1)),
            dma((2, half)),
            dma((2, half - 1)),
            dma((8,)),
        ],
        compiler_params=pltpu.CompilerParams(
            collective_id=0, has_side_effects=True, vmem_limit_bytes=40 * 1024 * 1024
        ),
        name="two_sided",
    )(
        user_embed,
        item_embed,
        positive.reshape(rows // LANES, LANES),
        user_count.reshape(rows // LANES, LANES),
        item_count.reshape(tiles, LANES),
    )
    return user_grad, item_grad, loss.reshape(())


def solution(mesh):
    row_size, rings = mesh.shape["row"], mesh.shape["col"]

    def whole(user_embed, *others):
        body = functools.partial(per_device, user_embed.shape[0], row_size // 2, rings)
        return jax.shard_map(
            body,
            mesh=mesh,
            in_specs=(P("row", None), P("col", None), P("row"), P("row"), P("col")),
            out_specs=(P("row", None), P("col", None), P()),
            check_vma=False,
        )(user_embed, *others)

    return whole
```

```python
import functools

import jax
import jax.numpy as jnp
from jax import lax
from jax.experimental import pallas as pl
from jax.experimental.pallas import tpu as pltpu
from jax.sharding import PartitionSpec as P

MESH = pl.DeviceIdType.MESH
LANES = 128
BLOCK = 128
WINDOW = 4
CORE_PARTS = 4
F32 = jnp.float32


def columns_of(row):
    return jnp.transpose(jnp.broadcast_to(row, (LANES, LANES)))


def fold(block):
    return block.reshape(block.shape[0] // 8, 8, LANES)


def merged_lse(parts):
    top = jnp.max(parts, axis=0)
    return top + jnp.log(jnp.sum(jnp.exp(parts - top[None]), axis=0))


def kernel(
    total_users,
    chips,
    rings,
    user_hbm,
    item_hbm,
    pos_ref,
    ucnt_ref,
    icnt_ref,
    ug_ref,
    ig_ref,
    loss_ref,
    user_ref,
    item_ref,
    scores,
    coupling,
    part,
    items,
    log_item,
    lu_col,
    pos_col,
    row_col,
    col_max,
    col_sum,
    hits_acc,
    z_stats,
    c_stats,
    p_stats,
    z_loss,
    window_in,
    stride_in,
    core_in,
    plane_out,
    plane_in,
    z_sems,
    c_sems,
    p_sems,
    l_sems,
    w_sems,
    g_sems,
    x_sems,
    back_sems,
    in_sems,
):
    rows_here, width = user_ref.shape
    cols_here = item_ref.shape[0]
    tiles = cols_here // LANES
    row_tiles = rows_here // LANES
    half_cols = cols_here // 2
    half_tiles = tiles // 2
    blocks = rows_here // BLOCK
    piece = half_cols // chips

    user_in = pltpu.make_async_copy(user_hbm, user_ref, in_sems.at[0])
    item_in = pltpu.make_async_copy(item_hbm, item_ref, in_sems.at[1])
    item_in.start()
    user_in.start()

    mine = lax.axis_index("row")
    ring = lax.axis_index("col")
    chip = mine // 2
    core = mine % 2
    other = 1 - core
    twin = chip * 2 + other

    def z_peer(step):
        return (mine, (ring + step) % rings)

    def chip_peer(step):
        return (((chip + step) % chips) * 2 + core, ring)

    z_steps = sorted(range(1, rings), key=lambda k: -min(k, rings - k))
    chip_steps = list(range(1, chips))

    barrier = pltpu.get_barrier_semaphore()
    for step in z_steps:
        pl.semaphore_signal(barrier, inc=1, device_id=z_peer(step), device_id_type=MESH)
    for step in chip_steps:
        pl.semaphore_signal(barrier, inc=1, device_id=chip_peer(step), device_id_type=MESH)
    pl.semaphore_signal(barrier, inc=1, device_id=(twin, ring), device_id_type=MESH)

    def remote(src, dst, send_sem, recv_sem, device):
        return pltpu.make_async_remote_copy(
            src_ref=src,
            dst_ref=dst,
            send_sem=send_sem,
            recv_sem=recv_sem,
            device_id=device,
            device_id_type=MESH,
        )

    def wait_bytes(ref, sem):
        pltpu.make_async_copy(ref, ref, sem).wait()

    log_item[...] = jnp.log(icnt_ref[...].astype(F32))
    log_user = jnp.log(ucnt_ref[...].astype(F32))
    local_pos = pos_ref[...].astype(F32) - (ring * cols_here).astype(F32)
    for k in range(row_tiles):
        span = pl.ds(k * LANES, LANES)
        lu_col[span, :] = columns_of(log_user[k : k + 1, :])
        pos_col[span, :] = columns_of(local_pos[k : k + 1, :])
    col_max[...] = jnp.full(col_max.shape, -jnp.inf, F32)
    col_sum[...] = jnp.zeros(col_sum.shape, F32)
    hits_acc[...] = jnp.zeros(hits_acc.shape, F32)
    lane = lax.broadcasted_iota(jnp.int32, (BLOCK, LANES), 1).astype(F32)

    def sweep_one(b, z_part):
        span = pl.ds(pl.multiple_of(b * BLOCK, BLOCK), BLOCK)
        scores[span, :] = 2.0 * lax.dot_general(
            user_ref[span, :],
            item_ref[...],
            (((1,), (1,)), ((), ())),
            preferred_element_type=F32,
        )
        lu = lu_col[span, :]
        pos = pos_col[span, :]
        top = None
        for t in range(tiles):
            s = scores[span, t * LANES : (t + 1) * LANES]
            shifted = s - log_item[t : t + 1, :]
            top = shifted if top is None else jnp.maximum(top, shifted)
            col_max[t] = jnp.maximum(col_max[t], jnp.max(fold(s - lu), axis=0))
            match = pos == lane + float(t * LANES)
            hits_acc[t] += jnp.sum(fold(jnp.where(match, 1.0, 0.0)), axis=0)
            z_part = z_part + jnp.sum(fold(jnp.where(match, s + shifted, 0.0)), axis=0)
        row_col[span, :] = jnp.broadcast_to(jnp.max(top, axis=1, keepdims=True), (BLOCK, LANES))
        return z_part

    item_in.wait()
    user_in.wait()
    z_part = lax.fori_loop(0, blocks, sweep_one, jnp.zeros((8, LANES), F32))
    for t in range(tiles):
        col_max[t] = jnp.broadcast_to(jnp.max(col_max[t], axis=0, keepdims=True), (8, LANES))

    z_stats[ring] = jnp.zeros((8, LANES), F32)

    def sweep_two(b, carry):
        span = pl.ds(pl.multiple_of(b * BLOCK, BLOCK), BLOCK)
        lu = lu_col[span, :]
        row_max = row_col[span, :]
        total = jnp.zeros((BLOCK, LANES), F32)
        for t in range(tiles):
            s = scores[span, t * LANES : (t + 1) * LANES]
            total = total + jnp.exp(s - log_item[t : t + 1, :] - row_max)
            col = jnp.exp(fold(s - lu) - col_max[t][None])
            col_sum[t] += jnp.sum(col, axis=0)
        lse = row_max + jnp.log(jnp.sum(total, axis=1, keepdims=True))
        z_stats[ring, pl.ds(b, 1), :] = jnp.transpose(lse)[0:1, :]
        return carry

    lax.fori_loop(0, blocks, sweep_two, 0)
    z_stats[ring, pl.ds(row_tiles, 1), :] = jnp.sum(z_part, axis=0, keepdims=True)
    col_lse_rows = []
    hits_rows = []
    for t in range(tiles):
        total = jnp.sum(col_sum[t], axis=0, keepdims=True)
        col_lse_rows.append(col_max[t, 0:1, :] + jnp.log(total))
        hits_rows.append(jnp.sum(hits_acc[t], axis=0, keepdims=True))
    c_stats[0] = jnp.concatenate(col_lse_rows + hits_rows, axis=0)

    pl.semaphore_wait(barrier, rings - 1 + chips - 1 + 1)
    core_stat = remote(c_stats.at[0], c_stats.at[1], c_sems.at[0], c_sems.at[1], (twin, ring))
    core_stat.start()
    for step in z_steps:
        remote(
            z_stats.at[ring], z_stats.at[ring], z_sems.at[0], z_sems.at[1], z_peer(step)
        ).start()
    core_stat.wait()
    one, two = c_stats[0], c_stats[1]
    p_stats[chip, 0:tiles, :] = merged_lse(jnp.stack([one[:tiles], two[:tiles]]))
    p_stats[chip, tiles : 2 * tiles, :] = one[tiles:] + two[tiles:]
    for step in chip_steps:
        remote(
            p_stats.at[chip], p_stats.at[chip], p_sems.at[0], p_sems.at[1], chip_peer(step)
        ).start()
    wait_bytes(z_stats.at[pl.ds(0, rings - 1)], z_sems.at[1])
    user_stats = z_stats[...]
    row_lse = merged_lse(user_stats[:, :row_tiles])
    for k in range(row_tiles):
        row_col[pl.ds(k * LANES, LANES), :] = columns_of(row_lse[k : k + 1, :])
    user_loss = jnp.sum(row_lse + log_user, axis=0, keepdims=True) - jnp.sum(
        user_stats[:, row_tiles : row_tiles + 1], axis=0
    )
    wait_bytes(p_stats.at[pl.ds(0, chips - 1)], p_sems.at[1])
    item_stats = p_stats[...]
    col_lse = merged_lse(item_stats[:, :tiles])
    pos_hits = jnp.sum(item_stats[:, tiles:], axis=0)
    z_loss[ring] = jnp.broadcast_to(
        jnp.sum(pos_hits * col_lse, axis=0, keepdims=True), (8, LANES)
    )

    group = rings // WINDOW
    strip = BLOCK // group
    place = ring // WINDOW
    halves = (pl.ds(0, BLOCK // 2), pl.ds(BLOCK // 2, BLOCK // 2))

    def block_at(index):
        return pl.ds(pl.multiple_of(index % WINDOW * BLOCK, BLOCK), BLOCK)

    def half_at(index, k):
        start = index % WINDOW * BLOCK + k * (BLOCK // 2)
        return pl.ds(pl.multiple_of(start, BLOCK // 2), BLOCK // 2)

    def strip_at(index, k):
        start = index % WINDOW * BLOCK + k % group * strip
        return pl.ds(pl.multiple_of(start, strip), strip)

    def user_block(index):
        span = block_at(index)
        lu = lu_col[span, :]
        pos = pos_col[span, :]
        row = row_col[span, :]
        for t in range(tiles):
            s = scores[span, t * LANES : (t + 1) * LANES]
            value = jnp.exp(s - log_item[t : t + 1, :] - row) + pos_hits[t : t + 1, :] * jnp.exp(
                s - lu - col_lse[t : t + 1, :]
            )
            match = pos == lane + float(t * LANES)
            value = value - jnp.where(match, 2.0, 0.0)
            at = (t % half_tiles) * LANES
            coupling[t // half_tiles, span, at : at + LANES] = value.astype(jnp.bfloat16)
        part[span, :] = 2.0 * (
            jnp.dot(coupling[0, span, :], item_ref[:half_cols, :], preferred_element_type=F32)
            + jnp.dot(coupling[1, span, :], item_ref[half_cols:, :], preferred_element_type=F32)
        )

    near = ((1, 0), (rings - 1, 1))

    def window_send(step, slot):
        for k in range(2):
            remote(
                part.at[half_at(ring + step, k), :],
                window_in.at[slot, halves[k], :],
                w_sems.at[0],
                w_sems.at[1],
                z_peer(step),
            ).start()

    for step, slot in near:
        user_block(ring + step)
        window_send(step, slot)
    user_block(ring + 2)
    for k, step in enumerate((2, rings - 2)):
        remote(
            part.at[half_at(ring + 2, k), :],
            window_in.at[2, halves[k], :],
            w_sems.at[0],
            w_sems.at[1],
            z_peer(step),
        ).start()
    user_block(ring)

    def stride_send():
        wait_bytes(window_in, w_sems.at[1])
        span = block_at(ring)
        part[span, :] += window_in[0] + window_in[1] + window_in[2]
        for k in range(1, group):
            remote(
                part.at[strip_at(ring, place + k), :],
                stride_in.at[k - 1],
                w_sems.at[2],
                w_sems.at[3],
                z_peer(k * WINDOW),
            ).start()

    def spread(index):
        here = ug_ref.at[strip_at(ring, index), :]
        for step in (1, rings - 1):
            remote(here, here, w_sems.at[4], w_sems.at[5], z_peer(step)).start()
        low = index % group < group // 2
        far = jnp.where(low, 2, rings - 2)
        remote(here, here, w_sems.at[4], w_sems.at[5], z_peer(far)).start()

    def stride_sum():
        wait_bytes(stride_in, w_sems.at[3])
        span = strip_at(ring, place)
        total = part[span, :]
        for k in range(group - 1):
            total = total + stride_in[k]
        ug_ref[span, :] = total
        here = ug_ref.at[span, :]
        for k in range(1, group):
            remote(here, here, w_sems.at[6], g_sems.at[k - 1], z_peer(k * WINDOW)).start()
        spread(place)

    def spread_on(k):
        index = place + group - k
        wait_bytes(ug_ref.at[strip_at(ring, index), :], g_sems.at[k - 1])
        spread(index)

    def gather_end():
        wait_bytes(ug_ref.at[pl.ds(0, (WINDOW - 1) * BLOCK), :], w_sems.at[5])

    def item_part(which):
        items[which, :half_cols, :] = 2.0 * lax.dot_general(
            coupling[which],
            user_ref[...],
            (((0,), (0,)), ((), ())),
            preferred_element_type=F32,
        )

    core_rows = half_cols // CORE_PARTS

    def core_send():
        item_part(other)
        items[other, half_cols:, :LANES] = jnp.broadcast_to(user_loss, (8, LANES))
        items[other, half_cols:, LANES:] = jnp.zeros((8, width - LANES), F32)
        for k in range(CORE_PARTS):
            extra = 8 if k == CORE_PARTS - 1 else 0
            span = pl.ds(k * core_rows, core_rows + extra)
            remote(
                items.at[other, span, :],
                core_in.at[span, :],
                x_sems.at[0],
                x_sems.at[1],
                (twin, ring),
            ).start()

    def loss_send():
        for step in z_steps:
            remote(
                z_loss.at[ring], z_loss.at[ring], l_sems.at[0], l_sems.at[1], z_peer(step)
            ).start()

    def plane_send():
        wait_bytes(core_in, x_sems.at[1])
        pair_loss = core_in[half_cols:, :LANES] + user_loss

        def pack(k, carry):
            span = pl.ds(pl.multiple_of(k * piece, piece), piece)
            plane_out[k, :piece, :] = items[core, span, :] + core_in[span, :]
            plane_out[k, piece:, :LANES] = pair_loss
            plane_out[k, piece:, LANES:] = jnp.zeros((8, width - LANES), F32)
            return carry

        lax.fori_loop(0, chips, pack, 0)
        for step in chip_steps:
            remote(
                plane_out.at[(chip + step) % chips],
                plane_in.at[chip],
                x_sems.at[2],
                x_sems.at[3],
                chip_peer(step),
            ).start()
        plane_in[chip] = plane_out[chip]

    def piece_at(half_index, index):
        start = half_index * half_cols + index % chips * piece
        return pl.ds(pl.multiple_of(start, piece), piece)

    def plane_sum():
        wait_bytes(plane_in.at[pl.ds(0, chips - 1)], x_sems.at[3])
        total = plane_in[0]
        for k in range(1, chips):
            total = total + plane_in[k]
        here = ig_ref.at[piece_at(core, chip), :]
        here[...] = total[:piece, :]
        for step in chip_steps:
            remote(
                here, here, x_sems.at[4], back_sems.at[step - 1], chip_peer(step)
            ).start()
        remote(here, here, x_sems.at[5], x_sems.at[6], (twin, ring)).start()
        return total[piece : piece + 1, :LANES]

    def forward(step):
        here = ig_ref.at[piece_at(core, chip + chips - step), :]
        wait_bytes(here, back_sems.at[step - 1])
        remote(here, here, x_sems.at[5], x_sems.at[6], (twin, ring)).start()

    others = pl.ds(0, (chips - 1) * piece)

    def loss_end(users):
        wait_bytes(z_loss.at[pl.ds(0, rings - 1)], l_sems.at[1])
        total = users
        for k in range(rings):
            total = total + z_loss[k, 0:1, :]
        loss_ref[0, 0] = jnp.sum(total) * (1.0 / total_users)

    core_send()
    item_part(core)
    loss_send()
    plane_send()
    stride_send()
    stride_sum()
    loss_end(plane_sum())
    for k in sorted(range(1, group), key=lambda k: min(k, group - k)):
        spread_on(k)
    for step in chip_steps:
        forward(step)
    gather_end()
    wait_bytes(ig_ref.at[pl.ds(0, half_cols), :], x_sems.at[6])

    wait_bytes(z_stats.at[pl.ds(0, rings - 1)], z_sems.at[0])
    wait_bytes(p_stats.at[pl.ds(0, chips - 1)], p_sems.at[0])
    wait_bytes(z_loss.at[pl.ds(0, rings - 1)], l_sems.at[0])
    wait_bytes(window_in, w_sems.at[0])
    wait_bytes(stride_in, w_sems.at[2])
    wait_bytes(ug_ref.at[pl.ds(0, (WINDOW - 1) * BLOCK), :], w_sems.at[4])
    wait_bytes(stride_in, w_sems.at[6])
    wait_bytes(core_in, x_sems.at[0])
    wait_bytes(plane_in.at[pl.ds(0, chips - 1)], x_sems.at[2])
    wait_bytes(ig_ref.at[others, :], x_sems.at[4])
    wait_bytes(ig_ref.at[pl.ds(0, half_cols), :], x_sems.at[5])


def per_device(total_users, chips, rings, user_embed, item_embed, positive, user_count, item_count):
    rows, width = user_embed.shape
    cols = item_embed.shape[0]
    tiles = cols // LANES
    group = rings // WINDOW
    piece = cols // 2 // chips
    vmem = pl.BlockSpec(memory_space=pltpu.VMEM)
    dma = pltpu.SemaphoreType.DMA
    user_grad, item_grad, loss = pl.pallas_call(
        functools.partial(kernel, total_users, chips, rings),
        out_shape=(
            jax.ShapeDtypeStruct((rows, width), F32),
            jax.ShapeDtypeStruct((cols, width), F32),
            jax.ShapeDtypeStruct((1, 1), F32),
        ),
        in_specs=[pl.BlockSpec(memory_space=pltpu.HBM)] * 2 + [vmem] * 3,
        out_specs=(vmem, vmem, pl.BlockSpec(memory_space=pltpu.SMEM)),
        scratch_shapes=[
            pltpu.VMEM((rows, width), user_embed.dtype),
            pltpu.VMEM((cols, width), item_embed.dtype),
            pltpu.VMEM((rows, cols), F32),
            pltpu.VMEM((2, rows, cols // 2), jnp.bfloat16),
            pltpu.VMEM((rows, width), F32),
            pltpu.VMEM((2, cols // 2 + 8, width), F32),
            pltpu.VMEM((tiles, LANES), F32),
            pltpu.VMEM((rows, LANES), F32),
            pltpu.VMEM((rows, LANES), F32),
            pltpu.VMEM((rows, LANES), F32),
            pltpu.VMEM((tiles, 8, LANES), F32),
            pltpu.VMEM((tiles, 8, LANES), F32),
            pltpu.VMEM((tiles, 8, LANES), F32),
            pltpu.VMEM((rings, 8, LANES), F32),
            pltpu.VMEM((2, 2 * tiles, LANES), F32),
            pltpu.VMEM((chips, 2 * tiles, LANES), F32),
            pltpu.VMEM((rings, 8, LANES), F32),
            pltpu.VMEM((WINDOW - 1, BLOCK, width), F32),
            pltpu.VMEM((group - 1, BLOCK // group, width), F32),
            pltpu.VMEM((cols // 2 + 8, width), F32),
            pltpu.VMEM((chips, piece + 8, width), F32),
            pltpu.VMEM((chips, piece + 8, width), F32),
            dma((2,)),
            dma((2,)),
            dma((2,)),
            dma((2,)),
            dma((7,)),
            dma((group - 1,)),
            dma((8,)),
            dma((chips - 1,)),
            dma((2,)),
        ],
        compiler_params=pltpu.CompilerParams(
            collective_id=0, has_side_effects=True, vmem_limit_bytes=60 * 1024 * 1024
        ),
        name="two_sided",
    )(
        user_embed,
        item_embed,
        positive.reshape(rows // LANES, LANES),
        user_count.reshape(rows // LANES, LANES),
        item_count.reshape(tiles, LANES),
    )
    return user_grad, item_grad, loss.reshape(())


def solution(mesh):
    row_size, rings = mesh.shape["row"], mesh.shape["col"]

    def whole(user_embed, *others):
        body = functools.partial(per_device, user_embed.shape[0], row_size // 2, rings)
        return jax.shard_map(
            body,
            mesh=mesh,
            in_specs=(P("row", None), P("col", None), P("row"), P("row"), P("col")),
            out_specs=(P("row", None), P("col", None), P()),
            check_vma=False,
        )(user_embed, *others)

    return whole
```

```python
import functools

import jax
import jax.numpy as jnp
from jax import lax
from jax.experimental import pallas as pl
from jax.experimental.pallas import tpu as pltpu
from jax.sharding import PartitionSpec as P

MESH = pl.DeviceIdType.MESH
LANES = 128
BLOCK = 128
CORE_PARTS = 4
F32 = jnp.float32


def columns_of(row):
    return jnp.transpose(jnp.broadcast_to(row, (LANES, LANES)))


def fold(block):
    return block.reshape(block.shape[0] // 8, 8, LANES)


def merged_lse(parts):
    top = jnp.max(parts, axis=0)
    return top + jnp.log(jnp.sum(jnp.exp(parts - top[None]), axis=0))


def kernel(
    total_users,
    chips,
    rings,
    user_hbm,
    item_hbm,
    pos_ref,
    ucnt_ref,
    icnt_ref,
    ug_ref,
    ig_ref,
    loss_ref,
    user_ref,
    item_ref,
    users,
    scores,
    coupling,
    part,
    items,
    log_item,
    lu_col,
    pos_col,
    row_col,
    col_max,
    col_sum,
    hits_acc,
    z_stats,
    p_stats,
    z_loss,
    hub_in,
    near_in,
    core_in,
    plane_out,
    plane_in,
    z_sems,
    p_sems,
    l_sems,
    w_sems,
    g_sems,
    x_sems,
    back_sems,
    in_sems,
):
    rows_here, width = user_ref.shape
    cols_here = item_ref.shape[0]
    tiles = cols_here // LANES
    row_tiles = rows_here // LANES
    half_cols = cols_here // 2
    half_tiles = tiles // 2
    blocks = rows_here // BLOCK
    piece = half_cols // chips

    user_in = pltpu.make_async_copy(user_hbm, user_ref, in_sems.at[0])
    item_in = pltpu.make_async_copy(item_hbm, item_ref, in_sems.at[1])
    item_in.start()
    user_in.start()

    mine = lax.axis_index("row")
    ring = lax.axis_index("col")
    chip = mine // 2
    core = mine % 2
    other = 1 - core
    twin = chip * 2 + other

    def z_peer(step):
        return (mine, (ring + step) % rings)

    def chip_peer(step):
        return (((chip + step) % chips) * 2 + core, ring)

    def row_peer(step):
        return ((mine + step) % (2 * chips), ring)

    z_steps = sorted(range(1, rings), key=lambda k: -min(k, rings - k))
    chip_steps = list(range(1, chips))
    row_steps = list(range(1, 2 * chips))

    barrier = pltpu.get_barrier_semaphore()
    for step in z_steps:
        pl.semaphore_signal(barrier, inc=1, device_id=z_peer(step), device_id_type=MESH)
    for step in row_steps:
        pl.semaphore_signal(barrier, inc=1, device_id=row_peer(step), device_id_type=MESH)

    def remote(src, dst, send_sem, recv_sem, device):
        return pltpu.make_async_remote_copy(
            src_ref=src,
            dst_ref=dst,
            send_sem=send_sem,
            recv_sem=recv_sem,
            device_id=device,
            device_id_type=MESH,
        )

    def wait_bytes(ref, sem):
        pltpu.make_async_copy(ref, ref, sem).wait()

    log_item[...] = jnp.log(icnt_ref[...].astype(F32))
    log_user = jnp.log(ucnt_ref[...].astype(F32))
    local_pos = pos_ref[...].astype(F32) - (ring * cols_here).astype(F32)
    for k in range(row_tiles):
        span = pl.ds(k * LANES, LANES)
        lu_col[span, :] = columns_of(log_user[k : k + 1, :])
        pos_col[span, :] = columns_of(local_pos[k : k + 1, :])
    col_max[...] = jnp.full(col_max.shape, -jnp.inf, F32)
    col_sum[...] = jnp.zeros(col_sum.shape, F32)
    hits_acc[...] = jnp.zeros(hits_acc.shape, F32)
    lane = lax.broadcasted_iota(jnp.int32, (BLOCK, LANES), 1).astype(F32)

    def sweep_one(b, z_part):
        span = pl.ds(pl.multiple_of(b * BLOCK, BLOCK), BLOCK)
        scores[span, :] = 2.0 * lax.dot_general(
            user_ref[span, :],
            item_ref[...],
            (((1,), (1,)), ((), ())),
            preferred_element_type=F32,
        )
        lu = lu_col[span, :]
        pos = pos_col[span, :]
        top = None
        for t in range(tiles):
            s = scores[span, t * LANES : (t + 1) * LANES]
            shifted = s - log_item[t : t + 1, :]
            top = shifted if top is None else jnp.maximum(top, shifted)
            col_max[t] = jnp.maximum(col_max[t], jnp.max(fold(s - lu), axis=0))
            match = pos == lane + float(t * LANES)
            hits_acc[t] += jnp.sum(fold(jnp.where(match, 1.0, 0.0)), axis=0)
            z_part = z_part + jnp.sum(fold(jnp.where(match, s + shifted, 0.0)), axis=0)
        row_col[span, :] = jnp.broadcast_to(jnp.max(top, axis=1, keepdims=True), (BLOCK, LANES))
        return z_part

    item_in.wait()
    user_in.wait()
    z_part = lax.fori_loop(0, blocks, sweep_one, jnp.zeros((8, LANES), F32))
    for t in range(tiles):
        col_max[t] = jnp.broadcast_to(jnp.max(col_max[t], axis=0, keepdims=True), (8, LANES))

    def sweep_two(b, carry):
        span = pl.ds(pl.multiple_of(b * BLOCK, BLOCK), BLOCK)
        lu = lu_col[span, :]
        row_max = row_col[span, :]
        total = jnp.zeros((BLOCK, LANES), F32)
        for t in range(tiles):
            s = scores[span, t * LANES : (t + 1) * LANES]
            total = total + jnp.exp(s - log_item[t : t + 1, :] - row_max)
            col = jnp.exp(fold(s - lu) - col_max[t][None])
            col_sum[t] += jnp.sum(col, axis=0)
        lse = row_max + jnp.log(jnp.sum(total, axis=1, keepdims=True))
        z_stats[ring, pl.ds(b, 1), :] = jnp.transpose(lse)[0:1, :]
        return carry

    lax.fori_loop(0, blocks, sweep_two, 0)
    col_lse_rows = []
    hits_rows = []
    for t in range(tiles):
        total = jnp.sum(col_sum[t], axis=0, keepdims=True)
        col_lse_rows.append(col_max[t, 0:1, :] + jnp.log(total))
        hits_rows.append(jnp.sum(hits_acc[t], axis=0, keepdims=True))
    p_stats[mine] = jnp.concatenate(col_lse_rows + hits_rows, axis=0)

    pl.semaphore_wait(barrier, rings - 1 + 2 * chips - 1)
    for step in z_steps:
        remote(
            z_stats.at[ring], z_stats.at[ring], z_sems.at[0], z_sems.at[1], z_peer(step)
        ).start()
    for step in row_steps:
        remote(
            p_stats.at[mine], p_stats.at[mine], p_sems.at[0], p_sems.at[1], row_peer(step)
        ).start()
    wait_bytes(z_stats.at[pl.ds(0, rings - 1)], z_sems.at[1])
    row_lse = merged_lse(z_stats[...])
    for k in range(row_tiles):
        row_col[pl.ds(k * LANES, LANES), :] = columns_of(row_lse[k : k + 1, :])
    user_loss = jnp.sum(row_lse + log_user, axis=0, keepdims=True)
    match_loss = jnp.sum(z_part, axis=0, keepdims=True)
    loss_rows = jnp.concatenate([user_loss, match_loss, jnp.zeros((6, LANES), F32)], axis=0)
    wait_bytes(p_stats.at[pl.ds(0, 2 * chips - 1)], p_sems.at[1])
    item_stats = p_stats[...]
    col_lse = merged_lse(item_stats[:, :tiles])
    pos_hits = jnp.sum(item_stats[:, tiles:], axis=0)
    item_loss = jnp.sum(pos_hits * col_lse, axis=0, keepdims=True)

    strip = rows_here // rings
    per_block = BLOCK // strip
    direct = rings // 8
    hub = 2 * direct + 1
    covers = [c for c in range(-direct, direct + 1) if c != 0 and hub + c < rings // 2]
    far = rings // 2 - hub
    order = [(direct + 1 + j) % rings for j in range(rings)]
    signs = (1, -1)

    def strip_at(offset):
        start = (ring + offset + rings) % rings * strip
        return pl.ds(pl.multiple_of(start, strip), strip)

    def part_at(offset):
        return pl.ds(order.index(offset % rings) * strip, strip)

    def z_at(offset):
        return z_peer(offset % rings)

    def halves(index):
        return pl.ds(index * (strip // 2), strip // 2)

    strip_lane = lane[:strip, :]

    def user_block(b):
        for j in range(b * per_block, (b + 1) * per_block):
            source = strip_at(order[j])
            target = pl.ds(j * strip, strip)
            users[target, :] = user_ref[source, :]
            lu = lu_col[source, :]
            pos = pos_col[source, :]
            row = row_col[source, :]
            for t in range(tiles):
                s = scores[source, t * LANES : (t + 1) * LANES]
                value = jnp.exp(s - log_item[t : t + 1, :] - row) + pos_hits[
                    t : t + 1, :
                ] * jnp.exp(s - lu - col_lse[t : t + 1, :])
                match = pos == strip_lane + float(t * LANES)
                value = value - jnp.where(match, 2.0, 0.0)
                at = (t % half_tiles) * LANES
                coupling[t // half_tiles, target, at : at + LANES] = value.astype(jnp.bfloat16)
        span = pl.ds(b * BLOCK, BLOCK)
        part[span, :] = 2.0 * (
            jnp.dot(coupling[0, span, :], item_ref[:half_cols, :], preferred_element_type=F32)
            + jnp.dot(coupling[1, span, :], item_ref[half_cols:, :], preferred_element_type=F32)
        )

    leaving = {}
    hub_half = pl.ds(len(covers) * strip, strip // 2)
    for index, sign in enumerate(signs):
        for slot, c in enumerate(covers):
            leaving.setdefault(-sign * (hub + c) % rings, []).append(
                (
                    part.at[part_at(-sign * (hub + c)), :],
                    hub_in.at[index, pl.ds(slot * strip, strip), :],
                    w_sems.at[0],
                    w_sems.at[1 + index],
                    z_at(-sign * c),
                )
            )
        leaving.setdefault(rings // 2, []).append(
            (
                part.at[pl.ds(part_at(rings // 2).start + index * (strip // 2), strip // 2), :],
                hub_in.at[index, hub_half, :],
                w_sems.at[0],
                w_sems.at[1 + index],
                z_at(-sign * far),
            )
        )
        for step in range(1, direct + 1):
            leaving.setdefault(-sign * step % rings, []).append(
                (
                    part.at[part_at(-sign * step), :],
                    near_in.at[index * direct + step - 1],
                    w_sems.at[3],
                    w_sems.at[4],
                    z_at(-sign * step),
                )
            )

    for b in range(blocks):
        user_block(b)
        for j in range(b * per_block, (b + 1) * per_block):
            for copy in leaving.get(order[j], ()):
                remote(*copy).start()

    def hub_sum(index):
        sign = signs[index]
        wait_bytes(hub_in.at[index], w_sems.at[1 + index])
        span = part_at(-sign * hub)
        total = part[span, :]
        for slot in range(len(covers)):
            total = total + hub_in[index, slot * strip : (slot + 1) * strip, :]
        part[span, :] = total
        half = pl.ds(span.start + index * (strip // 2), strip // 2)
        part[half, :] += hub_in[index, hub_half, :]
        remote(
            part.at[span, :],
            near_in.at[2 * direct + index],
            w_sems.at[3],
            w_sems.at[4],
            z_at(-sign * hub),
        ).start()

    def own_sum():
        wait_bytes(near_in, w_sems.at[4])
        total = part[part_at(0), :]
        for slot in range(2 * direct + 2):
            total = total + near_in[slot]
        span = strip_at(0)
        ug_ref[span, :] = total
        here = ug_ref.at[span, :]
        for index, sign in enumerate(signs):
            remote(here, here, w_sems.at[5], g_sems.at[index], z_at(sign * hub)).start()
        for step in range(1, direct + 1):
            for sign in signs:
                remote(here, here, w_sems.at[5], w_sems.at[6], z_at(sign * step)).start()

    def hub_spread(index):
        sign = signs[index]
        start = (ring - sign * hub + rings) % rings * strip
        here = ug_ref.at[pl.ds(pl.multiple_of(start, strip), strip), :]
        wait_bytes(here, g_sems.at[index])
        half_start = pl.multiple_of(start + index * (strip // 2), strip // 2)
        half = ug_ref.at[pl.ds(half_start, strip // 2), :]
        remote(half, half, w_sems.at[5], w_sems.at[6], z_at(sign * far)).start()
        for c in sorted(covers, key=lambda c: -abs(c)):
            remote(here, here, w_sems.at[5], w_sems.at[6], z_at(sign * c)).start()

    def gather_end():
        wait_bytes(ug_ref.at[pl.ds(0, (rings - 3) * strip), :], w_sems.at[6])

    def item_part(which):
        items[which, :half_cols, :] = 2.0 * lax.dot_general(
            coupling[which],
            users[...],
            (((0,), (0,)), ((), ())),
            preferred_element_type=F32,
        )

    core_rows = half_cols // CORE_PARTS

    def core_send():
        item_part(other)
        items[other, half_cols:, :LANES] = loss_rows
        items[other, half_cols:, LANES:] = jnp.zeros((8, width - LANES), F32)
        for k in range(CORE_PARTS):
            extra = 8 if k == CORE_PARTS - 1 else 0
            span = pl.ds(k * core_rows, core_rows + extra)
            remote(
                items.at[other, span, :],
                core_in.at[span, :],
                x_sems.at[0],
                x_sems.at[1],
                (twin, ring),
            ).start()

    def plane_send():
        wait_bytes(core_in, x_sems.at[1])
        pair_loss = core_in[half_cols:, :LANES] + loss_rows

        def pack(k, carry):
            span = pl.ds(pl.multiple_of(k * piece, piece), piece)
            plane_out[k, :piece, :] = items[core, span, :] + core_in[span, :]
            plane_out[k, piece:, :LANES] = pair_loss
            plane_out[k, piece:, LANES:] = jnp.zeros((8, width - LANES), F32)
            return carry

        lax.fori_loop(0, chips, pack, 0)
        for step in chip_steps:
            remote(
                plane_out.at[(chip + step) % chips],
                plane_in.at[chip],
                x_sems.at[2],
                x_sems.at[3],
                chip_peer(step),
            ).start()
        plane_in[chip] = plane_out[chip]

    def piece_at(half_index, index):
        start = half_index * half_cols + index % chips * piece
        return pl.ds(pl.multiple_of(start, piece), piece)

    def plane_sum():
        wait_bytes(plane_in.at[pl.ds(0, chips - 1)], x_sems.at[3])
        total = plane_in[0]
        for k in range(1, chips):
            total = total + plane_in[k]
        here = ig_ref.at[piece_at(core, chip), :]
        here[...] = total[:piece, :]
        for step in chip_steps:
            remote(
                here, here, x_sems.at[4], back_sems.at[step - 1], chip_peer(step)
            ).start()
        remote(here, here, x_sems.at[5], x_sems.at[6], (twin, ring)).start()
        z_loss[ring] = jnp.broadcast_to(
            item_loss - total[piece + 1 : piece + 2, :LANES], (8, LANES)
        )
        for step in z_steps:
            remote(
                z_loss.at[ring], z_loss.at[ring], l_sems.at[0], l_sems.at[1], z_peer(step)
            ).start()
        return total[piece : piece + 1, :LANES]

    def forward(step):
        here = ig_ref.at[piece_at(core, chip + chips - step), :]
        wait_bytes(here, back_sems.at[step - 1])
        remote(here, here, x_sems.at[5], x_sems.at[6], (twin, ring)).start()

    others = pl.ds(0, (chips - 1) * piece)

    def loss_end(users):
        wait_bytes(z_loss.at[pl.ds(0, rings - 1)], l_sems.at[1])
        total = users
        for k in range(rings):
            total = total + z_loss[k, 0:1, :]
        loss_ref[0, 0] = jnp.sum(total) * (1.0 / total_users)

    core_send()
    item_part(core)
    plane_send()
    hub_sum(0)
    hub_sum(1)
    own_sum()
    users_total = plane_sum()
    hub_spread(0)
    hub_spread(1)
    for step in chip_steps:
        forward(step)
    loss_end(users_total)
    gather_end()
    wait_bytes(ig_ref.at[pl.ds(0, half_cols), :], x_sems.at[6])

    wait_bytes(z_stats.at[pl.ds(0, rings - 1)], z_sems.at[0])
    wait_bytes(p_stats.at[pl.ds(0, 2 * chips - 1)], p_sems.at[0])
    wait_bytes(z_loss.at[pl.ds(0, rings - 1)], l_sems.at[0])
    wait_bytes(hub_in, w_sems.at[0])
    wait_bytes(near_in, w_sems.at[3])
    wait_bytes(ug_ref.at[pl.ds(0, (rings - 1) * strip), :], w_sems.at[5])
    wait_bytes(core_in, x_sems.at[0])
    wait_bytes(plane_in.at[pl.ds(0, chips - 1)], x_sems.at[2])
    wait_bytes(ig_ref.at[others, :], x_sems.at[4])
    wait_bytes(ig_ref.at[pl.ds(0, half_cols), :], x_sems.at[5])


def per_device(total_users, chips, rings, user_embed, item_embed, positive, user_count, item_count):
    rows, width = user_embed.shape
    cols = item_embed.shape[0]
    tiles = cols // LANES
    strip = rows // rings
    direct = rings // 8
    hub_rows = (2 * direct if rings > 8 else 1) * strip + strip // 2
    piece = cols // 2 // chips
    vmem = pl.BlockSpec(memory_space=pltpu.VMEM)
    dma = pltpu.SemaphoreType.DMA
    user_grad, item_grad, loss = pl.pallas_call(
        functools.partial(kernel, total_users, chips, rings),
        out_shape=(
            jax.ShapeDtypeStruct((rows, width), F32),
            jax.ShapeDtypeStruct((cols, width), F32),
            jax.ShapeDtypeStruct((1, 1), F32),
        ),
        in_specs=[pl.BlockSpec(memory_space=pltpu.HBM)] * 2 + [vmem] * 3,
        out_specs=(vmem, vmem, pl.BlockSpec(memory_space=pltpu.SMEM)),
        scratch_shapes=[
            pltpu.VMEM((rows, width), user_embed.dtype),
            pltpu.VMEM((cols, width), item_embed.dtype),
            pltpu.VMEM((rows, width), user_embed.dtype),
            pltpu.VMEM((rows, cols), F32),
            pltpu.VMEM((2, rows, cols // 2), jnp.bfloat16),
            pltpu.VMEM((rows, width), F32),
            pltpu.VMEM((2, cols // 2 + 8, width), F32),
            pltpu.VMEM((tiles, LANES), F32),
            pltpu.VMEM((rows, LANES), F32),
            pltpu.VMEM((rows, LANES), F32),
            pltpu.VMEM((rows, LANES), F32),
            pltpu.VMEM((tiles, 8, LANES), F32),
            pltpu.VMEM((tiles, 8, LANES), F32),
            pltpu.VMEM((tiles, 8, LANES), F32),
            pltpu.VMEM((rings, rows // LANES, LANES), F32),
            pltpu.VMEM((2 * chips, 2 * tiles, LANES), F32),
            pltpu.VMEM((rings, 8, LANES), F32),
            pltpu.VMEM((2, hub_rows, width), F32),
            pltpu.VMEM((2 * direct + 2, strip, width), F32),
            pltpu.VMEM((cols // 2 + 8, width), F32),
            pltpu.VMEM((chips, piece + 8, width), F32),
            pltpu.VMEM((chips, piece + 8, width), F32),
            dma((2,)),
            dma((2,)),
            dma((2,)),
            dma((7,)),
            dma((2,)),
            dma((8,)),
            dma((chips - 1,)),
            dma((2,)),
        ],
        compiler_params=pltpu.CompilerParams(
            collective_id=0, has_side_effects=True, vmem_limit_bytes=60 * 1024 * 1024
        ),
        name="two_sided",
    )(
        user_embed,
        item_embed,
        positive.reshape(rows // LANES, LANES),
        user_count.reshape(rows // LANES, LANES),
        item_count.reshape(tiles, LANES),
    )
    return user_grad, item_grad, loss.reshape(())


def solution(mesh):
    row_size, rings = mesh.shape["row"], mesh.shape["col"]

    def whole(user_embed, *others):
        body = functools.partial(per_device, user_embed.shape[0], row_size // 2, rings)
        return jax.shard_map(
            body,
            mesh=mesh,
            in_specs=(P("row", None), P("col", None), P("row"), P("row"), P("col")),
            out_specs=(P("row", None), P("col", None), P()),
            check_vma=False,
        )(user_embed, *others)

    return whole
```

```python
import functools

import jax
import jax.numpy as jnp
from jax import lax
from jax.experimental import pallas as pl
from jax.experimental.pallas import tpu as pltpu
from jax.sharding import PartitionSpec as P

MESH = pl.DeviceIdType.MESH
LANES = 128
BLOCK = 128
CORE_PARTS = 4
F32 = jnp.float32


def columns_of(row):
    return jnp.transpose(jnp.broadcast_to(row, (LANES, LANES)))


def fold(block):
    return block.reshape(block.shape[0] // 8, 8, LANES)


def merged_lse(parts):
    top = jnp.max(parts, axis=0)
    return top + jnp.log(jnp.sum(jnp.exp(parts - top[None]), axis=0))


def kernel(
    total_users,
    chips,
    rings,
    user_hbm,
    item_hbm,
    pos_ref,
    ucnt_ref,
    icnt_ref,
    ug_ref,
    ig_ref,
    loss_ref,
    user_ref,
    item_ref,
    users,
    scores,
    row_exp,
    col_exp,
    coupling,
    part,
    items,
    log_item,
    lu_col,
    pos_col,
    row_col,
    col_max,
    col_sum,
    hits_acc,
    z_stats,
    p_stats,
    z_loss,
    hub_in,
    near_in,
    core_in,
    plane_out,
    plane_in,
    z_sems,
    p_sems,
    l_sems,
    w_sems,
    g_sems,
    x_sems,
    back_sems,
    in_sems,
):
    rows_here, width = user_ref.shape
    cols_here = item_ref.shape[0]
    tiles = cols_here // LANES
    row_tiles = rows_here // LANES
    half_cols = cols_here // 2
    half_tiles = tiles // 2
    blocks = rows_here // BLOCK
    piece = half_cols // chips

    user_in = pltpu.make_async_copy(user_hbm, user_ref, in_sems.at[0])
    item_in = pltpu.make_async_copy(item_hbm, item_ref, in_sems.at[1])
    item_in.start()
    user_in.start()

    mine = lax.axis_index("row")
    ring = lax.axis_index("col")
    chip = mine // 2
    core = mine % 2
    other = 1 - core
    twin = chip * 2 + other

    def z_peer(step):
        return (mine, (ring + step) % rings)

    def chip_peer(step):
        return (((chip + step) % chips) * 2 + core, ring)

    def row_peer(step):
        return ((mine + step) % (2 * chips), ring)

    z_steps = sorted(range(1, rings), key=lambda k: -min(k, rings - k))
    chip_steps = list(range(1, chips))
    row_steps = list(range(1, 2 * chips))

    barrier = pltpu.get_barrier_semaphore()
    for step in z_steps:
        pl.semaphore_signal(barrier, inc=1, device_id=z_peer(step), device_id_type=MESH)
    for step in row_steps:
        pl.semaphore_signal(barrier, inc=1, device_id=row_peer(step), device_id_type=MESH)

    def remote(src, dst, send_sem, recv_sem, device):
        return pltpu.make_async_remote_copy(
            src_ref=src,
            dst_ref=dst,
            send_sem=send_sem,
            recv_sem=recv_sem,
            device_id=device,
            device_id_type=MESH,
        )

    def wait_bytes(ref, sem):
        pltpu.make_async_copy(ref, ref, sem).wait()

    log_item[...] = jnp.log(icnt_ref[...].astype(F32))
    log_user = jnp.log(ucnt_ref[...].astype(F32))
    local_pos = pos_ref[...].astype(F32) - (ring * cols_here).astype(F32)
    for k in range(row_tiles):
        span = pl.ds(k * LANES, LANES)
        lu_col[span, :] = columns_of(log_user[k : k + 1, :])
        pos_col[span, :] = columns_of(local_pos[k : k + 1, :])
    col_max[...] = jnp.full(col_max.shape, -jnp.inf, F32)
    col_sum[...] = jnp.zeros(col_sum.shape, F32)
    hits_acc[...] = jnp.zeros(hits_acc.shape, F32)
    lane = lax.broadcasted_iota(jnp.int32, (BLOCK, LANES), 1).astype(F32)

    def count_hits(b, carry):
        span = pl.ds(pl.multiple_of(b * BLOCK, BLOCK), BLOCK)
        pos = pos_col[span, :]
        for t in range(tiles):
            match = pos == lane + float(t * LANES)
            hits_acc[t] += jnp.sum(fold(jnp.where(match, 1.0, 0.0)), axis=0)
        return carry

    lax.fori_loop(0, blocks, count_hits, 0)

    def sweep_one(b, carry):
        span = pl.ds(pl.multiple_of(b * BLOCK, BLOCK), BLOCK)
        scores[span, :] = 2.0 * lax.dot_general(
            user_ref[span, :],
            item_ref[...],
            (((1,), (1,)), ((), ())),
            preferred_element_type=F32,
        )
        lu = lu_col[span, :]
        top = None
        for t in range(tiles):
            s = scores[span, t * LANES : (t + 1) * LANES]
            shifted = s - log_item[t : t + 1, :]
            top = shifted if top is None else jnp.maximum(top, shifted)
            col_max[t] = jnp.maximum(col_max[t], jnp.max(fold(s - lu), axis=0))
        row_col[span, :] = jnp.broadcast_to(jnp.max(top, axis=1, keepdims=True), (BLOCK, LANES))
        return carry

    item_in.wait()
    user_in.wait()
    lax.fori_loop(0, blocks, sweep_one, 0)
    for t in range(tiles):
        col_max[t] = jnp.broadcast_to(jnp.max(col_max[t], axis=0, keepdims=True), (8, LANES))

    def sweep_two(b, carry):
        span = pl.ds(pl.multiple_of(b * BLOCK, BLOCK), BLOCK)
        lu = lu_col[span, :]
        row_max = row_col[span, :]
        total = jnp.zeros((BLOCK, LANES), F32)
        for t in range(tiles):
            s = scores[span, t * LANES : (t + 1) * LANES]
            row = jnp.exp(s - log_item[t : t + 1, :] - row_max)
            row_exp[span, t * LANES : (t + 1) * LANES] = row
            total = total + row
            col = jnp.exp(s - lu - col_max[t, 0:1, :])
            col_exp[span, t * LANES : (t + 1) * LANES] = col
            col_sum[t] += jnp.sum(fold(col), axis=0)
        lse = row_max + jnp.log(jnp.sum(total, axis=1, keepdims=True))
        z_stats[ring, pl.ds(b, 1), :] = jnp.transpose(lse)[0:1, :]
        return carry

    lax.fori_loop(0, blocks, sweep_two, 0)
    col_lse_rows = []
    hits_rows = []
    for t in range(tiles):
        total = jnp.sum(col_sum[t], axis=0, keepdims=True)
        col_lse_rows.append(col_max[t, 0:1, :] + jnp.log(total))
        hits_rows.append(jnp.sum(hits_acc[t], axis=0, keepdims=True))
    p_stats[mine] = jnp.concatenate(col_lse_rows + hits_rows, axis=0)

    pl.semaphore_wait(barrier, rings - 1 + 2 * chips - 1)
    for step in z_steps:
        remote(
            z_stats.at[ring], z_stats.at[ring], z_sems.at[0], z_sems.at[1], z_peer(step)
        ).start()
    for step in row_steps:
        remote(
            p_stats.at[mine], p_stats.at[mine], p_sems.at[0], p_sems.at[1], row_peer(step)
        ).start()

    def match_scores(b, so_far):
        span = pl.ds(pl.multiple_of(b * BLOCK, BLOCK), BLOCK)
        pos = pos_col[span, :]
        for t in range(tiles):
            s = scores[span, t * LANES : (t + 1) * LANES]
            match = pos == lane + float(t * LANES)
            value = jnp.where(match, s + s - log_item[t : t + 1, :], 0.0)
            so_far = so_far + jnp.sum(fold(value), axis=0)
        return so_far

    z_part = lax.fori_loop(0, blocks, match_scores, jnp.zeros((8, LANES), F32))
    match_loss = jnp.sum(z_part, axis=0, keepdims=True)

    wait_bytes(z_stats.at[pl.ds(0, rings - 1)], z_sems.at[1])
    row_lse = merged_lse(z_stats[...])
    for k in range(row_tiles):
        span = pl.ds(k * LANES, LANES)
        row_col[span, :] = jnp.exp(row_col[span, :] - columns_of(row_lse[k : k + 1, :]))
    user_loss = jnp.sum(row_lse + log_user, axis=0, keepdims=True)
    loss_rows = jnp.concatenate([user_loss, match_loss, jnp.zeros((6, LANES), F32)], axis=0)
    wait_bytes(p_stats.at[pl.ds(0, 2 * chips - 1)], p_sems.at[1])
    item_stats = p_stats[...]
    col_lse = merged_lse(item_stats[:, :tiles])
    pos_hits = jnp.sum(item_stats[:, tiles:], axis=0)
    item_loss = jnp.sum(pos_hits * col_lse, axis=0, keepdims=True)
    col_top = jnp.concatenate([col_max[t, 0:1, :] for t in range(tiles)], axis=0)
    col_scale = pos_hits * jnp.exp(col_top - col_lse)

    strip = rows_here // rings
    per_block = BLOCK // strip
    direct = rings // 8
    hub = 2 * direct + 1
    covers = [c for c in range(-direct, direct + 1) if c != 0 and hub + c < rings // 2]
    far = rings // 2 - hub
    order = [(direct + 1 + j) % rings for j in range(rings)]
    signs = (1, -1)

    def strip_at(offset):
        start = (ring + offset + rings) % rings * strip
        return pl.ds(pl.multiple_of(start, strip), strip)

    def part_at(offset):
        return pl.ds(order.index(offset % rings) * strip, strip)

    def z_at(offset):
        return z_peer(offset % rings)

    def halves(index):
        return pl.ds(index * (strip // 2), strip // 2)

    strip_lane = lane[:strip, :]

    def user_block(b):
        for j in range(b * per_block, (b + 1) * per_block):
            source = strip_at(order[j])
            target = pl.ds(j * strip, strip)
            users[target, :] = user_ref[source, :]
            pos = pos_col[source, :]
            row = row_col[source, :]
            for t in range(tiles):
                here = slice(t * LANES, (t + 1) * LANES)
                value = row_exp[source, here] * row + col_exp[source, here] * col_scale[t : t + 1, :]
                match = pos == strip_lane + float(t * LANES)
                value = value - jnp.where(match, 2.0, 0.0)
                at = (t % half_tiles) * LANES
                coupling[t // half_tiles, target, at : at + LANES] = value.astype(jnp.bfloat16)
        span = pl.ds(b * BLOCK, BLOCK)
        part[span, :] = 2.0 * (
            jnp.dot(coupling[0, span, :], item_ref[:half_cols, :], preferred_element_type=F32)
            + jnp.dot(coupling[1, span, :], item_ref[half_cols:, :], preferred_element_type=F32)
        )

    leaving = {}
    hub_half = pl.ds(len(covers) * strip, strip // 2)
    for index, sign in enumerate(signs):
        for slot, c in enumerate(covers):
            leaving.setdefault(-sign * (hub + c) % rings, []).append(
                (
                    part.at[part_at(-sign * (hub + c)), :],
                    hub_in.at[index, pl.ds(slot * strip, strip), :],
                    w_sems.at[0],
                    w_sems.at[1 + index],
                    z_at(-sign * c),
                )
            )
        leaving.setdefault(rings // 2, []).append(
            (
                part.at[pl.ds(part_at(rings // 2).start + index * (strip // 2), strip // 2), :],
                hub_in.at[index, hub_half, :],
                w_sems.at[0],
                w_sems.at[1 + index],
                z_at(-sign * far),
            )
        )
        for step in range(1, direct + 1):
            leaving.setdefault(-sign * step % rings, []).append(
                (
                    part.at[part_at(-sign * step), :],
                    near_in.at[index * direct + step - 1],
                    w_sems.at[3],
                    w_sems.at[4],
                    z_at(-sign * step),
                )
            )

    for b in range(blocks):
        user_block(b)
        for j in range(b * per_block, (b + 1) * per_block):
            for copy in leaving.get(order[j], ()):
                remote(*copy).start()

    def hub_sum(index):
        sign = signs[index]
        wait_bytes(hub_in.at[index], w_sems.at[1 + index])
        span = part_at(-sign * hub)
        total = part[span, :]
        for slot in range(len(covers)):
            total = total + hub_in[index, slot * strip : (slot + 1) * strip, :]
        part[span, :] = total
        half = pl.ds(span.start + index * (strip // 2), strip // 2)
        part[half, :] += hub_in[index, hub_half, :]
        remote(
            part.at[span, :],
            near_in.at[2 * direct + index],
            w_sems.at[3],
            w_sems.at[4],
            z_at(-sign * hub),
        ).start()

    def own_sum():
        wait_bytes(near_in, w_sems.at[4])
        total = part[part_at(0), :]
        for slot in range(2 * direct + 2):
            total = total + near_in[slot]
        span = strip_at(0)
        ug_ref[span, :] = total
        here = ug_ref.at[span, :]
        for index, sign in enumerate(signs):
            remote(here, here, w_sems.at[5], g_sems.at[index], z_at(sign * hub)).start()
        for step in range(1, direct + 1):
            for sign in signs:
                remote(here, here, w_sems.at[5], w_sems.at[6], z_at(sign * step)).start()

    def hub_spread(index):
        sign = signs[index]
        start = (ring - sign * hub + rings) % rings * strip
        here = ug_ref.at[pl.ds(pl.multiple_of(start, strip), strip), :]
        wait_bytes(here, g_sems.at[index])
        half_start = pl.multiple_of(start + index * (strip // 2), strip // 2)
        half = ug_ref.at[pl.ds(half_start, strip // 2), :]
        remote(half, half, w_sems.at[5], w_sems.at[6], z_at(sign * far)).start()
        for c in sorted(covers, key=lambda c: -abs(c)):
            remote(here, here, w_sems.at[5], w_sems.at[6], z_at(sign * c)).start()

    def gather_end():
        wait_bytes(ug_ref.at[pl.ds(0, (rings - 3) * strip), :], w_sems.at[6])

    def item_part(which):
        items[which, :half_cols, :] = 2.0 * lax.dot_general(
            coupling[which],
            users[...],
            (((0,), (0,)), ((), ())),
            preferred_element_type=F32,
        )

    core_rows = half_cols // CORE_PARTS

    def core_send():
        item_part(other)
        items[other, half_cols:, :LANES] = loss_rows
        items[other, half_cols:, LANES:] = jnp.zeros((8, width - LANES), F32)
        for k in range(CORE_PARTS):
            extra = 8 if k == CORE_PARTS - 1 else 0
            span = pl.ds(k * core_rows, core_rows + extra)
            remote(
                items.at[other, span, :],
                core_in.at[span, :],
                x_sems.at[0],
                x_sems.at[1],
                (twin, ring),
            ).start()

    def plane_send():
        wait_bytes(core_in, x_sems.at[1])
        pair_loss = core_in[half_cols:, :LANES] + loss_rows

        def pack(k, carry):
            span = pl.ds(pl.multiple_of(k * piece, piece), piece)
            plane_out[k, :piece, :] = items[core, span, :] + core_in[span, :]
            plane_out[k, piece:, :LANES] = pair_loss
            plane_out[k, piece:, LANES:] = jnp.zeros((8, width - LANES), F32)
            return carry

        lax.fori_loop(0, chips, pack, 0)
        for step in chip_steps:
            remote(
                plane_out.at[(chip + step) % chips],
                plane_in.at[chip],
                x_sems.at[2],
                x_sems.at[3],
                chip_peer(step),
            ).start()
        plane_in[chip] = plane_out[chip]

    def piece_at(half_index, index):
        start = half_index * half_cols + index % chips * piece
        return pl.ds(pl.multiple_of(start, piece), piece)

    def plane_sum():
        wait_bytes(plane_in.at[pl.ds(0, chips - 1)], x_sems.at[3])
        total = plane_in[0]
        for k in range(1, chips):
            total = total + plane_in[k]
        here = ig_ref.at[piece_at(core, chip), :]
        here[...] = total[:piece, :]
        for step in chip_steps:
            remote(
                here, here, x_sems.at[4], back_sems.at[step - 1], chip_peer(step)
            ).start()
        remote(here, here, x_sems.at[5], x_sems.at[6], (twin, ring)).start()
        return total[piece : piece + 8, :LANES]

    def loss_send(total):
        z_loss[ring] = jnp.broadcast_to(item_loss - total[1:2, :], (8, LANES))
        for step in z_steps:
            remote(
                z_loss.at[ring], z_loss.at[ring], l_sems.at[0], l_sems.at[1], z_peer(step)
            ).start()

    def forward(step):
        here = ig_ref.at[piece_at(core, chip + chips - step), :]
        wait_bytes(here, back_sems.at[step - 1])
        remote(here, here, x_sems.at[5], x_sems.at[6], (twin, ring)).start()

    others = pl.ds(0, (chips - 1) * piece)

    def loss_end(users):
        wait_bytes(z_loss.at[pl.ds(0, rings - 1)], l_sems.at[1])
        total = users
        for k in range(rings):
            total = total + z_loss[k, 0:1, :]
        loss_ref[0, 0] = jnp.sum(total) * (1.0 / total_users)

    core_send()
    item_part(core)
    hub_sum(0)
    hub_sum(1)
    plane_send()
    own_sum()
    plane_total = plane_sum()
    hub_spread(0)
    hub_spread(1)
    loss_send(plane_total)
    for step in chip_steps:
        forward(step)
    loss_end(plane_total[0:1, :])
    gather_end()
    wait_bytes(ig_ref.at[pl.ds(0, half_cols), :], x_sems.at[6])

    wait_bytes(z_stats.at[pl.ds(0, rings - 1)], z_sems.at[0])
    wait_bytes(p_stats.at[pl.ds(0, 2 * chips - 1)], p_sems.at[0])
    wait_bytes(z_loss.at[pl.ds(0, rings - 1)], l_sems.at[0])
    wait_bytes(hub_in, w_sems.at[0])
    wait_bytes(near_in, w_sems.at[3])
    wait_bytes(ug_ref.at[pl.ds(0, (rings - 1) * strip), :], w_sems.at[5])
    wait_bytes(core_in, x_sems.at[0])
    wait_bytes(plane_in.at[pl.ds(0, chips - 1)], x_sems.at[2])
    wait_bytes(ig_ref.at[others, :], x_sems.at[4])
    wait_bytes(ig_ref.at[pl.ds(0, half_cols), :], x_sems.at[5])


def per_device(total_users, chips, rings, user_embed, item_embed, positive, user_count, item_count):
    rows, width = user_embed.shape
    cols = item_embed.shape[0]
    tiles = cols // LANES
    strip = rows // rings
    direct = rings // 8
    hub_rows = (2 * direct if rings > 8 else 1) * strip + strip // 2
    piece = cols // 2 // chips
    vmem = pl.BlockSpec(memory_space=pltpu.VMEM)
    dma = pltpu.SemaphoreType.DMA
    user_grad, item_grad, loss = pl.pallas_call(
        functools.partial(kernel, total_users, chips, rings),
        out_shape=(
            jax.ShapeDtypeStruct((rows, width), F32),
            jax.ShapeDtypeStruct((cols, width), F32),
            jax.ShapeDtypeStruct((1, 1), F32),
        ),
        in_specs=[pl.BlockSpec(memory_space=pltpu.HBM)] * 2 + [vmem] * 3,
        out_specs=(vmem, vmem, pl.BlockSpec(memory_space=pltpu.SMEM)),
        scratch_shapes=[
            pltpu.VMEM((rows, width), user_embed.dtype),
            pltpu.VMEM((cols, width), item_embed.dtype),
            pltpu.VMEM((rows, width), user_embed.dtype),
            pltpu.VMEM((rows, cols), F32),
            pltpu.VMEM((rows, cols), F32),
            pltpu.VMEM((rows, cols), F32),
            pltpu.VMEM((2, rows, cols // 2), jnp.bfloat16),
            pltpu.VMEM((rows, width), F32),
            pltpu.VMEM((2, cols // 2 + 8, width), F32),
            pltpu.VMEM((tiles, LANES), F32),
            pltpu.VMEM((rows, LANES), F32),
            pltpu.VMEM((rows, LANES), F32),
            pltpu.VMEM((rows, LANES), F32),
            pltpu.VMEM((tiles, 8, LANES), F32),
            pltpu.VMEM((tiles, 8, LANES), F32),
            pltpu.VMEM((tiles, 8, LANES), F32),
            pltpu.VMEM((rings, rows // LANES, LANES), F32),
            pltpu.VMEM((2 * chips, 2 * tiles, LANES), F32),
            pltpu.VMEM((rings, 8, LANES), F32),
            pltpu.VMEM((2, hub_rows, width), F32),
            pltpu.VMEM((2 * direct + 2, strip, width), F32),
            pltpu.VMEM((cols // 2 + 8, width), F32),
            pltpu.VMEM((chips, piece + 8, width), F32),
            pltpu.VMEM((chips, piece + 8, width), F32),
            dma((2,)),
            dma((2,)),
            dma((2,)),
            dma((7,)),
            dma((2,)),
            dma((8,)),
            dma((chips - 1,)),
            dma((2,)),
        ],
        compiler_params=pltpu.CompilerParams(
            collective_id=0, has_side_effects=True, vmem_limit_bytes=60 * 1024 * 1024
        ),
        name="two_sided",
    )(
        user_embed,
        item_embed,
        positive.reshape(rows // LANES, LANES),
        user_count.reshape(rows // LANES, LANES),
        item_count.reshape(tiles, LANES),
    )
    return user_grad, item_grad, loss.reshape(())


def solution(mesh):
    row_size, rings = mesh.shape["row"], mesh.shape["col"]

    def whole(user_embed, *others):
        body = functools.partial(per_device, user_embed.shape[0], row_size // 2, rings)
        return jax.shard_map(
            body,
            mesh=mesh,
            in_specs=(P("row", None), P("col", None), P("row"), P("row"), P("col")),
            out_specs=(P("row", None), P("col", None), P()),
            check_vma=False,
        )(user_embed, *others)

    return whole
```

```python
import functools

import jax
import jax.numpy as jnp
from jax import lax
from jax.experimental import pallas as pl
from jax.experimental.pallas import tpu as pltpu
from jax.sharding import PartitionSpec as P

MESH = pl.DeviceIdType.MESH
LANES = 128
BLOCK = 128
CORE_PARTS = 4
F32 = jnp.float32


def columns_of(row):
    return jnp.transpose(jnp.broadcast_to(row, (LANES, LANES)))


def fold(block):
    return block.reshape(block.shape[0] // 8, 8, LANES)


def merged_lse(parts):
    top = jnp.max(parts, axis=0)
    return top + jnp.log(jnp.sum(jnp.exp(parts - top[None]), axis=0))


def kernel(
    total_users,
    chips,
    rings,
    user_hbm,
    item_hbm,
    pos_ref,
    ucnt_ref,
    icnt_ref,
    ug_hbm,
    ig_hbm,
    loss_ref,
    ug_ref,
    ig_ref,
    user_ref,
    item_ref,
    users,
    scores,
    row_exp,
    col_exp,
    coupling,
    part,
    items,
    log_item,
    lu_col,
    pos_col,
    row_col,
    col_max,
    col_sum,
    hits_acc,
    z_stats,
    p_stats,
    z_loss,
    hub_in,
    near_in,
    core_in,
    plane_out,
    plane_in,
    z_sems,
    p_sems,
    l_sems,
    w_sems,
    g_sems,
    x_sems,
    back_sems,
    in_sems,
    out_sems,
):
    rows_here, width = user_ref.shape
    cols_here = item_ref.shape[0]
    tiles = cols_here // LANES
    row_tiles = rows_here // LANES
    half_cols = cols_here // 2
    half_tiles = tiles // 2
    blocks = rows_here // BLOCK
    piece = half_cols // chips

    user_in = pltpu.make_async_copy(user_hbm, user_ref, in_sems.at[0])
    item_in = pltpu.make_async_copy(item_hbm, item_ref, in_sems.at[1])
    item_in.start()
    user_in.start()

    mine = lax.axis_index("row")
    ring = lax.axis_index("col")
    chip = mine // 2
    core = mine % 2
    other = 1 - core
    twin = chip * 2 + other

    def z_peer(step):
        return (mine, (ring + step) % rings)

    def chip_peer(step):
        return (((chip + step) % chips) * 2 + core, ring)

    def row_peer(step):
        return ((mine + step) % (2 * chips), ring)

    z_steps = sorted(range(1, rings), key=lambda k: -min(k, rings - k))
    chip_steps = list(range(1, chips))
    row_steps = list(range(1, 2 * chips))

    barrier = pltpu.get_barrier_semaphore()
    for step in z_steps:
        pl.semaphore_signal(barrier, inc=1, device_id=z_peer(step), device_id_type=MESH)
    for step in row_steps:
        pl.semaphore_signal(barrier, inc=1, device_id=row_peer(step), device_id_type=MESH)

    def remote(src, dst, send_sem, recv_sem, device):
        return pltpu.make_async_remote_copy(
            src_ref=src,
            dst_ref=dst,
            send_sem=send_sem,
            recv_sem=recv_sem,
            device_id=device,
            device_id_type=MESH,
        )

    def wait_bytes(ref, sem):
        pltpu.make_async_copy(ref, ref, sem).wait()

    log_item[...] = jnp.log(icnt_ref[...].astype(F32))
    log_user = jnp.log(ucnt_ref[...].astype(F32))
    local_pos = pos_ref[...].astype(F32) - (ring * cols_here).astype(F32)
    for k in range(row_tiles):
        span = pl.ds(k * LANES, LANES)
        lu_col[span, :] = columns_of(log_user[k : k + 1, :])
        pos_col[span, :] = columns_of(local_pos[k : k + 1, :])
    col_max[...] = jnp.full(col_max.shape, -jnp.inf, F32)
    col_sum[...] = jnp.zeros(col_sum.shape, F32)
    hits_acc[...] = jnp.zeros(hits_acc.shape, F32)
    lane = lax.broadcasted_iota(jnp.int32, (BLOCK, LANES), 1).astype(F32)

    def sweep_one(b, z_part):
        span = pl.ds(pl.multiple_of(b * BLOCK, BLOCK), BLOCK)
        scores[span, :] = 2.0 * lax.dot_general(
            user_ref[span, :],
            item_ref[...],
            (((1,), (1,)), ((), ())),
            preferred_element_type=F32,
        )
        lu = lu_col[span, :]
        pos = pos_col[span, :]
        top = None
        for t in range(tiles):
            s = scores[span, t * LANES : (t + 1) * LANES]
            shifted = s - log_item[t : t + 1, :]
            top = shifted if top is None else jnp.maximum(top, shifted)
            col_max[t] = jnp.maximum(col_max[t], jnp.max(fold(s - lu), axis=0))
            match = pos == lane + float(t * LANES)
            hits_acc[t] += jnp.sum(fold(jnp.where(match, 1.0, 0.0)), axis=0)
            z_part = z_part + jnp.sum(fold(jnp.where(match, s + shifted, 0.0)), axis=0)
        row_col[span, :] = jnp.broadcast_to(jnp.max(top, axis=1, keepdims=True), (BLOCK, LANES))
        return z_part

    item_in.wait()
    user_in.wait()
    z_part = lax.fori_loop(0, blocks, sweep_one, jnp.zeros((8, LANES), F32))
    for t in range(tiles):
        col_max[t] = jnp.broadcast_to(jnp.max(col_max[t], axis=0, keepdims=True), (8, LANES))

    def sweep_two(b, carry):
        span = pl.ds(pl.multiple_of(b * BLOCK, BLOCK), BLOCK)
        lu = lu_col[span, :]
        row_max = row_col[span, :]
        total = jnp.zeros((BLOCK, LANES), F32)
        for t in range(tiles):
            s = scores[span, t * LANES : (t + 1) * LANES]
            row = jnp.exp(s - log_item[t : t + 1, :] - row_max)
            row_exp[span, t * LANES : (t + 1) * LANES] = row
            total = total + row
            col = jnp.exp(s - lu - col_max[t, 0:1, :])
            col_exp[span, t * LANES : (t + 1) * LANES] = col
            col_sum[t] += jnp.sum(fold(col), axis=0)
        lse = row_max + jnp.log(jnp.sum(total, axis=1, keepdims=True))
        z_stats[ring, pl.ds(b, 1), :] = jnp.transpose(lse)[0:1, :]
        return carry

    lax.fori_loop(0, blocks, sweep_two, 0)
    col_lse_rows = []
    hits_rows = []
    for t in range(tiles):
        total = jnp.sum(col_sum[t], axis=0, keepdims=True)
        col_lse_rows.append(col_max[t, 0:1, :] + jnp.log(total))
        hits_rows.append(jnp.sum(hits_acc[t], axis=0, keepdims=True))
    p_stats[mine] = jnp.concatenate(col_lse_rows + hits_rows, axis=0)

    pl.semaphore_wait(barrier, rings - 1 + 2 * chips - 1)
    for step in z_steps:
        remote(
            z_stats.at[ring], z_stats.at[ring], z_sems.at[0], z_sems.at[1], z_peer(step)
        ).start()
    for step in row_steps:
        remote(
            p_stats.at[mine], p_stats.at[mine], p_sems.at[0], p_sems.at[1], row_peer(step)
        ).start()
    wait_bytes(z_stats.at[pl.ds(0, rings - 1)], z_sems.at[1])
    row_lse = merged_lse(z_stats[...])
    for k in range(row_tiles):
        span = pl.ds(k * LANES, LANES)
        row_col[span, :] = jnp.exp(row_col[span, :] - columns_of(row_lse[k : k + 1, :]))
    user_loss = jnp.sum(row_lse + log_user, axis=0, keepdims=True)
    match_loss = jnp.sum(z_part, axis=0, keepdims=True)
    loss_rows = jnp.concatenate([user_loss, match_loss, jnp.zeros((6, LANES), F32)], axis=0)
    wait_bytes(p_stats.at[pl.ds(0, 2 * chips - 1)], p_sems.at[1])
    item_stats = p_stats[...]
    col_lse = merged_lse(item_stats[:, :tiles])
    pos_hits = jnp.sum(item_stats[:, tiles:], axis=0)
    item_loss = jnp.sum(pos_hits * col_lse, axis=0, keepdims=True)
    col_top = jnp.concatenate([col_max[t, 0:1, :] for t in range(tiles)], axis=0)
    col_scale = pos_hits * jnp.exp(col_top - col_lse)

    strip = rows_here // rings
    per_block = BLOCK // strip
    direct = rings // 8
    hub = 2 * direct + 1
    covers = [c for c in range(-direct, direct + 1) if c != 0 and hub + c < rings // 2]
    far = rings // 2 - hub
    order = [(direct + 1 + j) % rings for j in range(rings)]
    signs = (1, -1)

    def strip_at(offset):
        start = (ring + offset + rings) % rings * strip
        return pl.ds(pl.multiple_of(start, strip), strip)

    def part_at(offset):
        return pl.ds(order.index(offset % rings) * strip, strip)

    def z_at(offset):
        return z_peer(offset % rings)

    def halves(index):
        return pl.ds(index * (strip // 2), strip // 2)

    strip_lane = lane[:strip, :]

    def user_block(b):
        for j in range(b * per_block, (b + 1) * per_block):
            source = strip_at(order[j])
            target = pl.ds(j * strip, strip)
            users[target, :] = user_ref[source, :]
            pos = pos_col[source, :]
            row = row_col[source, :]
            for t in range(tiles):
                here = slice(t * LANES, (t + 1) * LANES)
                value = row_exp[source, here] * row + col_exp[source, here] * col_scale[t : t + 1, :]
                match = pos == strip_lane + float(t * LANES)
                value = value - jnp.where(match, 2.0, 0.0)
                at = (t % half_tiles) * LANES
                coupling[t // half_tiles, target, at : at + LANES] = value.astype(jnp.bfloat16)
        span = pl.ds(b * BLOCK, BLOCK)
        part[span, :] = 2.0 * (
            jnp.dot(coupling[0, span, :], item_ref[:half_cols, :], preferred_element_type=F32)
            + jnp.dot(coupling[1, span, :], item_ref[half_cols:, :], preferred_element_type=F32)
        )

    leaving = {}
    hub_half = pl.ds(len(covers) * strip, strip // 2)
    for index, sign in enumerate(signs):
        for slot, c in enumerate(covers):
            leaving.setdefault(-sign * (hub + c) % rings, []).append(
                (
                    part.at[part_at(-sign * (hub + c)), :],
                    hub_in.at[index, pl.ds(slot * strip, strip), :],
                    w_sems.at[0],
                    w_sems.at[1 + index],
                    z_at(-sign * c),
                )
            )
        leaving.setdefault(rings // 2, []).append(
            (
                part.at[pl.ds(part_at(rings // 2).start + index * (strip // 2), strip // 2), :],
                hub_in.at[index, hub_half, :],
                w_sems.at[0],
                w_sems.at[1 + index],
                z_at(-sign * far),
            )
        )
        for step in range(1, direct + 1):
            leaving.setdefault(-sign * step % rings, []).append(
                (
                    part.at[part_at(-sign * step), :],
                    near_in.at[index * direct + step - 1],
                    w_sems.at[3],
                    w_sems.at[4],
                    z_at(-sign * step),
                )
            )

    for b in range(blocks):
        user_block(b)
        for j in range(b * per_block, (b + 1) * per_block):
            for copy in leaving.get(order[j], ()):
                remote(*copy).start()

    def hub_sum(index):
        sign = signs[index]
        wait_bytes(hub_in.at[index], w_sems.at[1 + index])
        span = part_at(-sign * hub)
        total = part[span, :]
        for slot in range(len(covers)):
            total = total + hub_in[index, slot * strip : (slot + 1) * strip, :]
        part[span, :] = total
        half = pl.ds(span.start + index * (strip // 2), strip // 2)
        part[half, :] += hub_in[index, hub_half, :]
        remote(
            part.at[span, :],
            near_in.at[2 * direct + index],
            w_sems.at[3],
            w_sems.at[4],
            z_at(-sign * hub),
        ).start()

    def own_sum():
        wait_bytes(near_in, w_sems.at[4])
        total = part[part_at(0), :]
        for slot in range(2 * direct + 2):
            total = total + near_in[slot]
        span = strip_at(0)
        ug_ref[span, :] = total
        here = ug_ref.at[span, :]
        for index, sign in enumerate(signs):
            remote(here, here, w_sems.at[5], g_sems.at[index], z_at(sign * hub)).start()
        for step in range(1, direct + 1):
            for sign in signs:
                remote(here, here, w_sems.at[5], w_sems.at[6], z_at(sign * step)).start()

    def hub_spread(index):
        sign = signs[index]
        start = (ring - sign * hub + rings) % rings * strip
        here = ug_ref.at[pl.ds(pl.multiple_of(start, strip), strip), :]
        wait_bytes(here, g_sems.at[index])
        half_start = pl.multiple_of(start + index * (strip // 2), strip // 2)
        half = ug_ref.at[pl.ds(half_start, strip // 2), :]
        remote(half, half, w_sems.at[5], w_sems.at[6], z_at(sign * far)).start()
        for c in sorted(covers, key=lambda c: -abs(c)):
            remote(here, here, w_sems.at[5], w_sems.at[6], z_at(sign * c)).start()

    def gather_end():
        wait_bytes(ug_ref.at[pl.ds(0, (rings - 3) * strip), :], w_sems.at[6])

    def item_part(which):
        items[which, :half_cols, :] = 2.0 * lax.dot_general(
            coupling[which],
            users[...],
            (((0,), (0,)), ((), ())),
            preferred_element_type=F32,
        )

    core_rows = half_cols // CORE_PARTS

    def core_send():
        item_part(other)
        items[other, half_cols:, :LANES] = loss_rows
        items[other, half_cols:, LANES:] = jnp.zeros((8, width - LANES), F32)
        for k in range(CORE_PARTS):
            extra = 8 if k == CORE_PARTS - 1 else 0
            span = pl.ds(k * core_rows, core_rows + extra)
            remote(
                items.at[other, span, :],
                core_in.at[span, :],
                x_sems.at[0],
                x_sems.at[1],
                (twin, ring),
            ).start()

    def plane_send():
        wait_bytes(core_in, x_sems.at[1])
        pair_loss = core_in[half_cols:, :LANES] + loss_rows

        def pack(k, carry):
            span = pl.ds(pl.multiple_of(k * piece, piece), piece)
            plane_out[k, :piece, :] = items[core, span, :] + core_in[span, :]
            plane_out[k, piece:, :LANES] = pair_loss
            plane_out[k, piece:, LANES:] = jnp.zeros((8, width - LANES), F32)
            return carry

        lax.fori_loop(0, chips, pack, 0)
        for step in chip_steps:
            remote(
                plane_out.at[(chip + step) % chips],
                plane_in.at[chip],
                x_sems.at[2],
                x_sems.at[3],
                chip_peer(step),
            ).start()
        plane_in[chip] = plane_out[chip]

    def piece_at(half_index, index):
        start = half_index * half_cols + index % chips * piece
        return pl.ds(pl.multiple_of(start, piece), piece)

    def plane_sum():
        wait_bytes(plane_in.at[pl.ds(0, chips - 1)], x_sems.at[3])
        total = plane_in[0]
        for k in range(1, chips):
            total = total + plane_in[k]
        here = ig_ref.at[piece_at(core, chip), :]
        here[...] = total[:piece, :]
        for step in chip_steps:
            remote(
                here, here, x_sems.at[4], back_sems.at[step - 1], chip_peer(step)
            ).start()
        remote(here, here, x_sems.at[5], x_sems.at[6], (twin, ring)).start()
        z_loss[ring] = jnp.broadcast_to(
            item_loss - total[piece + 1 : piece + 2, :LANES], (8, LANES)
        )
        for step in z_steps:
            remote(
                z_loss.at[ring], z_loss.at[ring], l_sems.at[0], l_sems.at[1], z_peer(step)
            ).start()
        return total[piece : piece + 1, :LANES]

    def forward(step):
        here = ig_ref.at[piece_at(core, chip + chips - step), :]
        wait_bytes(here, back_sems.at[step - 1])
        remote(here, here, x_sems.at[5], x_sems.at[6], (twin, ring)).start()

    others = pl.ds(0, (chips - 1) * piece)

    def loss_end(users):
        wait_bytes(z_loss.at[pl.ds(0, rings - 1)], l_sems.at[1])
        total = users
        for k in range(rings):
            total = total + z_loss[k, 0:1, :]
        loss_ref[0, 0] = jnp.sum(total) * (1.0 / total_users)

    core_send()
    item_part(core)
    plane_send()
    hub_sum(0)
    hub_sum(1)
    own_sum()
    users_total = plane_sum()
    hub_spread(0)
    hub_spread(1)
    for step in chip_steps:
        forward(step)
    loss_end(users_total)
    def half_out(which):
        span = pl.ds(pl.multiple_of(which * half_cols, half_cols), half_cols)
        return pltpu.make_async_copy(ig_ref.at[span, :], ig_hbm.at[span, :], out_sems.at[which])

    half_out(core).start()
    gather_end()
    user_out = pltpu.make_async_copy(ug_ref, ug_hbm, out_sems.at[2])
    user_out.start()
    wait_bytes(ig_ref.at[pl.ds(0, half_cols), :], x_sems.at[6])
    half_out(other).start()

    wait_bytes(z_stats.at[pl.ds(0, rings - 1)], z_sems.at[0])
    wait_bytes(p_stats.at[pl.ds(0, 2 * chips - 1)], p_sems.at[0])
    wait_bytes(z_loss.at[pl.ds(0, rings - 1)], l_sems.at[0])
    wait_bytes(hub_in, w_sems.at[0])
    wait_bytes(near_in, w_sems.at[3])
    wait_bytes(ug_ref.at[pl.ds(0, (rings - 1) * strip), :], w_sems.at[5])
    wait_bytes(core_in, x_sems.at[0])
    wait_bytes(plane_in.at[pl.ds(0, chips - 1)], x_sems.at[2])
    wait_bytes(ig_ref.at[others, :], x_sems.at[4])
    wait_bytes(ig_ref.at[pl.ds(0, half_cols), :], x_sems.at[5])
    half_out(core).wait()
    user_out.wait()
    half_out(other).wait()


def copy_out(ug_in, ig_in, ug_out, ig_out, ug_here, ig_here, sems):
    loads = []
    stores = []
    for source, here, target, count in (
        (ug_in, ug_here, ug_out, 2),
        (ig_in, ig_here, ig_out, 4),
    ):
        rows = source.shape[0] // count
        for k in range(count):
            span = pl.ds(k * rows, rows)
            slot = len(loads)
            loads.append(
                pltpu.make_async_copy(source.at[span, :], here.at[span, :], sems.at[0, slot])
            )
            stores.append(
                pltpu.make_async_copy(here.at[span, :], target.at[span, :], sems.at[1, slot])
            )
    for load in loads:
        load.start()
    for load, store in zip(loads, stores):
        load.wait()
        store.start()
    for store in stores:
        store.wait()


def per_device(total_users, chips, rings, user_embed, item_embed, positive, user_count, item_count):
    rows, width = user_embed.shape
    cols = item_embed.shape[0]
    tiles = cols // LANES
    strip = rows // rings
    direct = rings // 8
    hub_rows = (2 * direct if rings > 8 else 1) * strip + strip // 2
    piece = cols // 2 // chips
    vmem = pl.BlockSpec(memory_space=pltpu.VMEM)
    hbm = pl.BlockSpec(memory_space=pltpu.HBM)
    dma = pltpu.SemaphoreType.DMA
    user_grad, item_grad, loss = pl.pallas_call(
        functools.partial(kernel, total_users, chips, rings),
        out_shape=(
            jax.ShapeDtypeStruct((rows, width), F32),
            jax.ShapeDtypeStruct((cols, width), F32),
            jax.ShapeDtypeStruct((1, 1), F32),
        ),
        in_specs=[hbm] * 2 + [vmem] * 3,
        out_specs=(hbm, hbm, pl.BlockSpec(memory_space=pltpu.SMEM)),
        scratch_shapes=[
            pltpu.VMEM((rows, width), F32),
            pltpu.VMEM((cols, width), F32),
            pltpu.VMEM((rows, width), user_embed.dtype),
            pltpu.VMEM((cols, width), item_embed.dtype),
            pltpu.VMEM((rows, width), user_embed.dtype),
            pltpu.VMEM((rows, cols), F32),
            pltpu.VMEM((rows, cols), F32),
            pltpu.VMEM((rows, cols), F32),
            pltpu.VMEM((2, rows, cols // 2), jnp.bfloat16),
            pltpu.VMEM((rows, width), F32),
            pltpu.VMEM((2, cols // 2 + 8, width), F32),
            pltpu.VMEM((tiles, LANES), F32),
            pltpu.VMEM((rows, LANES), F32),
            pltpu.VMEM((rows, LANES), F32),
            pltpu.VMEM((rows, LANES), F32),
            pltpu.VMEM((tiles, 8, LANES), F32),
            pltpu.VMEM((tiles, 8, LANES), F32),
            pltpu.VMEM((tiles, 8, LANES), F32),
            pltpu.VMEM((rings, rows // LANES, LANES), F32),
            pltpu.VMEM((2 * chips, 2 * tiles, LANES), F32),
            pltpu.VMEM((rings, 8, LANES), F32),
            pltpu.VMEM((2, hub_rows, width), F32),
            pltpu.VMEM((2 * direct + 2, strip, width), F32),
            pltpu.VMEM((cols // 2 + 8, width), F32),
            pltpu.VMEM((chips, piece + 8, width), F32),
            pltpu.VMEM((chips, piece + 8, width), F32),
            dma((2,)),
            dma((2,)),
            dma((2,)),
            dma((7,)),
            dma((2,)),
            dma((8,)),
            dma((chips - 1,)),
            dma((2,)),
            dma((3,)),
        ],
        compiler_params=pltpu.CompilerParams(
            collective_id=0, has_side_effects=True, vmem_limit_bytes=60 * 1024 * 1024
        ),
        name="two_sided",
    )(
        user_embed,
        item_embed,
        positive.reshape(rows // LANES, LANES),
        user_count.reshape(rows // LANES, LANES),
        item_count.reshape(tiles, LANES),
    )
    user_grad, item_grad = pl.pallas_call(
        copy_out,
        out_shape=(
            jax.ShapeDtypeStruct((rows, width), F32),
            jax.ShapeDtypeStruct((cols, width), F32),
        ),
        in_specs=[hbm] * 2,
        out_specs=(hbm, hbm),
        scratch_shapes=[
            pltpu.VMEM((rows, width), F32),
            pltpu.VMEM((cols, width), F32),
            dma((2, 6)),
        ],
        compiler_params=pltpu.CompilerParams(vmem_limit_bytes=60 * 1024 * 1024),
        name="copy_out",
    )(user_grad, item_grad)
    return user_grad, item_grad, loss.reshape(())


def solution(mesh):
    row_size, rings = mesh.shape["row"], mesh.shape["col"]

    def whole(user_embed, *others):
        body = functools.partial(per_device, user_embed.shape[0], row_size // 2, rings)
        return jax.shard_map(
            body,
            mesh=mesh,
            in_specs=(P("row", None), P("col", None), P("row"), P("row"), P("col")),
            out_specs=(P("row", None), P("col", None), P()),
            check_vma=False,
        )(user_embed, *others)

    return whole
```

```python
import functools

import jax
import jax.numpy as jnp
from jax import lax
from jax.experimental import pallas as pl
from jax.experimental.pallas import tpu as pltpu
from jax.sharding import PartitionSpec as P

MESH = pl.DeviceIdType.MESH
LANES = 128
BLOCK = 128
CORE_PARTS = 4
PARTS = 2
F32 = jnp.float32


def columns_of(row):
    return jnp.transpose(jnp.broadcast_to(row, (LANES, LANES)))


def fold(block):
    return block.reshape(block.shape[0] // 8, 8, LANES)


def merged_lse(parts):
    top = jnp.max(parts, axis=0)
    return top + jnp.log(jnp.sum(jnp.exp(parts - top[None]), axis=0))


def kernel(
    total_users,
    chips,
    rings,
    user_hbm,
    item_hbm,
    pos_ref,
    ucnt_ref,
    icnt_ref,
    ug_hbm,
    ig_hbm,
    loss_ref,
    ug_ref,
    ig_ref,
    user_ref,
    item_ref,
    users,
    scores,
    row_exp,
    col_exp,
    coupling,
    part,
    items,
    log_item,
    lu_col,
    pos_col,
    row_col,
    col_max,
    col_sum,
    hits_acc,
    z_stats,
    p_stats,
    z_loss,
    hub_in,
    near_in,
    core_in,
    plane_out,
    plane_in,
    p_loss,
    z_sems,
    p_sems,
    l_sems,
    w_sems,
    h_sems,
    n_sems,
    g_sems,
    x_sems,
    back_sems,
    in_sems,
    out_sems,
):
    rows_here, width = user_ref.shape
    cols_here = item_ref.shape[0]
    tiles = cols_here // LANES
    row_tiles = rows_here // LANES
    half_cols = cols_here // 2
    half_tiles = tiles // 2
    blocks = rows_here // BLOCK
    piece = half_cols // chips

    user_in = pltpu.make_async_copy(user_hbm, user_ref, in_sems.at[0])
    item_in = pltpu.make_async_copy(item_hbm, item_ref, in_sems.at[1])
    item_in.start()
    user_in.start()

    mine = lax.axis_index("row")
    ring = lax.axis_index("col")
    chip = mine // 2
    core = mine % 2
    other = 1 - core
    twin = chip * 2 + other

    def z_peer(step):
        return (mine, (ring + step) % rings)

    def chip_peer(step):
        return (((chip + step) % chips) * 2 + core, ring)

    def row_peer(step):
        return ((mine + step) % (2 * chips), ring)

    z_steps = sorted(range(1, rings), key=lambda k: -min(k, rings - k))
    chip_steps = list(range(1, chips))
    row_steps = list(range(1, 2 * chips))

    barrier = pltpu.get_barrier_semaphore()
    for step in z_steps:
        pl.semaphore_signal(barrier, inc=1, device_id=z_peer(step), device_id_type=MESH)
    for step in row_steps:
        pl.semaphore_signal(barrier, inc=1, device_id=row_peer(step), device_id_type=MESH)

    def remote(src, dst, send_sem, recv_sem, device):
        return pltpu.make_async_remote_copy(
            src_ref=src,
            dst_ref=dst,
            send_sem=send_sem,
            recv_sem=recv_sem,
            device_id=device,
            device_id_type=MESH,
        )

    def wait_bytes(ref, sem):
        pltpu.make_async_copy(ref, ref, sem).wait()

    log_item[...] = jnp.log(icnt_ref[...].astype(F32))
    log_user = jnp.log(ucnt_ref[...].astype(F32))
    local_pos = pos_ref[...].astype(F32) - (ring * cols_here).astype(F32)
    for k in range(row_tiles):
        span = pl.ds(k * LANES, LANES)
        lu_col[span, :] = columns_of(log_user[k : k + 1, :])
        pos_col[span, :] = columns_of(local_pos[k : k + 1, :])
    col_max[...] = jnp.full(col_max.shape, -jnp.inf, F32)
    col_sum[...] = jnp.zeros(col_sum.shape, F32)
    hits_acc[...] = jnp.zeros(hits_acc.shape, F32)
    lane = lax.broadcasted_iota(jnp.int32, (BLOCK, LANES), 1).astype(F32)

    def sweep_one(b, z_part):
        span = pl.ds(pl.multiple_of(b * BLOCK, BLOCK), BLOCK)
        scores[span, :] = 2.0 * lax.dot_general(
            user_ref[span, :],
            item_ref[...],
            (((1,), (1,)), ((), ())),
            preferred_element_type=F32,
        )
        lu = lu_col[span, :]
        pos = pos_col[span, :]
        top = None
        for t in range(tiles):
            s = scores[span, t * LANES : (t + 1) * LANES]
            shifted = s - log_item[t : t + 1, :]
            top = shifted if top is None else jnp.maximum(top, shifted)
            col_max[t] = jnp.maximum(col_max[t], jnp.max(fold(s - lu), axis=0))
            match = pos == lane + float(t * LANES)
            hits_acc[t] += jnp.sum(fold(jnp.where(match, 1.0, 0.0)), axis=0)
            z_part = z_part + jnp.sum(fold(jnp.where(match, s + shifted, 0.0)), axis=0)
        row_col[span, :] = jnp.broadcast_to(jnp.max(top, axis=1, keepdims=True), (BLOCK, LANES))
        return z_part

    item_in.wait()
    user_in.wait()
    z_part = lax.fori_loop(0, blocks, sweep_one, jnp.zeros((8, LANES), F32))
    for t in range(tiles):
        col_max[t] = jnp.broadcast_to(jnp.max(col_max[t], axis=0, keepdims=True), (8, LANES))

    def sweep_two(b, carry):
        span = pl.ds(pl.multiple_of(b * BLOCK, BLOCK), BLOCK)
        lu = lu_col[span, :]
        row_max = row_col[span, :]
        total = jnp.zeros((BLOCK, LANES), F32)
        for t in range(tiles):
            s = scores[span, t * LANES : (t + 1) * LANES]
            row = jnp.exp(s - log_item[t : t + 1, :] - row_max)
            row_exp[span, t * LANES : (t + 1) * LANES] = row
            total = total + row
            col = jnp.exp(s - lu - col_max[t, 0:1, :])
            col_exp[span, t * LANES : (t + 1) * LANES] = col
            col_sum[t] += jnp.sum(fold(col), axis=0)
        lse = row_max + jnp.log(jnp.sum(total, axis=1, keepdims=True))
        z_stats[ring, pl.ds(b, 1), :] = jnp.transpose(lse)[0:1, :]
        return carry

    lax.fori_loop(0, blocks, sweep_two, 0)
    col_lse_rows = []
    hits_rows = []
    for t in range(tiles):
        total = jnp.sum(col_sum[t], axis=0, keepdims=True)
        col_lse_rows.append(col_max[t, 0:1, :] + jnp.log(total))
        hits_rows.append(jnp.sum(hits_acc[t], axis=0, keepdims=True))
    p_stats[mine] = jnp.concatenate(col_lse_rows + hits_rows, axis=0)

    pl.semaphore_wait(barrier, rings - 1 + 2 * chips - 1)
    for step in z_steps:
        remote(
            z_stats.at[ring], z_stats.at[ring], z_sems.at[0], z_sems.at[1], z_peer(step)
        ).start()
    for step in row_steps:
        remote(
            p_stats.at[mine], p_stats.at[mine], p_sems.at[0], p_sems.at[1], row_peer(step)
        ).start()
    wait_bytes(z_stats.at[pl.ds(0, rings - 1)], z_sems.at[1])
    row_lse = merged_lse(z_stats[...])
    for k in range(row_tiles):
        span = pl.ds(k * LANES, LANES)
        row_col[span, :] = jnp.exp(row_col[span, :] - columns_of(row_lse[k : k + 1, :]))
    user_loss = jnp.sum(row_lse + log_user, axis=0, keepdims=True)
    match_loss = jnp.sum(z_part, axis=0, keepdims=True)
    loss_rows = jnp.concatenate([user_loss, match_loss, jnp.zeros((6, LANES), F32)], axis=0)
    wait_bytes(p_stats.at[pl.ds(0, 2 * chips - 1)], p_sems.at[1])
    item_stats = p_stats[...]
    col_lse = merged_lse(item_stats[:, :tiles])
    pos_hits = jnp.sum(item_stats[:, tiles:], axis=0)
    item_loss = jnp.sum(pos_hits * col_lse, axis=0, keepdims=True)
    col_top = jnp.concatenate([col_max[t, 0:1, :] for t in range(tiles)], axis=0)
    col_scale = pos_hits * jnp.exp(col_top - col_lse)

    strip = rows_here // rings
    sub = strip // PARTS
    per_block = BLOCK // sub
    direct = rings // 8
    hub = 2 * direct + 1
    covers = [c for c in range(-direct, direct + 1) if c != 0 and hub + c < rings // 2]
    far = rings // 2 - hub
    order = [(direct + 1 + j) % rings for j in range(rings)]
    signs = (1, -1)

    def sub_at(offset, h, start=0, size=None):
        size = sub if size is None else size
        first = (ring + offset + rings) % rings * strip + h * sub + start
        return pl.ds(pl.multiple_of(first, 8 if size < 16 else size), size)

    def part_at(offset, h):
        return pl.ds(h * (rows_here // PARTS) + order.index(offset % rings) * sub, sub)

    def z_at(offset):
        return z_peer(offset % rings)

    sub_lane = lane[:sub, :]

    def user_block(b):
        for k in range(b * per_block, (b + 1) * per_block):
            h, j = k // rings, k % rings
            source = sub_at(order[j], h)
            target = pl.ds(k * sub, sub)
            users[target, :] = user_ref[source, :]
            pos = pos_col[source, :]
            row = row_col[source, :]
            for t in range(tiles):
                here = slice(t * LANES, (t + 1) * LANES)
                value = row_exp[source, here] * row + col_exp[source, here] * col_scale[t : t + 1, :]
                match = pos == sub_lane + float(t * LANES)
                value = value - jnp.where(match, 2.0, 0.0)
                at = (t % half_tiles) * LANES
                coupling[t // half_tiles, target, at : at + LANES] = value.astype(jnp.bfloat16)
        span = pl.ds(b * BLOCK, BLOCK)
        part[span, :] = 2.0 * (
            jnp.dot(coupling[0, span, :], item_ref[:half_cols, :], preferred_element_type=F32)
            + jnp.dot(coupling[1, span, :], item_ref[half_cols:, :], preferred_element_type=F32)
        )

    leaving = {}
    hub_half = pl.ds(len(covers) * sub, sub // 2)
    for h in range(PARTS):
        for index, sign in enumerate(signs):
            for slot, c in enumerate(covers):
                leaving.setdefault((h, -sign * (hub + c) % rings), []).append(
                    (
                        part.at[part_at(-sign * (hub + c), h), :],
                        hub_in.at[h, index, pl.ds(slot * sub, sub), :],
                        w_sems.at[0],
                        h_sems.at[h, index],
                        z_at(-sign * c),
                    )
                )
            first = part_at(rings // 2, h).start + index * (sub // 2)
            leaving.setdefault((h, rings // 2), []).append(
                (
                    part.at[pl.ds(first, sub // 2), :],
                    hub_in.at[h, index, hub_half, :],
                    w_sems.at[0],
                    h_sems.at[h, index],
                    z_at(-sign * far),
                )
            )
            for step in range(1, direct + 1):
                leaving.setdefault((h, -sign * step % rings), []).append(
                    (
                        part.at[part_at(-sign * step, h), :],
                        near_in.at[h, index * direct + step - 1],
                        w_sems.at[1],
                        n_sems.at[h],
                        z_at(-sign * step),
                    )
                )

    for b in range(blocks):
        user_block(b)
        for k in range(b * per_block, (b + 1) * per_block):
            for copy in leaving.get((k // rings, order[k % rings]), ()):
                remote(*copy).start()

    def hub_sum(h):
        for index, sign in enumerate(signs):
            wait_bytes(hub_in.at[h, index], h_sems.at[h, index])
            span = part_at(-sign * hub, h)
            total = part[span, :]
            for slot in range(len(covers)):
                total = total + hub_in[h, index, slot * sub : (slot + 1) * sub, :]
            part[span, :] = total
            half = pl.ds(span.start + index * (sub // 2), sub // 2)
            part[half, :] += hub_in[h, index, hub_half, :]
            remote(
                part.at[span, :],
                near_in.at[h, 2 * direct + index],
                w_sems.at[1],
                n_sems.at[h],
                z_at(-sign * hub),
            ).start()

    def own_sum(h):
        wait_bytes(near_in.at[h], n_sems.at[h])
        total = part[part_at(0, h), :]
        for slot in range(2 * direct + 2):
            total = total + near_in[h, slot]
        span = sub_at(0, h)
        ug_ref[span, :] = total
        here = ug_ref.at[span, :]
        for index, sign in enumerate(signs):
            remote(here, here, w_sems.at[2], g_sems.at[h, index], z_at(sign * hub)).start()
        for step in range(1, direct + 1):
            for sign in signs:
                remote(here, here, w_sems.at[2], w_sems.at[3], z_at(sign * step)).start()

    def hub_spread(h):
        for index, sign in enumerate(signs):
            here = ug_ref.at[sub_at(-sign * hub, h), :]
            wait_bytes(here, g_sems.at[h, index])
            half = ug_ref.at[sub_at(-sign * hub, h, index * (sub // 2), sub // 2), :]
            remote(half, half, w_sems.at[2], w_sems.at[3], z_at(sign * far)).start()
            for c in sorted(covers, key=lambda c: -abs(c)):
                remote(here, here, w_sems.at[2], w_sems.at[3], z_at(sign * c)).start()

    def gather_end():
        wait_bytes(ug_ref.at[pl.ds(0, (rings - 3) * strip), :], w_sems.at[3])

    def item_part(which):
        items[which, :half_cols, :] = 2.0 * lax.dot_general(
            coupling[which],
            users[...],
            (((0,), (0,)), ((), ())),
            preferred_element_type=F32,
        )

    core_rows = half_cols // CORE_PARTS

    def core_send():
        item_part(other)
        items[other, half_cols:, :LANES] = loss_rows
        items[other, half_cols:, LANES:] = jnp.zeros((8, width - LANES), F32)
        for k in range(CORE_PARTS):
            extra = 8 if k == CORE_PARTS - 1 else 0
            span = pl.ds(k * core_rows, core_rows + extra)
            remote(
                items.at[other, span, :],
                core_in.at[span, :],
                x_sems.at[0],
                x_sems.at[1],
                (twin, ring),
            ).start()

    def plane_send():
        wait_bytes(core_in, x_sems.at[1])
        p_loss[chip] = core_in[half_cols:, :LANES] + loss_rows

        def pack(k, carry):
            span = pl.ds(pl.multiple_of(k * piece, piece), piece)
            plane_out[k] = items[core, span, :] + core_in[span, :]
            return carry

        lax.fori_loop(0, chips, pack, 0)
        for step in chip_steps:
            remote(
                plane_out.at[(chip + step) % chips],
                plane_in.at[chip],
                x_sems.at[2],
                x_sems.at[3],
                chip_peer(step),
            ).start()
        plane_in[chip] = plane_out[chip]

    def pair_loss_send():
        for step in chip_steps:
            remote(
                p_loss.at[chip], p_loss.at[chip], l_sems.at[2], l_sems.at[3], chip_peer(step)
            ).start()

    def pair_loss_sum():
        wait_bytes(p_loss.at[pl.ds(0, chips - 1)], l_sems.at[3])
        total = p_loss[0]
        for k in range(1, chips):
            total = total + p_loss[k]
        return total

    def piece_at(half_index, index):
        start = half_index * half_cols + index % chips * piece
        return pl.ds(pl.multiple_of(start, piece), piece)

    def plane_sum():
        wait_bytes(plane_in.at[pl.ds(0, chips - 1)], x_sems.at[3])
        total = plane_in[0]
        for k in range(1, chips):
            total = total + plane_in[k]
        here = ig_ref.at[piece_at(core, chip), :]
        here[...] = total
        for step in chip_steps:
            remote(
                here, here, x_sems.at[4], back_sems.at[step - 1], chip_peer(step)
            ).start()
        remote(here, here, x_sems.at[5], x_sems.at[6], (twin, ring)).start()

    def loss_send(total):
        z_loss[ring] = jnp.broadcast_to(item_loss - total[1:2, :], (8, LANES))
        for step in z_steps:
            remote(
                z_loss.at[ring], z_loss.at[ring], l_sems.at[0], l_sems.at[1], z_peer(step)
            ).start()

    def forward(step):
        here = ig_ref.at[piece_at(core, chip + chips - step), :]
        wait_bytes(here, back_sems.at[step - 1])
        remote(here, here, x_sems.at[5], x_sems.at[6], (twin, ring)).start()

    others = pl.ds(0, (chips - 1) * piece)

    def loss_end(users):
        wait_bytes(z_loss.at[pl.ds(0, rings - 1)], l_sems.at[1])
        total = users
        for k in range(rings):
            total = total + z_loss[k, 0:1, :]
        loss_ref[0, 0] = jnp.sum(total) * (1.0 / total_users)

    core_send()
    item_part(core)
    hub_sum(0)
    plane_send()
    hub_sum(1)
    own_sum(0)
    pair_loss_send()
    own_sum(1)
    plane_sum()
    hub_spread(0)
    hub_spread(1)
    plane_total = pair_loss_sum()
    loss_send(plane_total)
    for step in chip_steps:
        forward(step)
    loss_end(plane_total[0:1, :])

    def half_out(which):
        span = pl.ds(pl.multiple_of(which * half_cols, half_cols), half_cols)
        return pltpu.make_async_copy(ig_ref.at[span, :], ig_hbm.at[span, :], out_sems.at[which])

    half_out(core).start()
    gather_end()
    user_out = pltpu.make_async_copy(ug_ref, ug_hbm, out_sems.at[2])
    user_out.start()
    wait_bytes(ig_ref.at[pl.ds(0, half_cols), :], x_sems.at[6])
    half_out(other).start()

    wait_bytes(z_stats.at[pl.ds(0, rings - 1)], z_sems.at[0])
    wait_bytes(p_stats.at[pl.ds(0, 2 * chips - 1)], p_sems.at[0])
    wait_bytes(z_loss.at[pl.ds(0, rings - 1)], l_sems.at[0])
    wait_bytes(hub_in, w_sems.at[0])
    wait_bytes(near_in, w_sems.at[1])
    wait_bytes(ug_ref.at[pl.ds(0, (rings - 1) * strip), :], w_sems.at[2])
    wait_bytes(p_loss.at[pl.ds(0, chips - 1)], l_sems.at[2])
    wait_bytes(core_in, x_sems.at[0])
    wait_bytes(plane_in.at[pl.ds(0, chips - 1)], x_sems.at[2])
    wait_bytes(ig_ref.at[others, :], x_sems.at[4])
    wait_bytes(ig_ref.at[pl.ds(0, half_cols), :], x_sems.at[5])
    half_out(core).wait()
    user_out.wait()
    half_out(other).wait()


def copy_out(ug_in, ig_in, ug_out, ig_out, ug_here, ig_here, sems):
    loads = []
    stores = []
    for source, here, target, count in (
        (ug_in, ug_here, ug_out, 2),
        (ig_in, ig_here, ig_out, 4),
    ):
        rows = source.shape[0] // count
        for k in range(count):
            span = pl.ds(k * rows, rows)
            slot = len(loads)
            loads.append(
                pltpu.make_async_copy(source.at[span, :], here.at[span, :], sems.at[0, slot])
            )
            stores.append(
                pltpu.make_async_copy(here.at[span, :], target.at[span, :], sems.at[1, slot])
            )
    for load in loads:
        load.start()
    for load, store in zip(loads, stores):
        load.wait()
        store.start()
    for store in stores:
        store.wait()


def per_device(total_users, chips, rings, user_embed, item_embed, positive, user_count, item_count):
    rows, width = user_embed.shape
    cols = item_embed.shape[0]
    tiles = cols // LANES
    strip = rows // rings
    direct = rings // 8
    sub = strip // PARTS
    hub_rows = (2 * direct if rings > 8 else 1) * sub + sub // 2
    piece = cols // 2 // chips
    vmem = pl.BlockSpec(memory_space=pltpu.VMEM)
    hbm = pl.BlockSpec(memory_space=pltpu.HBM)
    dma = pltpu.SemaphoreType.DMA
    user_grad, item_grad, loss = pl.pallas_call(
        functools.partial(kernel, total_users, chips, rings),
        out_shape=(
            jax.ShapeDtypeStruct((rows, width), F32),
            jax.ShapeDtypeStruct((cols, width), F32),
            jax.ShapeDtypeStruct((1, 1), F32),
        ),
        in_specs=[hbm] * 2 + [vmem] * 3,
        out_specs=(hbm, hbm, pl.BlockSpec(memory_space=pltpu.SMEM)),
        scratch_shapes=[
            pltpu.VMEM((rows, width), F32),
            pltpu.VMEM((cols, width), F32),
            pltpu.VMEM((rows, width), user_embed.dtype),
            pltpu.VMEM((cols, width), item_embed.dtype),
            pltpu.VMEM((rows, width), user_embed.dtype),
            pltpu.VMEM((rows, cols), F32),
            pltpu.VMEM((rows, cols), F32),
            pltpu.VMEM((rows, cols), F32),
            pltpu.VMEM((2, rows, cols // 2), jnp.bfloat16),
            pltpu.VMEM((rows, width), F32),
            pltpu.VMEM((2, cols // 2 + 8, width), F32),
            pltpu.VMEM((tiles, LANES), F32),
            pltpu.VMEM((rows, LANES), F32),
            pltpu.VMEM((rows, LANES), F32),
            pltpu.VMEM((rows, LANES), F32),
            pltpu.VMEM((tiles, 8, LANES), F32),
            pltpu.VMEM((tiles, 8, LANES), F32),
            pltpu.VMEM((tiles, 8, LANES), F32),
            pltpu.VMEM((rings, rows // LANES, LANES), F32),
            pltpu.VMEM((2 * chips, 2 * tiles, LANES), F32),
            pltpu.VMEM((rings, 8, LANES), F32),
            pltpu.VMEM((PARTS, 2, hub_rows, width), F32),
            pltpu.VMEM((PARTS, 2 * direct + 2, sub, width), F32),
            pltpu.VMEM((cols // 2 + 8, width), F32),
            pltpu.VMEM((chips, piece, width), F32),
            pltpu.VMEM((chips, piece, width), F32),
            pltpu.VMEM((chips, 8, LANES), F32),
            dma((2,)),
            dma((2,)),
            dma((4,)),
            dma((4,)),
            dma((PARTS, 2)),
            dma((PARTS,)),
            dma((PARTS, 2)),
            dma((8,)),
            dma((chips - 1,)),
            dma((2,)),
            dma((3,)),
        ],
        compiler_params=pltpu.CompilerParams(
            collective_id=0, has_side_effects=True, vmem_limit_bytes=60 * 1024 * 1024
        ),
        name="two_sided",
    )(
        user_embed,
        item_embed,
        positive.reshape(rows // LANES, LANES),
        user_count.reshape(rows // LANES, LANES),
        item_count.reshape(tiles, LANES),
    )
    user_grad, item_grad = pl.pallas_call(
        copy_out,
        out_shape=(
            jax.ShapeDtypeStruct((rows, width), F32),
            jax.ShapeDtypeStruct((cols, width), F32),
        ),
        in_specs=[hbm] * 2,
        out_specs=(hbm, hbm),
        scratch_shapes=[
            pltpu.VMEM((rows, width), F32),
            pltpu.VMEM((cols, width), F32),
            dma((2, 6)),
        ],
        compiler_params=pltpu.CompilerParams(vmem_limit_bytes=60 * 1024 * 1024),
        name="copy_out",
    )(user_grad, item_grad)
    return user_grad, item_grad, loss.reshape(())


def solution(mesh):
    row_size, rings = mesh.shape["row"], mesh.shape["col"]

    def whole(user_embed, *others):
        body = functools.partial(per_device, user_embed.shape[0], row_size // 2, rings)
        return jax.shard_map(
            body,
            mesh=mesh,
            in_specs=(P("row", None), P("col", None), P("row"), P("row"), P("col")),
            out_specs=(P("row", None), P("col", None), P()),
            check_vma=False,
        )(user_embed, *others)

    return whole
```

```python
import functools

import jax
import jax.numpy as jnp
from jax import lax
from jax.experimental import pallas as pl
from jax.experimental.pallas import tpu as pltpu
from jax.sharding import PartitionSpec as P

MESH = pl.DeviceIdType.MESH
LANES = 128
BLOCK = 128
CORE_PARTS = 4
F32 = jnp.float32


def columns_of(row):
    return jnp.transpose(jnp.broadcast_to(row, (LANES, LANES)))


def fold(block):
    return block.reshape(block.shape[0] // 8, 8, LANES)


def merged_lse(parts):
    top = jnp.max(parts, axis=0)
    return top + jnp.log(jnp.sum(jnp.exp(parts - top[None]), axis=0))


def kernel(
    total_users,
    chips,
    rings,
    user_hbm,
    item_hbm,
    pos_ref,
    ucnt_ref,
    icnt_ref,
    ug_hbm,
    ig_hbm,
    loss_ref,
    ug_ref,
    ig_ref,
    user_ref,
    item_ref,
    users,
    scores,
    row_exp,
    col_exp,
    coupling,
    part,
    items,
    log_item,
    lu_col,
    pos_col,
    row_col,
    col_max,
    col_sum,
    hits_acc,
    z_stats,
    p_stats,
    z_loss,
    z_match,
    hub_in,
    near_in,
    core_in,
    plane_out,
    plane_in,
    z_sems,
    p_sems,
    l_sems,
    w_sems,
    g_sems,
    x_sems,
    back_sems,
    in_sems,
    out_sems,
):
    rows_here, width = user_ref.shape
    cols_here = item_ref.shape[0]
    tiles = cols_here // LANES
    row_tiles = rows_here // LANES
    half_cols = cols_here // 2
    half_tiles = tiles // 2
    blocks = rows_here // BLOCK
    piece = half_cols // chips

    user_in = pltpu.make_async_copy(user_hbm, user_ref, in_sems.at[0])
    item_in = pltpu.make_async_copy(item_hbm, item_ref, in_sems.at[1])
    item_in.start()
    user_in.start()

    mine = lax.axis_index("row")
    ring = lax.axis_index("col")
    chip = mine // 2
    core = mine - 2 * chip
    other = 1 - core
    twin = chip * 2 + other

    def around(start, size):
        places = [start + step for step in range(size)]
        return [jnp.where(place >= size, place - size, place) for place in places]

    rings_from = around(ring, rings)
    chips_from = around(chip, chips)
    rows_from = around(mine, 2 * chips)

    def z_peer(step):
        return (mine, rings_from[step])

    def chip_peer(step):
        return (chips_from[step] * 2 + core, ring)

    def row_peer(step):
        return (rows_from[step], ring)

    z_steps = sorted(range(1, rings), key=lambda k: -min(k, rings - k))
    chip_steps = list(range(1, chips))
    row_steps = list(range(1, 2 * chips))

    barrier = pltpu.get_barrier_semaphore()
    for step in z_steps:
        pl.semaphore_signal(barrier, inc=1, device_id=z_peer(step), device_id_type=MESH)
    for step in row_steps:
        pl.semaphore_signal(barrier, inc=1, device_id=row_peer(step), device_id_type=MESH)

    def remote(src, dst, send_sem, recv_sem, device):
        return pltpu.make_async_remote_copy(
            src_ref=src,
            dst_ref=dst,
            send_sem=send_sem,
            recv_sem=recv_sem,
            device_id=device,
            device_id_type=MESH,
        )

    def wait_bytes(ref, sem):
        pltpu.make_async_copy(ref, ref, sem).wait()

    log_item[...] = jnp.log(icnt_ref[...].astype(F32))
    log_user = jnp.log(ucnt_ref[...].astype(F32))
    local_pos = pos_ref[...].astype(F32) - (ring * cols_here).astype(F32)
    for k in range(row_tiles):
        span = pl.ds(k * LANES, LANES)
        lu_col[span, :] = columns_of(log_user[k : k + 1, :])
        pos_col[span, :] = columns_of(local_pos[k : k + 1, :])
    col_max[...] = jnp.full(col_max.shape, -jnp.inf, F32)
    col_sum[...] = jnp.zeros(col_sum.shape, F32)
    hits_acc[...] = jnp.zeros(hits_acc.shape, F32)
    lane = lax.broadcasted_iota(jnp.int32, (BLOCK, LANES), 1).astype(F32)

    def sweep_one(b, z_part):
        span = pl.ds(pl.multiple_of(b * BLOCK, BLOCK), BLOCK)
        scores[span, :] = 2.0 * lax.dot_general(
            user_ref[span, :],
            item_ref[...],
            (((1,), (1,)), ((), ())),
            preferred_element_type=F32,
        )
        lu = lu_col[span, :]
        pos = pos_col[span, :]
        top = None
        for t in range(tiles):
            s = scores[span, t * LANES : (t + 1) * LANES]
            shifted = s - log_item[t : t + 1, :]
            top = shifted if top is None else jnp.maximum(top, shifted)
            col_max[t] = jnp.maximum(col_max[t], jnp.max(fold(s - lu), axis=0))
            match = pos == lane + float(t * LANES)
            hits_acc[t] += jnp.sum(fold(jnp.where(match, 1.0, 0.0)), axis=0)
            z_part = z_part + jnp.sum(fold(jnp.where(match, s + shifted, 0.0)), axis=0)
        row_col[span, :] = jnp.broadcast_to(jnp.max(top, axis=1, keepdims=True), (BLOCK, LANES))
        return z_part

    item_in.wait()
    user_in.wait()
    z_part = lax.fori_loop(0, blocks, sweep_one, jnp.zeros((8, LANES), F32))
    for t in range(tiles):
        col_max[t] = jnp.broadcast_to(jnp.max(col_max[t], axis=0, keepdims=True), (8, LANES))

    def sweep_two(b, carry):
        span = pl.ds(pl.multiple_of(b * BLOCK, BLOCK), BLOCK)
        lu = lu_col[span, :]
        row_max = row_col[span, :]
        total = jnp.zeros((BLOCK, LANES), F32)
        for t in range(tiles):
            s = scores[span, t * LANES : (t + 1) * LANES]
            row = jnp.exp(s - log_item[t : t + 1, :] - row_max)
            row_exp[span, t * LANES : (t + 1) * LANES] = row
            total = total + row
            col = jnp.exp(s - lu - col_max[t, 0:1, :])
            col_exp[span, t * LANES : (t + 1) * LANES] = col
            col_sum[t] += jnp.sum(fold(col), axis=0)
        lse = row_max + jnp.log(jnp.sum(total, axis=1, keepdims=True))
        z_stats[ring, pl.ds(b, 1), :] = jnp.transpose(lse)[0:1, :]
        return carry

    lax.fori_loop(0, blocks, sweep_two, 0)
    col_lse_rows = []
    hits_rows = []
    for t in range(tiles):
        total = jnp.sum(col_sum[t], axis=0, keepdims=True)
        col_lse_rows.append(col_max[t, 0:1, :] + jnp.log(total))
        hits_rows.append(jnp.sum(hits_acc[t], axis=0, keepdims=True))
    p_stats[mine] = jnp.concatenate(col_lse_rows + hits_rows, axis=0)

    pl.semaphore_wait(barrier, rings - 1 + 2 * chips - 1)
    for step in z_steps:
        remote(
            z_stats.at[ring], z_stats.at[ring], z_sems.at[0], z_sems.at[1], z_peer(step)
        ).start()
    for step in row_steps:
        remote(
            p_stats.at[mine], p_stats.at[mine], p_sems.at[0], p_sems.at[1], row_peer(step)
        ).start()
    z_match[ring] = jnp.broadcast_to(jnp.sum(z_part, axis=0, keepdims=True), (8, LANES))
    for step in z_steps:
        remote(
            z_match.at[ring], z_match.at[ring], l_sems.at[2], l_sems.at[3], z_peer(step)
        ).start()
    wait_bytes(z_stats.at[pl.ds(0, rings - 1)], z_sems.at[1])
    row_lse = merged_lse(z_stats[...])
    for k in range(row_tiles):
        span = pl.ds(k * LANES, LANES)
        row_col[span, :] = jnp.exp(row_col[span, :] - columns_of(row_lse[k : k + 1, :]))
    user_loss = jnp.sum(row_lse + log_user, axis=0, keepdims=True)
    wait_bytes(p_stats.at[pl.ds(0, 2 * chips - 1)], p_sems.at[1])
    item_stats = p_stats[...]
    col_lse = merged_lse(item_stats[:, :tiles])
    pos_hits = jnp.sum(item_stats[:, tiles:], axis=0)
    item_loss = jnp.sum(pos_hits * col_lse, axis=0, keepdims=True)
    col_top = jnp.concatenate([col_max[t, 0:1, :] for t in range(tiles)], axis=0)
    col_scale = pos_hits * jnp.exp(col_top - col_lse)

    strip = rows_here // rings
    per_block = BLOCK // strip
    direct = rings // 8
    hub = 2 * direct + 1
    covers = [c for c in range(-direct, direct + 1) if c != 0 and hub + c < rings // 2]
    far = rings // 2 - hub
    order = [(direct + 1 + j) % rings for j in range(rings)]
    signs = (1, -1)

    def strip_at(offset):
        return pl.ds(pl.multiple_of(rings_from[offset % rings] * strip, strip), strip)

    def part_at(offset):
        return pl.ds(order.index(offset % rings) * strip, strip)

    def z_at(offset):
        return z_peer(offset % rings)

    def halves(index):
        return pl.ds(index * (strip // 2), strip // 2)

    strip_lane = lane[:strip, :]

    def user_block(b):
        for j in range(b * per_block, (b + 1) * per_block):
            source = strip_at(order[j])
            target = pl.ds(j * strip, strip)
            users[target, :] = user_ref[source, :]
            pos = pos_col[source, :]
            row = row_col[source, :]
            for t in range(tiles):
                here = slice(t * LANES, (t + 1) * LANES)
                value = row_exp[source, here] * row + col_exp[source, here] * col_scale[t : t + 1, :]
                match = pos == strip_lane + float(t * LANES)
                value = value - jnp.where(match, 2.0, 0.0)
                at = (t % half_tiles) * LANES
                coupling[t // half_tiles, target, at : at + LANES] = value.astype(jnp.bfloat16)
        span = pl.ds(b * BLOCK, BLOCK)
        part[span, :] = 2.0 * (
            jnp.dot(coupling[0, span, :], item_ref[:half_cols, :], preferred_element_type=F32)
            + jnp.dot(coupling[1, span, :], item_ref[half_cols:, :], preferred_element_type=F32)
        )

    leaving = {}
    hub_half = pl.ds(len(covers) * strip, strip // 2)
    for index, sign in enumerate(signs):
        for slot, c in enumerate(covers):
            leaving.setdefault(-sign * (hub + c) % rings, []).append(
                (
                    part.at[part_at(-sign * (hub + c)), :],
                    hub_in.at[index, pl.ds(slot * strip, strip), :],
                    w_sems.at[0],
                    w_sems.at[1 + index],
                    z_at(-sign * c),
                )
            )
        leaving.setdefault(rings // 2, []).append(
            (
                part.at[pl.ds(part_at(rings // 2).start + index * (strip // 2), strip // 2), :],
                hub_in.at[index, hub_half, :],
                w_sems.at[0],
                w_sems.at[1 + index],
                z_at(-sign * far),
            )
        )
        for step in range(1, direct + 1):
            leaving.setdefault(-sign * step % rings, []).append(
                (
                    part.at[part_at(-sign * step), :],
                    near_in.at[index * direct + step - 1],
                    w_sems.at[3],
                    w_sems.at[4],
                    z_at(-sign * step),
                )
            )

    for b in range(blocks):
        user_block(b)
        for j in range(b * per_block, (b + 1) * per_block):
            for copy in leaving.get(order[j], ()):
                remote(*copy).start()

    def hub_sum(index):
        sign = signs[index]
        wait_bytes(hub_in.at[index], w_sems.at[1 + index])
        span = part_at(-sign * hub)
        total = part[span, :]
        for slot in range(len(covers)):
            total = total + hub_in[index, slot * strip : (slot + 1) * strip, :]
        part[span, :] = total
        half = pl.ds(span.start + index * (strip // 2), strip // 2)
        part[half, :] += hub_in[index, hub_half, :]
        remote(
            part.at[span, :],
            near_in.at[2 * direct + index],
            w_sems.at[3],
            w_sems.at[4],
            z_at(-sign * hub),
        ).start()

    def own_sum():
        wait_bytes(near_in, w_sems.at[4])
        total = part[part_at(0), :]
        for slot in range(2 * direct + 2):
            total = total + near_in[slot]
        span = strip_at(0)
        ug_ref[span, :] = total
        here = ug_ref.at[span, :]
        for index, sign in enumerate(signs):
            remote(here, here, w_sems.at[5], g_sems.at[index], z_at(sign * hub)).start()
        for step in range(1, direct + 1):
            for sign in signs:
                remote(here, here, w_sems.at[5], w_sems.at[6], z_at(sign * step)).start()

    def hub_spread(index):
        sign = signs[index]
        start = rings_from[-sign * hub % rings] * strip
        here = ug_ref.at[pl.ds(pl.multiple_of(start, strip), strip), :]
        wait_bytes(here, g_sems.at[index])
        half_start = pl.multiple_of(start + index * (strip // 2), strip // 2)
        half = ug_ref.at[pl.ds(half_start, strip // 2), :]
        remote(half, half, w_sems.at[5], w_sems.at[6], z_at(sign * far)).start()
        for c in sorted(covers, key=lambda c: -abs(c)):
            remote(here, here, w_sems.at[5], w_sems.at[6], z_at(sign * c)).start()

    def gather_end():
        wait_bytes(ug_ref.at[pl.ds(0, (rings - 3) * strip), :], w_sems.at[6])

    def item_part(which):
        items[which, :half_cols, :] = 2.0 * lax.dot_general(
            coupling[which],
            users[...],
            (((0,), (0,)), ((), ())),
            preferred_element_type=F32,
        )

    core_rows = half_cols // CORE_PARTS

    def loss_send():
        z_loss[ring] = jnp.broadcast_to(item_loss, (8, LANES))
        for step in z_steps:
            remote(
                z_loss.at[ring], z_loss.at[ring], l_sems.at[0], l_sems.at[1], z_peer(step)
            ).start()

    def loss_rows():
        total = z_match[0]
        for k in range(1, rings):
            total = total + z_match[k]
        return user_loss - total

    def core_send():
        item_part(other)
        wait_bytes(z_match.at[pl.ds(0, rings - 1)], l_sems.at[3])
        items[other, half_cols:, :LANES] = loss_rows()
        items[other, half_cols:, LANES:] = jnp.zeros((8, width - LANES), F32)
        for k in range(CORE_PARTS):
            extra = 8 if k == CORE_PARTS - 1 else 0
            span = pl.ds(k * core_rows, core_rows + extra)
            remote(
                items.at[other, span, :],
                core_in.at[span, :],
                x_sems.at[0],
                x_sems.at[1],
                (twin, ring),
            ).start()

    def plane_send():
        wait_bytes(core_in, x_sems.at[1])
        pair_loss = core_in[half_cols:, :LANES] + loss_rows()

        def pack(k, carry):
            span = pl.ds(pl.multiple_of(k * piece, piece), piece)
            plane_out[k, :piece, :] = items[core, span, :] + core_in[span, :]
            plane_out[k, piece:, :LANES] = pair_loss
            plane_out[k, piece:, LANES:] = jnp.zeros((8, width - LANES), F32)
            return carry

        lax.fori_loop(0, chips, pack, 0)
        for step in chip_steps:
            remote(
                plane_out.at[chips_from[step]],
                plane_in.at[chip],
                x_sems.at[2],
                x_sems.at[3],
                chip_peer(step),
            ).start()
        plane_in[chip] = plane_out[chip]

    def piece_at(half_index, index):
        start = half_index * half_cols + index * piece
        return pl.ds(pl.multiple_of(start, piece), piece)

    def plane_sum():
        wait_bytes(plane_in.at[pl.ds(0, chips - 1)], x_sems.at[3])
        total = plane_in[0]
        for k in range(1, chips):
            total = total + plane_in[k]
        here = ig_ref.at[piece_at(core, chip), :]
        here[...] = total[:piece, :]
        for step in chip_steps:
            remote(
                here, here, x_sems.at[4], back_sems.at[step - 1], chip_peer(step)
            ).start()
        remote(here, here, x_sems.at[5], x_sems.at[6], (twin, ring)).start()
        return total[piece : piece + 8, :LANES]

    def forward(step):
        here = ig_ref.at[piece_at(core, chips_from[chips - step]), :]
        wait_bytes(here, back_sems.at[step - 1])
        remote(here, here, x_sems.at[5], x_sems.at[6], (twin, ring)).start()

    others = pl.ds(0, (chips - 1) * piece)

    def loss_end(users):
        wait_bytes(z_loss.at[pl.ds(0, rings - 1)], l_sems.at[1])
        total = users
        for k in range(rings):
            total = total + z_loss[k, 0:1, :]
        loss_ref[0, 0] = jnp.sum(total) * (1.0 / total_users)

    core_send()
    item_part(core)
    loss_send()
    hub_sum(0)
    hub_sum(1)
    plane_send()
    own_sum()
    plane_total = plane_sum()
    hub_spread(0)
    hub_spread(1)
    for step in chip_steps:
        forward(step)
    loss_end(plane_total[0:1, :])
    def half_out(which):
        span = pl.ds(pl.multiple_of(which * half_cols, half_cols), half_cols)
        return pltpu.make_async_copy(ig_ref.at[span, :], ig_hbm.at[span, :], out_sems.at[which])

    half_out(core).start()
    gather_end()
    user_out = pltpu.make_async_copy(ug_ref, ug_hbm, out_sems.at[2])
    user_out.start()
    wait_bytes(ig_ref.at[pl.ds(0, half_cols), :], x_sems.at[6])
    half_out(other).start()

    wait_bytes(z_stats.at[pl.ds(0, rings - 1)], z_sems.at[0])
    wait_bytes(p_stats.at[pl.ds(0, 2 * chips - 1)], p_sems.at[0])
    wait_bytes(z_loss.at[pl.ds(0, rings - 1)], l_sems.at[0])
    wait_bytes(z_match.at[pl.ds(0, rings - 1)], l_sems.at[2])
    wait_bytes(hub_in, w_sems.at[0])
    wait_bytes(near_in, w_sems.at[3])
    wait_bytes(ug_ref.at[pl.ds(0, (rings - 1) * strip), :], w_sems.at[5])
    wait_bytes(core_in, x_sems.at[0])
    wait_bytes(plane_in.at[pl.ds(0, chips - 1)], x_sems.at[2])
    wait_bytes(ig_ref.at[others, :], x_sems.at[4])
    wait_bytes(ig_ref.at[pl.ds(0, half_cols), :], x_sems.at[5])
    half_out(core).wait()
    user_out.wait()
    half_out(other).wait()


def copy_out(ug_in, ig_in, ug_out, ig_out, ug_here, ig_here, sems):
    loads = []
    stores = []
    for source, here, target, count in (
        (ug_in, ug_here, ug_out, 2),
        (ig_in, ig_here, ig_out, 4),
    ):
        rows = source.shape[0] // count
        for k in range(count):
            span = pl.ds(k * rows, rows)
            slot = len(loads)
            loads.append(
                pltpu.make_async_copy(source.at[span, :], here.at[span, :], sems.at[0, slot])
            )
            stores.append(
                pltpu.make_async_copy(here.at[span, :], target.at[span, :], sems.at[1, slot])
            )
    for load in loads:
        load.start()
    for load, store in zip(loads, stores):
        load.wait()
        store.start()
    for store in stores:
        store.wait()


def per_device(total_users, chips, rings, user_embed, item_embed, positive, user_count, item_count):
    rows, width = user_embed.shape
    cols = item_embed.shape[0]
    tiles = cols // LANES
    strip = rows // rings
    direct = rings // 8
    hub_rows = (2 * direct if rings > 8 else 1) * strip + strip // 2
    piece = cols // 2 // chips
    vmem = pl.BlockSpec(memory_space=pltpu.VMEM)
    hbm = pl.BlockSpec(memory_space=pltpu.HBM)
    dma = pltpu.SemaphoreType.DMA
    user_grad, item_grad, loss = pl.pallas_call(
        functools.partial(kernel, total_users, chips, rings),
        out_shape=(
            jax.ShapeDtypeStruct((rows, width), F32),
            jax.ShapeDtypeStruct((cols, width), F32),
            jax.ShapeDtypeStruct((1, 1), F32),
        ),
        in_specs=[hbm] * 2 + [vmem] * 3,
        out_specs=(hbm, hbm, pl.BlockSpec(memory_space=pltpu.SMEM)),
        scratch_shapes=[
            pltpu.VMEM((rows, width), F32),
            pltpu.VMEM((cols, width), F32),
            pltpu.VMEM((rows, width), user_embed.dtype),
            pltpu.VMEM((cols, width), item_embed.dtype),
            pltpu.VMEM((rows, width), user_embed.dtype),
            pltpu.VMEM((rows, cols), F32),
            pltpu.VMEM((rows, cols), F32),
            pltpu.VMEM((rows, cols), F32),
            pltpu.VMEM((2, rows, cols // 2), jnp.bfloat16),
            pltpu.VMEM((rows, width), F32),
            pltpu.VMEM((2, cols // 2 + 8, width), F32),
            pltpu.VMEM((tiles, LANES), F32),
            pltpu.VMEM((rows, LANES), F32),
            pltpu.VMEM((rows, LANES), F32),
            pltpu.VMEM((rows, LANES), F32),
            pltpu.VMEM((tiles, 8, LANES), F32),
            pltpu.VMEM((tiles, 8, LANES), F32),
            pltpu.VMEM((tiles, 8, LANES), F32),
            pltpu.VMEM((rings, rows // LANES, LANES), F32),
            pltpu.VMEM((2 * chips, 2 * tiles, LANES), F32),
            pltpu.VMEM((rings, 8, LANES), F32),
            pltpu.VMEM((rings, 8, LANES), F32),
            pltpu.VMEM((2, hub_rows, width), F32),
            pltpu.VMEM((2 * direct + 2, strip, width), F32),
            pltpu.VMEM((cols // 2 + 8, width), F32),
            pltpu.VMEM((chips, piece + 8, width), F32),
            pltpu.VMEM((chips, piece + 8, width), F32),
            dma((2,)),
            dma((2,)),
            dma((4,)),
            dma((7,)),
            dma((2,)),
            dma((8,)),
            dma((chips - 1,)),
            dma((2,)),
            dma((3,)),
        ],
        compiler_params=pltpu.CompilerParams(
            collective_id=0, has_side_effects=True, vmem_limit_bytes=60 * 1024 * 1024
        ),
        name="two_sided",
    )(
        user_embed,
        item_embed,
        positive.reshape(rows // LANES, LANES),
        user_count.reshape(rows // LANES, LANES),
        item_count.reshape(tiles, LANES),
    )
    user_grad, item_grad = pl.pallas_call(
        copy_out,
        out_shape=(
            jax.ShapeDtypeStruct((rows, width), F32),
            jax.ShapeDtypeStruct((cols, width), F32),
        ),
        in_specs=[hbm] * 2,
        out_specs=(hbm, hbm),
        scratch_shapes=[
            pltpu.VMEM((rows, width), F32),
            pltpu.VMEM((cols, width), F32),
            dma((2, 6)),
        ],
        compiler_params=pltpu.CompilerParams(vmem_limit_bytes=60 * 1024 * 1024),
        name="copy_out",
    )(user_grad, item_grad)
    return user_grad, item_grad, loss.reshape(())


def solution(mesh):
    row_size, rings = mesh.shape["row"], mesh.shape["col"]

    def whole(user_embed, *others):
        body = functools.partial(per_device, user_embed.shape[0], row_size // 2, rings)
        return jax.shard_map(
            body,
            mesh=mesh,
            in_specs=(P("row", None), P("col", None), P("row"), P("row"), P("col")),
            out_specs=(P("row", None), P("col", None), P()),
            check_vma=False,
        )(user_embed, *others)

    return whole
```

```python
import functools

import jax
import jax.numpy as jnp
from jax import lax
from jax.experimental import pallas as pl
from jax.experimental.pallas import tpu as pltpu
from jax.sharding import PartitionSpec as P

MESH = pl.DeviceIdType.MESH
LANES = 128
BLOCK = 128
GROUP = 64
CORE_PARTS = 4
F32 = jnp.float32


def columns_of(row):
    return jnp.transpose(jnp.broadcast_to(row, (LANES, LANES)))


def fold(block):
    return block.reshape(block.shape[0] // 8, 8, LANES)


def merged_lse(parts):
    top = jnp.max(parts, axis=0)
    return top + jnp.log(jnp.sum(jnp.exp(parts - top[None]), axis=0))


def kernel(
    total_users,
    chips,
    rings,
    user_hbm,
    item_hbm,
    pos_ref,
    ucnt_ref,
    icnt_ref,
    ug_hbm,
    ig_hbm,
    loss_ref,
    ug_ref,
    ig_ref,
    user_ref,
    item_ref,
    users,
    scores,
    row_exp,
    col_exp,
    coupling,
    part,
    items,
    log_item,
    lu_col,
    pos_col,
    row_col,
    row_lse_col,
    col_max,
    col_sum,
    hits_acc,
    z_stats,
    p_stats,
    z_loss,
    hub_in,
    near_in,
    core_in,
    plane_out,
    plane_in,
    z_sems,
    p_sems,
    l_sems,
    w_sems,
    g_sems,
    x_sems,
    back_sems,
    in_sems,
    out_sems,
):
    rows_here, width = user_ref.shape
    cols_here = item_ref.shape[0]
    tiles = cols_here // LANES
    row_tiles = rows_here // LANES
    half_cols = cols_here // 2
    half_tiles = tiles // 2
    blocks = rows_here // BLOCK
    piece = half_cols // chips

    user_in = pltpu.make_async_copy(user_hbm, user_ref, in_sems.at[0])
    item_in = pltpu.make_async_copy(item_hbm, item_ref, in_sems.at[1])
    item_in.start()
    user_in.start()

    mine = lax.axis_index("row")
    ring = lax.axis_index("col")
    chip = mine // 2
    core = mine % 2
    other = 1 - core
    twin = chip * 2 + other

    def z_peer(step):
        return (mine, (ring + step) % rings)

    def chip_peer(step):
        return (((chip + step) % chips) * 2 + core, ring)

    def row_peer(step):
        return ((mine + step) % (2 * chips), ring)

    z_steps = sorted(range(1, rings), key=lambda k: -min(k, rings - k))
    chip_steps = list(range(1, chips))
    row_steps = list(range(1, 2 * chips))

    barrier = pltpu.get_barrier_semaphore()
    for step in z_steps:
        pl.semaphore_signal(barrier, inc=1, device_id=z_peer(step), device_id_type=MESH)
    for step in row_steps:
        pl.semaphore_signal(barrier, inc=1, device_id=row_peer(step), device_id_type=MESH)

    def remote(src, dst, send_sem, recv_sem, device):
        return pltpu.make_async_remote_copy(
            src_ref=src,
            dst_ref=dst,
            send_sem=send_sem,
            recv_sem=recv_sem,
            device_id=device,
            device_id_type=MESH,
        )

    def wait_bytes(ref, sem):
        pltpu.make_async_copy(ref, ref, sem).wait()

    log_item[...] = jnp.log(icnt_ref[...].astype(F32))
    log_user = jnp.log(ucnt_ref[...].astype(F32))
    local_pos = pos_ref[...].astype(F32) - (ring * cols_here).astype(F32)
    for k in range(row_tiles):
        span = pl.ds(k * LANES, LANES)
        lu_col[span, :] = columns_of(log_user[k : k + 1, :])
        pos_col[span, :] = columns_of(local_pos[k : k + 1, :])
    lane = lax.broadcasted_iota(jnp.int32, (BLOCK, LANES), 1).astype(F32)

    groups = [pl.ds(g * GROUP, GROUP) for g in range(rows_here // GROUP)]
    group_lane = lane[:GROUP, :]

    item_in.wait()
    user_in.wait()
    z_part = jnp.zeros((8, LANES), F32)
    for n in range(cols_here // width):
        scores[:, n * width : (n + 1) * width] = 2.0 * lax.dot_general(
            user_ref[...],
            item_ref[n * width : (n + 1) * width, :],
            (((1,), (1,)), ((), ())),
            preferred_element_type=F32,
        )
        for t in range(n * width // LANES, (n + 1) * width // LANES):
            here = slice(t * LANES, (t + 1) * LANES)
            tops = None
            hits = None
            for span in groups:
                s = scores[span, here]
                shifted = s - log_item[t : t + 1, :]
                row_col[span, :] = shifted if t == 0 else jnp.maximum(row_col[span, :], shifted)
                top = jnp.max(fold(s - lu_col[span, :]), axis=0)
                tops = top if tops is None else jnp.maximum(tops, top)
                match = pos_col[span, :] == group_lane + float(t * LANES)
                hit = jnp.sum(fold(jnp.where(match, 1.0, 0.0)), axis=0)
                hits = hit if hits is None else hits + hit
                z_part = z_part + jnp.sum(fold(jnp.where(match, s + shifted, 0.0)), axis=0)
            hits_acc[t] = hits
            top = jnp.broadcast_to(jnp.max(tops, axis=0, keepdims=True), (8, LANES))
            col_max[t] = top
            total = jnp.zeros((8, LANES), F32)
            for span in groups:
                col = jnp.exp(scores[span, here] - lu_col[span, :] - top[0:1, :])
                col_exp[span, here] = col
                total = total + jnp.sum(fold(col), axis=0)
            col_sum[t] = total

    for span in groups:
        row_max = jnp.max(row_col[span, :], axis=1, keepdims=True)
        row_max = jnp.broadcast_to(row_max, (GROUP, LANES))
        row_col[span, :] = row_max
        total = jnp.zeros((GROUP, LANES), F32)
        for t in range(tiles):
            here = slice(t * LANES, (t + 1) * LANES)
            row = jnp.exp(scores[span, here] - log_item[t : t + 1, :] - row_max)
            row_exp[span, here] = row
            total = total + row
        lse = row_max + jnp.log(jnp.sum(total, axis=1, keepdims=True))
        row_lse_col[span, :] = lse
    for k in range(row_tiles):
        block = row_lse_col[pl.ds(k * LANES, LANES), :]
        z_stats[ring, k : k + 1, :] = jnp.transpose(block)[0:1, :]
    col_lse_rows = []
    hits_rows = []
    for t in range(tiles):
        total = jnp.sum(col_sum[t], axis=0, keepdims=True)
        col_lse_rows.append(col_max[t, 0:1, :] + jnp.log(total))
        hits_rows.append(jnp.sum(hits_acc[t], axis=0, keepdims=True))
    p_stats[mine] = jnp.concatenate(col_lse_rows + hits_rows, axis=0)

    pl.semaphore_wait(barrier, rings - 1 + 2 * chips - 1)
    for step in z_steps:
        remote(
            z_stats.at[ring], z_stats.at[ring], z_sems.at[0], z_sems.at[1], z_peer(step)
        ).start()
    for step in row_steps:
        remote(
            p_stats.at[mine], p_stats.at[mine], p_sems.at[0], p_sems.at[1], row_peer(step)
        ).start()
    wait_bytes(z_stats.at[pl.ds(0, rings - 1)], z_sems.at[1])
    row_lse = merged_lse(z_stats[...])
    for k in range(row_tiles):
        span = pl.ds(k * LANES, LANES)
        row_col[span, :] = jnp.exp(row_col[span, :] - columns_of(row_lse[k : k + 1, :]))
    user_loss = jnp.sum(row_lse + log_user, axis=0, keepdims=True)
    match_loss = jnp.sum(z_part, axis=0, keepdims=True)
    loss_rows = jnp.concatenate([user_loss, match_loss, jnp.zeros((6, LANES), F32)], axis=0)
    wait_bytes(p_stats.at[pl.ds(0, 2 * chips - 1)], p_sems.at[1])
    item_stats = p_stats[...]
    col_lse = merged_lse(item_stats[:, :tiles])
    pos_hits = jnp.sum(item_stats[:, tiles:], axis=0)
    item_loss = jnp.sum(pos_hits * col_lse, axis=0, keepdims=True)
    col_top = jnp.concatenate([col_max[t, 0:1, :] for t in range(tiles)], axis=0)
    col_scale = pos_hits * jnp.exp(col_top - col_lse)

    strip = rows_here // rings
    per_block = BLOCK // strip
    direct = rings // 8
    hub = 2 * direct + 1
    covers = [c for c in range(-direct, direct + 1) if c != 0 and hub + c < rings // 2]
    far = rings // 2 - hub
    order = [(direct + 1 + j) % rings for j in range(rings)]
    signs = (1, -1)

    def strip_at(offset):
        start = (ring + offset + rings) % rings * strip
        return pl.ds(pl.multiple_of(start, strip), strip)

    def part_at(offset):
        return pl.ds(order.index(offset % rings) * strip, strip)

    def z_at(offset):
        return z_peer(offset % rings)

    def halves(index):
        return pl.ds(index * (strip // 2), strip // 2)

    strip_lane = lane[:strip, :]

    def user_block(b):
        for j in range(b * per_block, (b + 1) * per_block):
            source = strip_at(order[j])
            target = pl.ds(j * strip, strip)
            users[target, :] = user_ref[source, :]
            pos = pos_col[source, :]
            row = row_col[source, :]
            for t in range(tiles):
                here = slice(t * LANES, (t + 1) * LANES)
                value = row_exp[source, here] * row + col_exp[source, here] * col_scale[t : t + 1, :]
                match = pos == strip_lane + float(t * LANES)
                value = value - jnp.where(match, 2.0, 0.0)
                at = (t % half_tiles) * LANES
                coupling[t // half_tiles, target, at : at + LANES] = value.astype(jnp.bfloat16)
        span = pl.ds(b * BLOCK, BLOCK)
        part[span, :] = 2.0 * (
            jnp.dot(coupling[0, span, :], item_ref[:half_cols, :], preferred_element_type=F32)
            + jnp.dot(coupling[1, span, :], item_ref[half_cols:, :], preferred_element_type=F32)
        )

    leaving = {}
    hub_half = pl.ds(len(covers) * strip, strip // 2)
    for index, sign in enumerate(signs):
        for slot, c in enumerate(covers):
            leaving.setdefault(-sign * (hub + c) % rings, []).append(
                (
                    part.at[part_at(-sign * (hub + c)), :],
                    hub_in.at[index, pl.ds(slot * strip, strip), :],
                    w_sems.at[0],
                    w_sems.at[1 + index],
                    z_at(-sign * c),
                )
            )
        leaving.setdefault(rings // 2, []).append(
            (
                part.at[pl.ds(part_at(rings // 2).start + index * (strip // 2), strip // 2), :],
                hub_in.at[index, hub_half, :],
                w_sems.at[0],
                w_sems.at[1 + index],
                z_at(-sign * far),
            )
        )
        for step in range(1, direct + 1):
            leaving.setdefault(-sign * step % rings, []).append(
                (
                    part.at[part_at(-sign * step), :],
                    near_in.at[index * direct + step - 1],
                    w_sems.at[3],
                    w_sems.at[4],
                    z_at(-sign * step),
                )
            )

    for b in range(blocks):
        user_block(b)
        for j in range(b * per_block, (b + 1) * per_block):
            for copy in leaving.get(order[j], ()):
                remote(*copy).start()

    def hub_sum(index):
        sign = signs[index]
        wait_bytes(hub_in.at[index], w_sems.at[1 + index])
        span = part_at(-sign * hub)
        total = part[span, :]
        for slot in range(len(covers)):
            total = total + hub_in[index, slot * strip : (slot + 1) * strip, :]
        part[span, :] = total
        half = pl.ds(span.start + index * (strip // 2), strip // 2)
        part[half, :] += hub_in[index, hub_half, :]
        remote(
            part.at[span, :],
            near_in.at[2 * direct + index],
            w_sems.at[3],
            w_sems.at[4],
            z_at(-sign * hub),
        ).start()

    def own_sum():
        wait_bytes(near_in, w_sems.at[4])
        total = part[part_at(0), :]
        for slot in range(2 * direct + 2):
            total = total + near_in[slot]
        span = strip_at(0)
        ug_ref[span, :] = total
        here = ug_ref.at[span, :]
        for index, sign in enumerate(signs):
            remote(here, here, w_sems.at[5], g_sems.at[index], z_at(sign * hub)).start()
        for step in range(1, direct + 1):
            for sign in signs:
                remote(here, here, w_sems.at[5], w_sems.at[6], z_at(sign * step)).start()

    def hub_spread(index):
        sign = signs[index]
        start = (ring - sign * hub + rings) % rings * strip
        here = ug_ref.at[pl.ds(pl.multiple_of(start, strip), strip), :]
        wait_bytes(here, g_sems.at[index])
        half_start = pl.multiple_of(start + index * (strip // 2), strip // 2)
        half = ug_ref.at[pl.ds(half_start, strip // 2), :]
        remote(half, half, w_sems.at[5], w_sems.at[6], z_at(sign * far)).start()
        for c in sorted(covers, key=lambda c: -abs(c)):
            remote(here, here, w_sems.at[5], w_sems.at[6], z_at(sign * c)).start()

    def gather_end():
        wait_bytes(ug_ref.at[pl.ds(0, (rings - 3) * strip), :], w_sems.at[6])

    def item_part(which):
        items[which, :half_cols, :] = 2.0 * lax.dot_general(
            coupling[which],
            users[...],
            (((0,), (0,)), ((), ())),
            preferred_element_type=F32,
        )

    core_rows = half_cols // CORE_PARTS

    def core_send():
        item_part(other)
        items[other, half_cols:, :LANES] = loss_rows
        items[other, half_cols:, LANES:] = jnp.zeros((8, width - LANES), F32)
        for k in range(CORE_PARTS):
            extra = 8 if k == CORE_PARTS - 1 else 0
            span = pl.ds(k * core_rows, core_rows + extra)
            remote(
                items.at[other, span, :],
                core_in.at[span, :],
                x_sems.at[0],
                x_sems.at[1],
                (twin, ring),
            ).start()

    def plane_send():
        wait_bytes(core_in, x_sems.at[1])
        pair_loss = core_in[half_cols:, :LANES] + loss_rows

        def pack(k, carry):
            span = pl.ds(pl.multiple_of(k * piece, piece), piece)
            plane_out[k, :piece, :] = items[core, span, :] + core_in[span, :]
            plane_out[k, piece:, :LANES] = pair_loss
            plane_out[k, piece:, LANES:] = jnp.zeros((8, width - LANES), F32)
            return carry

        lax.fori_loop(0, chips, pack, 0)
        for step in chip_steps:
            remote(
                plane_out.at[(chip + step) % chips],
                plane_in.at[chip],
                x_sems.at[2],
                x_sems.at[3],
                chip_peer(step),
            ).start()
        plane_in[chip] = plane_out[chip]

    def piece_at(half_index, index):
        start = half_index * half_cols + index % chips * piece
        return pl.ds(pl.multiple_of(start, piece), piece)

    def plane_sum():
        wait_bytes(plane_in.at[pl.ds(0, chips - 1)], x_sems.at[3])
        total = plane_in[0]
        for k in range(1, chips):
            total = total + plane_in[k]
        here = ig_ref.at[piece_at(core, chip), :]
        here[...] = total[:piece, :]
        for step in chip_steps:
            remote(
                here, here, x_sems.at[4], back_sems.at[step - 1], chip_peer(step)
            ).start()
        remote(here, here, x_sems.at[5], x_sems.at[6], (twin, ring)).start()
        z_loss[ring] = jnp.broadcast_to(
            item_loss - total[piece + 1 : piece + 2, :LANES], (8, LANES)
        )
        for step in z_steps:
            remote(
                z_loss.at[ring], z_loss.at[ring], l_sems.at[0], l_sems.at[1], z_peer(step)
            ).start()
        return total[piece : piece + 1, :LANES]

    def forward(step):
        here = ig_ref.at[piece_at(core, chip + chips - step), :]
        wait_bytes(here, back_sems.at[step - 1])
        remote(here, here, x_sems.at[5], x_sems.at[6], (twin, ring)).start()

    others = pl.ds(0, (chips - 1) * piece)

    def loss_end(users):
        wait_bytes(z_loss.at[pl.ds(0, rings - 1)], l_sems.at[1])
        total = users
        for k in range(rings):
            total = total + z_loss[k, 0:1, :]
        loss_ref[0, 0] = jnp.sum(total) * (1.0 / total_users)

    core_send()
    item_part(core)
    plane_send()
    hub_sum(0)
    hub_sum(1)
    own_sum()
    users_total = plane_sum()
    hub_spread(0)
    hub_spread(1)
    for step in chip_steps:
        forward(step)
    loss_end(users_total)
    def half_out(which):
        span = pl.ds(pl.multiple_of(which * half_cols, half_cols), half_cols)
        return pltpu.make_async_copy(ig_ref.at[span, :], ig_hbm.at[span, :], out_sems.at[which])

    half_out(core).start()
    gather_end()
    user_out = pltpu.make_async_copy(ug_ref, ug_hbm, out_sems.at[2])
    user_out.start()
    wait_bytes(ig_ref.at[pl.ds(0, half_cols), :], x_sems.at[6])
    half_out(other).start()

    wait_bytes(z_stats.at[pl.ds(0, rings - 1)], z_sems.at[0])
    wait_bytes(p_stats.at[pl.ds(0, 2 * chips - 1)], p_sems.at[0])
    wait_bytes(z_loss.at[pl.ds(0, rings - 1)], l_sems.at[0])
    wait_bytes(hub_in, w_sems.at[0])
    wait_bytes(near_in, w_sems.at[3])
    wait_bytes(ug_ref.at[pl.ds(0, (rings - 1) * strip), :], w_sems.at[5])
    wait_bytes(core_in, x_sems.at[0])
    wait_bytes(plane_in.at[pl.ds(0, chips - 1)], x_sems.at[2])
    wait_bytes(ig_ref.at[others, :], x_sems.at[4])
    wait_bytes(ig_ref.at[pl.ds(0, half_cols), :], x_sems.at[5])
    half_out(core).wait()
    user_out.wait()
    half_out(other).wait()


def copy_out(ug_in, ig_in, ug_out, ig_out, ug_here, ig_here, sems):
    loads = []
    stores = []
    for source, here, target, count in (
        (ug_in, ug_here, ug_out, 2),
        (ig_in, ig_here, ig_out, 4),
    ):
        rows = source.shape[0] // count
        for k in range(count):
            span = pl.ds(k * rows, rows)
            slot = len(loads)
            loads.append(
                pltpu.make_async_copy(source.at[span, :], here.at[span, :], sems.at[0, slot])
            )
            stores.append(
                pltpu.make_async_copy(here.at[span, :], target.at[span, :], sems.at[1, slot])
            )
    for load in loads:
        load.start()
    for load, store in zip(loads, stores):
        load.wait()
        store.start()
    for store in stores:
        store.wait()


def per_device(total_users, chips, rings, user_embed, item_embed, positive, user_count, item_count):
    rows, width = user_embed.shape
    cols = item_embed.shape[0]
    tiles = cols // LANES
    strip = rows // rings
    direct = rings // 8
    hub_rows = (2 * direct if rings > 8 else 1) * strip + strip // 2
    piece = cols // 2 // chips
    vmem = pl.BlockSpec(memory_space=pltpu.VMEM)
    hbm = pl.BlockSpec(memory_space=pltpu.HBM)
    dma = pltpu.SemaphoreType.DMA
    user_grad, item_grad, loss = pl.pallas_call(
        functools.partial(kernel, total_users, chips, rings),
        out_shape=(
            jax.ShapeDtypeStruct((rows, width), F32),
            jax.ShapeDtypeStruct((cols, width), F32),
            jax.ShapeDtypeStruct((1, 1), F32),
        ),
        in_specs=[hbm] * 2 + [vmem] * 3,
        out_specs=(hbm, hbm, pl.BlockSpec(memory_space=pltpu.SMEM)),
        scratch_shapes=[
            pltpu.VMEM((rows, width), F32),
            pltpu.VMEM((cols, width), F32),
            pltpu.VMEM((rows, width), user_embed.dtype),
            pltpu.VMEM((cols, width), item_embed.dtype),
            pltpu.VMEM((rows, width), user_embed.dtype),
            pltpu.VMEM((rows, cols), F32),
            pltpu.VMEM((rows, cols), F32),
            pltpu.VMEM((rows, cols), F32),
            pltpu.VMEM((2, rows, cols // 2), jnp.bfloat16),
            pltpu.VMEM((rows, width), F32),
            pltpu.VMEM((2, cols // 2 + 8, width), F32),
            pltpu.VMEM((tiles, LANES), F32),
            pltpu.VMEM((rows, LANES), F32),
            pltpu.VMEM((rows, LANES), F32),
            pltpu.VMEM((rows, LANES), F32),
            pltpu.VMEM((rows, LANES), F32),
            pltpu.VMEM((tiles, 8, LANES), F32),
            pltpu.VMEM((tiles, 8, LANES), F32),
            pltpu.VMEM((tiles, 8, LANES), F32),
            pltpu.VMEM((rings, rows // LANES, LANES), F32),
            pltpu.VMEM((2 * chips, 2 * tiles, LANES), F32),
            pltpu.VMEM((rings, 8, LANES), F32),
            pltpu.VMEM((2, hub_rows, width), F32),
            pltpu.VMEM((2 * direct + 2, strip, width), F32),
            pltpu.VMEM((cols // 2 + 8, width), F32),
            pltpu.VMEM((chips, piece + 8, width), F32),
            pltpu.VMEM((chips, piece + 8, width), F32),
            dma((2,)),
            dma((2,)),
            dma((2,)),
            dma((7,)),
            dma((2,)),
            dma((8,)),
            dma((chips - 1,)),
            dma((2,)),
            dma((3,)),
        ],
        compiler_params=pltpu.CompilerParams(
            collective_id=0, has_side_effects=True, vmem_limit_bytes=60 * 1024 * 1024
        ),
        name="two_sided",
    )(
        user_embed,
        item_embed,
        positive.reshape(rows // LANES, LANES),
        user_count.reshape(rows // LANES, LANES),
        item_count.reshape(tiles, LANES),
    )
    user_grad, item_grad = pl.pallas_call(
        copy_out,
        out_shape=(
            jax.ShapeDtypeStruct((rows, width), F32),
            jax.ShapeDtypeStruct((cols, width), F32),
        ),
        in_specs=[hbm] * 2,
        out_specs=(hbm, hbm),
        scratch_shapes=[
            pltpu.VMEM((rows, width), F32),
            pltpu.VMEM((cols, width), F32),
            dma((2, 6)),
        ],
        compiler_params=pltpu.CompilerParams(vmem_limit_bytes=60 * 1024 * 1024),
        name="copy_out",
    )(user_grad, item_grad)
    return user_grad, item_grad, loss.reshape(())


def solution(mesh):
    row_size, rings = mesh.shape["row"], mesh.shape["col"]

    def whole(user_embed, *others):
        body = functools.partial(per_device, user_embed.shape[0], row_size // 2, rings)
        return jax.shard_map(
            body,
            mesh=mesh,
            in_specs=(P("row", None), P("col", None), P("row"), P("row"), P("col")),
            out_specs=(P("row", None), P("col", None), P()),
            check_vma=False,
        )(user_embed, *others)

    return whole
```

```python
import functools

import jax
import jax.numpy as jnp
from jax import lax
from jax.experimental import pallas as pl
from jax.experimental.pallas import tpu as pltpu
from jax.sharding import PartitionSpec as P

MESH = pl.DeviceIdType.MESH
LANES = 128
BLOCK = 128
CORE_PARTS = 4
PARTS = 2
F32 = jnp.float32


def columns_of(row):
    return jnp.transpose(jnp.broadcast_to(row, (LANES, LANES)))


def fold(block):
    return block.reshape(block.shape[0] // 8, 8, LANES)


def merged_lse(parts):
    top = jnp.max(parts, axis=0)
    return top + jnp.log(jnp.sum(jnp.exp(parts - top[None]), axis=0))


def kernel(
    total_users,
    chips,
    rings,
    user_hbm,
    item_hbm,
    pos_ref,
    ucnt_ref,
    icnt_ref,
    ug_hbm,
    ig_hbm,
    loss_ref,
    ug_ref,
    ig_ref,
    user_ref,
    item_ref,
    users,
    scores,
    row_exp,
    col_exp,
    coupling,
    part,
    items,
    log_item,
    lu_col,
    pos_col,
    row_col,
    col_max,
    col_sum,
    hits_acc,
    z_stats,
    p_stats,
    z_loss,
    z_match,
    hub_in,
    near_in,
    core_in,
    plane_out,
    plane_in,
    z_sems,
    p_sems,
    l_sems,
    w_sems,
    h_sems,
    n_sems,
    g_sems,
    x_sems,
    back_sems,
    in_sems,
    out_sems,
):
    rows_here, width = user_ref.shape
    cols_here = item_ref.shape[0]
    tiles = cols_here // LANES
    row_tiles = rows_here // LANES
    half_cols = cols_here // 2
    half_tiles = tiles // 2
    blocks = rows_here // BLOCK
    piece = half_cols // chips

    user_in = pltpu.make_async_copy(user_hbm, user_ref, in_sems.at[0])
    item_in = pltpu.make_async_copy(item_hbm, item_ref, in_sems.at[1])
    item_in.start()
    user_in.start()

    mine = lax.axis_index("row")
    ring = lax.axis_index("col")
    chip = mine // 2
    core = mine % 2
    other = 1 - core
    twin = chip * 2 + other

    def z_peer(step):
        return (mine, (ring + step) % rings)

    def chip_peer(step):
        return (((chip + step) % chips) * 2 + core, ring)

    def row_peer(step):
        return ((mine + step) % (2 * chips), ring)

    z_steps = sorted(range(1, rings), key=lambda k: -min(k, rings - k))
    chip_steps = list(range(1, chips))
    row_steps = list(range(1, 2 * chips))

    barrier = pltpu.get_barrier_semaphore()
    for step in z_steps:
        pl.semaphore_signal(barrier, inc=1, device_id=z_peer(step), device_id_type=MESH)
    for step in row_steps:
        pl.semaphore_signal(barrier, inc=1, device_id=row_peer(step), device_id_type=MESH)

    def remote(src, dst, send_sem, recv_sem, device):
        return pltpu.make_async_remote_copy(
            src_ref=src,
            dst_ref=dst,
            send_sem=send_sem,
            recv_sem=recv_sem,
            device_id=device,
            device_id_type=MESH,
        )

    def wait_bytes(ref, sem):
        pltpu.make_async_copy(ref, ref, sem).wait()

    log_item[...] = jnp.log(icnt_ref[...].astype(F32))
    log_user = jnp.log(ucnt_ref[...].astype(F32))
    local_pos = pos_ref[...].astype(F32) - (ring * cols_here).astype(F32)
    for k in range(row_tiles):
        span = pl.ds(k * LANES, LANES)
        lu_col[span, :] = columns_of(log_user[k : k + 1, :])
        pos_col[span, :] = columns_of(local_pos[k : k + 1, :])
    col_max[...] = jnp.full(col_max.shape, -jnp.inf, F32)
    col_sum[...] = jnp.zeros(col_sum.shape, F32)
    hits_acc[...] = jnp.zeros(hits_acc.shape, F32)
    lane = lax.broadcasted_iota(jnp.int32, (BLOCK, LANES), 1).astype(F32)

    def sweep_one(b, z_part):
        span = pl.ds(pl.multiple_of(b * BLOCK, BLOCK), BLOCK)
        scores[span, :] = 2.0 * lax.dot_general(
            user_ref[span, :],
            item_ref[...],
            (((1,), (1,)), ((), ())),
            preferred_element_type=F32,
        )
        lu = lu_col[span, :]
        pos = pos_col[span, :]
        top = None
        for t in range(tiles):
            s = scores[span, t * LANES : (t + 1) * LANES]
            shifted = s - log_item[t : t + 1, :]
            top = shifted if top is None else jnp.maximum(top, shifted)
            col_max[t] = jnp.maximum(col_max[t], jnp.max(fold(s - lu), axis=0))
            match = pos == lane + float(t * LANES)
            hits_acc[t] += jnp.sum(fold(jnp.where(match, 1.0, 0.0)), axis=0)
            z_part = z_part + jnp.sum(fold(jnp.where(match, s + shifted, 0.0)), axis=0)
        row_col[span, :] = jnp.broadcast_to(jnp.max(top, axis=1, keepdims=True), (BLOCK, LANES))
        return z_part

    item_in.wait()
    user_in.wait()
    z_part = lax.fori_loop(0, blocks, sweep_one, jnp.zeros((8, LANES), F32))
    for t in range(tiles):
        col_max[t] = jnp.broadcast_to(jnp.max(col_max[t], axis=0, keepdims=True), (8, LANES))

    def sweep_two(b, carry):
        span = pl.ds(pl.multiple_of(b * BLOCK, BLOCK), BLOCK)
        lu = lu_col[span, :]
        row_max = row_col[span, :]
        total = jnp.zeros((BLOCK, LANES), F32)
        for t in range(tiles):
            s = scores[span, t * LANES : (t + 1) * LANES]
            row = jnp.exp(s - log_item[t : t + 1, :] - row_max)
            row_exp[span, t * LANES : (t + 1) * LANES] = row
            total = total + row
            col = jnp.exp(s - lu - col_max[t, 0:1, :])
            col_exp[span, t * LANES : (t + 1) * LANES] = col
            col_sum[t] += jnp.sum(fold(col), axis=0)
        lse = row_max + jnp.log(jnp.sum(total, axis=1, keepdims=True))
        z_stats[ring, pl.ds(b, 1), :] = jnp.transpose(lse)[0:1, :]
        return carry

    lax.fori_loop(0, blocks, sweep_two, 0)
    col_lse_rows = []
    hits_rows = []
    for t in range(tiles):
        total = jnp.sum(col_sum[t], axis=0, keepdims=True)
        col_lse_rows.append(col_max[t, 0:1, :] + jnp.log(total))
        hits_rows.append(jnp.sum(hits_acc[t], axis=0, keepdims=True))
    p_stats[mine] = jnp.concatenate(col_lse_rows + hits_rows, axis=0)

    pl.semaphore_wait(barrier, rings - 1 + 2 * chips - 1)
    for step in z_steps:
        remote(
            z_stats.at[ring], z_stats.at[ring], z_sems.at[0], z_sems.at[1], z_peer(step)
        ).start()
    for step in row_steps:
        remote(
            p_stats.at[mine], p_stats.at[mine], p_sems.at[0], p_sems.at[1], row_peer(step)
        ).start()
    z_match[ring] = jnp.broadcast_to(jnp.sum(z_part, axis=0, keepdims=True), (8, LANES))
    for step in z_steps:
        remote(
            z_match.at[ring], z_match.at[ring], l_sems.at[2], l_sems.at[3], z_peer(step)
        ).start()
    wait_bytes(z_stats.at[pl.ds(0, rings - 1)], z_sems.at[1])
    row_lse = merged_lse(z_stats[...])
    for k in range(row_tiles):
        span = pl.ds(k * LANES, LANES)
        row_col[span, :] = jnp.exp(row_col[span, :] - columns_of(row_lse[k : k + 1, :]))
    user_loss = jnp.sum(row_lse + log_user, axis=0, keepdims=True)
    wait_bytes(p_stats.at[pl.ds(0, 2 * chips - 1)], p_sems.at[1])
    item_stats = p_stats[...]
    col_lse = merged_lse(item_stats[:, :tiles])
    pos_hits = jnp.sum(item_stats[:, tiles:], axis=0)
    item_loss = jnp.sum(pos_hits * col_lse, axis=0, keepdims=True)
    col_top = jnp.concatenate([col_max[t, 0:1, :] for t in range(tiles)], axis=0)
    col_scale = pos_hits * jnp.exp(col_top - col_lse)

    strip = rows_here // rings
    sub = strip // PARTS
    per_block = BLOCK // sub
    direct = rings // 8
    hub = 2 * direct + 1
    covers = [c for c in range(-direct, direct + 1) if c != 0 and hub + c < rings // 2]
    far = rings // 2 - hub
    order = [(direct + 1 + j) % rings for j in range(rings)]
    signs = (1, -1)

    def sub_at(offset, h, start=0, size=None):
        size = sub if size is None else size
        first = (ring + offset + rings) % rings * strip + h * sub + start
        return pl.ds(pl.multiple_of(first, 8 if size < 16 else size), size)

    def part_at(offset, h):
        return pl.ds(h * (rows_here // PARTS) + order.index(offset % rings) * sub, sub)

    def z_at(offset):
        return z_peer(offset % rings)

    sub_lane = lane[:sub, :]

    def user_block(b):
        for k in range(b * per_block, (b + 1) * per_block):
            h, j = k // rings, k % rings
            source = sub_at(order[j], h)
            target = pl.ds(k * sub, sub)
            users[target, :] = user_ref[source, :]
            pos = pos_col[source, :]
            row = row_col[source, :]
            for t in range(tiles):
                here = slice(t * LANES, (t + 1) * LANES)
                value = row_exp[source, here] * row + col_exp[source, here] * col_scale[t : t + 1, :]
                match = pos == sub_lane + float(t * LANES)
                value = value - jnp.where(match, 2.0, 0.0)
                at = (t % half_tiles) * LANES
                coupling[t // half_tiles, target, at : at + LANES] = value.astype(jnp.bfloat16)
        span = pl.ds(b * BLOCK, BLOCK)
        part[span, :] = 2.0 * (
            jnp.dot(coupling[0, span, :], item_ref[:half_cols, :], preferred_element_type=F32)
            + jnp.dot(coupling[1, span, :], item_ref[half_cols:, :], preferred_element_type=F32)
        )

    leaving = {}
    hub_half = pl.ds(len(covers) * sub, sub // 2)
    for h in range(PARTS):
        for index, sign in enumerate(signs):
            for slot, c in enumerate(covers):
                leaving.setdefault((h, -sign * (hub + c) % rings), []).append(
                    (
                        part.at[part_at(-sign * (hub + c), h), :],
                        hub_in.at[h, index, pl.ds(slot * sub, sub), :],
                        w_sems.at[0],
                        h_sems.at[h, index],
                        z_at(-sign * c),
                    )
                )
            first = part_at(rings // 2, h).start + index * (sub // 2)
            leaving.setdefault((h, rings // 2), []).append(
                (
                    part.at[pl.ds(first, sub // 2), :],
                    hub_in.at[h, index, hub_half, :],
                    w_sems.at[0],
                    h_sems.at[h, index],
                    z_at(-sign * far),
                )
            )
            for step in range(1, direct + 1):
                leaving.setdefault((h, -sign * step % rings), []).append(
                    (
                        part.at[part_at(-sign * step, h), :],
                        near_in.at[h, index * direct + step - 1],
                        w_sems.at[1],
                        n_sems.at[h],
                        z_at(-sign * step),
                    )
                )

    for b in range(blocks):
        user_block(b)
        for k in range(b * per_block, (b + 1) * per_block):
            for copy in leaving.get((k // rings, order[k % rings]), ()):
                remote(*copy).start()

    def hub_sum(h):
        for index, sign in enumerate(signs):
            wait_bytes(hub_in.at[h, index], h_sems.at[h, index])
            span = part_at(-sign * hub, h)
            total = part[span, :]
            for slot in range(len(covers)):
                total = total + hub_in[h, index, slot * sub : (slot + 1) * sub, :]
            part[span, :] = total
            half = pl.ds(span.start + index * (sub // 2), sub // 2)
            part[half, :] += hub_in[h, index, hub_half, :]
            remote(
                part.at[span, :],
                near_in.at[h, 2 * direct + index],
                w_sems.at[1],
                n_sems.at[h],
                z_at(-sign * hub),
            ).start()

    def own_sum(h):
        wait_bytes(near_in.at[h], n_sems.at[h])
        total = part[part_at(0, h), :]
        for slot in range(2 * direct + 2):
            total = total + near_in[h, slot]
        span = sub_at(0, h)
        ug_ref[span, :] = total
        here = ug_ref.at[span, :]
        for index, sign in enumerate(signs):
            remote(here, here, w_sems.at[2], g_sems.at[h, index], z_at(sign * hub)).start()
        for step in range(1, direct + 1):
            for sign in signs:
                remote(here, here, w_sems.at[2], w_sems.at[3], z_at(sign * step)).start()

    def hub_spread(h):
        for index, sign in enumerate(signs):
            here = ug_ref.at[sub_at(-sign * hub, h), :]
            wait_bytes(here, g_sems.at[h, index])
            half = ug_ref.at[sub_at(-sign * hub, h, index * (sub // 2), sub // 2), :]
            remote(half, half, w_sems.at[2], w_sems.at[3], z_at(sign * far)).start()
            for c in sorted(covers, key=lambda c: -abs(c)):
                remote(here, here, w_sems.at[2], w_sems.at[3], z_at(sign * c)).start()

    def gather_end():
        wait_bytes(ug_ref.at[pl.ds(0, (rings - 3) * strip), :], w_sems.at[3])

    def item_part(which):
        items[which, :half_cols, :] = 2.0 * lax.dot_general(
            coupling[which],
            users[...],
            (((0,), (0,)), ((), ())),
            preferred_element_type=F32,
        )

    core_rows = half_cols // CORE_PARTS

    def loss_send():
        z_loss[ring] = jnp.broadcast_to(item_loss, (8, LANES))
        for step in z_steps:
            remote(
                z_loss.at[ring], z_loss.at[ring], l_sems.at[0], l_sems.at[1], z_peer(step)
            ).start()

    def loss_rows():
        total = z_match[0]
        for k in range(1, rings):
            total = total + z_match[k]
        return user_loss - total

    def core_send():
        item_part(other)
        wait_bytes(z_match.at[pl.ds(0, rings - 1)], l_sems.at[3])
        items[other, half_cols:, :LANES] = loss_rows()
        items[other, half_cols:, LANES:] = jnp.zeros((8, width - LANES), F32)
        for k in range(CORE_PARTS):
            extra = 8 if k == CORE_PARTS - 1 else 0
            span = pl.ds(k * core_rows, core_rows + extra)
            remote(
                items.at[other, span, :],
                core_in.at[span, :],
                x_sems.at[0],
                x_sems.at[1],
                (twin, ring),
            ).start()

    def plane_send():
        wait_bytes(core_in, x_sems.at[1])
        pair_loss = core_in[half_cols:, :LANES] + loss_rows()

        def pack(k, carry):
            span = pl.ds(pl.multiple_of(k * piece, piece), piece)
            plane_out[k, :piece, :] = items[core, span, :] + core_in[span, :]
            plane_out[k, piece:, :LANES] = pair_loss
            plane_out[k, piece:, LANES:] = jnp.zeros((8, width - LANES), F32)
            return carry

        lax.fori_loop(0, chips, pack, 0)
        for step in chip_steps:
            remote(
                plane_out.at[(chip + step) % chips],
                plane_in.at[chip],
                x_sems.at[2],
                x_sems.at[3],
                chip_peer(step),
            ).start()
        plane_in[chip] = plane_out[chip]

    def piece_at(half_index, index):
        start = half_index * half_cols + index % chips * piece
        return pl.ds(pl.multiple_of(start, piece), piece)

    def plane_sum():
        wait_bytes(plane_in.at[pl.ds(0, chips - 1)], x_sems.at[3])
        total = plane_in[0]
        for k in range(1, chips):
            total = total + plane_in[k]
        here = ig_ref.at[piece_at(core, chip), :]
        here[...] = total[:piece, :]
        for step in chip_steps:
            remote(
                here, here, x_sems.at[4], back_sems.at[step - 1], chip_peer(step)
            ).start()
        remote(here, here, x_sems.at[5], x_sems.at[6], (twin, ring)).start()
        return total[piece : piece + 8, :LANES]

    def forward(step):
        here = ig_ref.at[piece_at(core, chip + chips - step), :]
        wait_bytes(here, back_sems.at[step - 1])
        remote(here, here, x_sems.at[5], x_sems.at[6], (twin, ring)).start()

    others = pl.ds(0, (chips - 1) * piece)

    def loss_end(users):
        wait_bytes(z_loss.at[pl.ds(0, rings - 1)], l_sems.at[1])
        total = users
        for k in range(rings):
            total = total + z_loss[k, 0:1, :]
        loss_ref[0, 0] = jnp.sum(total) * (1.0 / total_users)

    core_send()
    item_part(core)
    loss_send()
    hub_sum(0)
    plane_send()
    hub_sum(1)
    own_sum(0)
    own_sum(1)
    plane_total = plane_sum()
    hub_spread(0)
    hub_spread(1)
    for step in chip_steps:
        forward(step)
    loss_end(plane_total[0:1, :])

    def half_out(which):
        span = pl.ds(pl.multiple_of(which * half_cols, half_cols), half_cols)
        return pltpu.make_async_copy(ig_ref.at[span, :], ig_hbm.at[span, :], out_sems.at[which])

    half_out(core).start()
    gather_end()
    user_out = pltpu.make_async_copy(ug_ref, ug_hbm, out_sems.at[2])
    user_out.start()
    wait_bytes(ig_ref.at[pl.ds(0, half_cols), :], x_sems.at[6])
    half_out(other).start()

    wait_bytes(z_stats.at[pl.ds(0, rings - 1)], z_sems.at[0])
    wait_bytes(p_stats.at[pl.ds(0, 2 * chips - 1)], p_sems.at[0])
    wait_bytes(z_loss.at[pl.ds(0, rings - 1)], l_sems.at[0])
    wait_bytes(hub_in, w_sems.at[0])
    wait_bytes(near_in, w_sems.at[1])
    wait_bytes(ug_ref.at[pl.ds(0, (rings - 1) * strip), :], w_sems.at[2])
    wait_bytes(z_match.at[pl.ds(0, rings - 1)], l_sems.at[2])
    wait_bytes(core_in, x_sems.at[0])
    wait_bytes(plane_in.at[pl.ds(0, chips - 1)], x_sems.at[2])
    wait_bytes(ig_ref.at[others, :], x_sems.at[4])
    wait_bytes(ig_ref.at[pl.ds(0, half_cols), :], x_sems.at[5])
    half_out(core).wait()
    user_out.wait()
    half_out(other).wait()


def copy_out(ug_in, ig_in, ug_out, ig_out, ug_here, ig_here, sems):
    loads = []
    stores = []
    for source, here, target, count in (
        (ug_in, ug_here, ug_out, 2),
        (ig_in, ig_here, ig_out, 4),
    ):
        rows = source.shape[0] // count
        for k in range(count):
            span = pl.ds(k * rows, rows)
            slot = len(loads)
            loads.append(
                pltpu.make_async_copy(source.at[span, :], here.at[span, :], sems.at[0, slot])
            )
            stores.append(
                pltpu.make_async_copy(here.at[span, :], target.at[span, :], sems.at[1, slot])
            )
    for load in loads:
        load.start()
    for load, store in zip(loads, stores):
        load.wait()
        store.start()
    for store in stores:
        store.wait()


def per_device(total_users, chips, rings, user_embed, item_embed, positive, user_count, item_count):
    rows, width = user_embed.shape
    cols = item_embed.shape[0]
    tiles = cols // LANES
    strip = rows // rings
    direct = rings // 8
    sub = strip // PARTS
    hub_rows = (2 * direct if rings > 8 else 1) * sub + sub // 2
    piece = cols // 2 // chips
    vmem = pl.BlockSpec(memory_space=pltpu.VMEM)
    hbm = pl.BlockSpec(memory_space=pltpu.HBM)
    dma = pltpu.SemaphoreType.DMA
    user_grad, item_grad, loss = pl.pallas_call(
        functools.partial(kernel, total_users, chips, rings),
        out_shape=(
            jax.ShapeDtypeStruct((rows, width), F32),
            jax.ShapeDtypeStruct((cols, width), F32),
            jax.ShapeDtypeStruct((1, 1), F32),
        ),
        in_specs=[hbm] * 2 + [vmem] * 3,
        out_specs=(hbm, hbm, pl.BlockSpec(memory_space=pltpu.SMEM)),
        scratch_shapes=[
            pltpu.VMEM((rows, width), F32),
            pltpu.VMEM((cols, width), F32),
            pltpu.VMEM((rows, width), user_embed.dtype),
            pltpu.VMEM((cols, width), item_embed.dtype),
            pltpu.VMEM((rows, width), user_embed.dtype),
            pltpu.VMEM((rows, cols), F32),
            pltpu.VMEM((rows, cols), F32),
            pltpu.VMEM((rows, cols), F32),
            pltpu.VMEM((2, rows, cols // 2), jnp.bfloat16),
            pltpu.VMEM((rows, width), F32),
            pltpu.VMEM((2, cols // 2 + 8, width), F32),
            pltpu.VMEM((tiles, LANES), F32),
            pltpu.VMEM((rows, LANES), F32),
            pltpu.VMEM((rows, LANES), F32),
            pltpu.VMEM((rows, LANES), F32),
            pltpu.VMEM((tiles, 8, LANES), F32),
            pltpu.VMEM((tiles, 8, LANES), F32),
            pltpu.VMEM((tiles, 8, LANES), F32),
            pltpu.VMEM((rings, rows // LANES, LANES), F32),
            pltpu.VMEM((2 * chips, 2 * tiles, LANES), F32),
            pltpu.VMEM((rings, 8, LANES), F32),
            pltpu.VMEM((rings, 8, LANES), F32),
            pltpu.VMEM((PARTS, 2, hub_rows, width), F32),
            pltpu.VMEM((PARTS, 2 * direct + 2, sub, width), F32),
            pltpu.VMEM((cols // 2 + 8, width), F32),
            pltpu.VMEM((chips, piece + 8, width), F32),
            pltpu.VMEM((chips, piece + 8, width), F32),
            dma((2,)),
            dma((2,)),
            dma((4,)),
            dma((4,)),
            dma((PARTS, 2)),
            dma((PARTS,)),
            dma((PARTS, 2)),
            dma((8,)),
            dma((chips - 1,)),
            dma((2,)),
            dma((3,)),
        ],
        compiler_params=pltpu.CompilerParams(
            collective_id=0, has_side_effects=True, vmem_limit_bytes=60 * 1024 * 1024
        ),
        name="two_sided",
    )(
        user_embed,
        item_embed,
        positive.reshape(rows // LANES, LANES),
        user_count.reshape(rows // LANES, LANES),
        item_count.reshape(tiles, LANES),
    )
    user_grad, item_grad = pl.pallas_call(
        copy_out,
        out_shape=(
            jax.ShapeDtypeStruct((rows, width), F32),
            jax.ShapeDtypeStruct((cols, width), F32),
        ),
        in_specs=[hbm] * 2,
        out_specs=(hbm, hbm),
        scratch_shapes=[
            pltpu.VMEM((rows, width), F32),
            pltpu.VMEM((cols, width), F32),
            dma((2, 6)),
        ],
        compiler_params=pltpu.CompilerParams(vmem_limit_bytes=60 * 1024 * 1024),
        name="copy_out",
    )(user_grad, item_grad)
    return user_grad, item_grad, loss.reshape(())


def solution(mesh):
    row_size, rings = mesh.shape["row"], mesh.shape["col"]

    def whole(user_embed, *others):
        body = functools.partial(per_device, user_embed.shape[0], row_size // 2, rings)
        return jax.shard_map(
            body,
            mesh=mesh,
            in_specs=(P("row", None), P("col", None), P("row"), P("row"), P("col")),
            out_specs=(P("row", None), P("col", None), P()),
            check_vma=False,
        )(user_embed, *others)

    return whole
```

```python
import functools

import jax
import jax.numpy as jnp
from jax import lax
from jax.experimental import pallas as pl
from jax.experimental.pallas import tpu as pltpu
from jax.sharding import PartitionSpec as P

MESH = pl.DeviceIdType.MESH
LANES = 128
BLOCK = 128
CORE_PARTS = 4
PARTS = 2
F32 = jnp.float32


def columns_of(row):
    return jnp.transpose(jnp.broadcast_to(row, (LANES, LANES)))


def fold(block):
    return block.reshape(block.shape[0] // 8, 8, LANES)


def merged_lse(parts):
    top = jnp.max(parts, axis=0)
    return top + jnp.log(jnp.sum(jnp.exp(parts - top[None]), axis=0))


def kernel(
    total_users,
    chips,
    rings,
    user_hbm,
    item_hbm,
    pos_ref,
    ucnt_ref,
    icnt_ref,
    ug_hbm,
    ig_hbm,
    loss_ref,
    ug_ref,
    ig_ref,
    user_ref,
    item_ref,
    users,
    scores,
    row_exp,
    col_exp,
    coupling,
    part,
    items,
    log_item,
    lu_col,
    pos_col,
    row_col,
    col_max,
    col_sum,
    hits_acc,
    z_stats,
    p_stats,
    z_loss,
    hub_in,
    near_in,
    core_in,
    plane_out,
    plane_in,
    z_sems,
    p_sems,
    l_sems,
    w_sems,
    h_sems,
    n_sems,
    g_sems,
    x_sems,
    back_sems,
    in_sems,
    out_sems,
):
    rows_here, width = user_ref.shape
    cols_here = item_ref.shape[0]
    tiles = cols_here // LANES
    row_tiles = rows_here // LANES
    half_cols = cols_here // 2
    half_tiles = tiles // 2
    blocks = rows_here // BLOCK
    piece = half_cols // chips

    user_in = pltpu.make_async_copy(user_hbm, user_ref, in_sems.at[0])
    item_in = pltpu.make_async_copy(item_hbm, item_ref, in_sems.at[1])
    item_in.start()
    user_in.start()

    mine = lax.axis_index("row")
    ring = lax.axis_index("col")
    chip = mine // 2
    core = mine % 2
    other = 1 - core
    twin = chip * 2 + other

    def z_peer(step):
        return (mine, (ring + step) % rings)

    def chip_peer(step):
        return (((chip + step) % chips) * 2 + core, ring)

    def row_peer(step):
        return ((mine + step) % (2 * chips), ring)

    z_steps = sorted(range(1, rings), key=lambda k: -min(k, rings - k))
    chip_steps = list(range(1, chips))
    row_steps = list(range(1, 2 * chips))

    barrier = pltpu.get_barrier_semaphore()
    for step in z_steps:
        pl.semaphore_signal(barrier, inc=1, device_id=z_peer(step), device_id_type=MESH)
    for step in row_steps:
        pl.semaphore_signal(barrier, inc=1, device_id=row_peer(step), device_id_type=MESH)

    def remote(src, dst, send_sem, recv_sem, device):
        return pltpu.make_async_remote_copy(
            src_ref=src,
            dst_ref=dst,
            send_sem=send_sem,
            recv_sem=recv_sem,
            device_id=device,
            device_id_type=MESH,
        )

    def wait_bytes(ref, sem):
        pltpu.make_async_copy(ref, ref, sem).wait()

    log_item[...] = jnp.log(icnt_ref[...].astype(F32))
    log_user = jnp.log(ucnt_ref[...].astype(F32))
    local_pos = pos_ref[...].astype(F32) - (ring * cols_here).astype(F32)
    for k in range(row_tiles):
        span = pl.ds(k * LANES, LANES)
        lu_col[span, :] = columns_of(log_user[k : k + 1, :])
        pos_col[span, :] = columns_of(local_pos[k : k + 1, :])
    col_max[...] = jnp.full(col_max.shape, -jnp.inf, F32)
    col_sum[...] = jnp.zeros(col_sum.shape, F32)
    hits_acc[...] = jnp.zeros(hits_acc.shape, F32)
    lane = lax.broadcasted_iota(jnp.int32, (BLOCK, LANES), 1).astype(F32)

    def sweep_one(b, z_part):
        span = pl.ds(pl.multiple_of(b * BLOCK, BLOCK), BLOCK)
        scores[span, :] = 2.0 * lax.dot_general(
            user_ref[span, :],
            item_ref[...],
            (((1,), (1,)), ((), ())),
            preferred_element_type=F32,
        )
        lu = lu_col[span, :]
        pos = pos_col[span, :]
        top = None
        for t in range(tiles):
            s = scores[span, t * LANES : (t + 1) * LANES]
            shifted = s - log_item[t : t + 1, :]
            top = shifted if top is None else jnp.maximum(top, shifted)
            col_max[t] = jnp.maximum(col_max[t], jnp.max(fold(s - lu), axis=0))
            match = pos == lane + float(t * LANES)
            hits_acc[t] += jnp.sum(fold(jnp.where(match, 1.0, 0.0)), axis=0)
            z_part = z_part + jnp.sum(fold(jnp.where(match, s + shifted, 0.0)), axis=0)
        row_col[span, :] = jnp.broadcast_to(jnp.max(top, axis=1, keepdims=True), (BLOCK, LANES))
        return z_part

    item_in.wait()
    user_in.wait()
    z_part = lax.fori_loop(0, blocks, sweep_one, jnp.zeros((8, LANES), F32))
    for t in range(tiles):
        col_max[t] = jnp.broadcast_to(jnp.max(col_max[t], axis=0, keepdims=True), (8, LANES))

    def sweep_two(b, carry):
        span = pl.ds(pl.multiple_of(b * BLOCK, BLOCK), BLOCK)
        lu = lu_col[span, :]
        row_max = row_col[span, :]
        total = jnp.zeros((BLOCK, LANES), F32)
        for t in range(tiles):
            s = scores[span, t * LANES : (t + 1) * LANES]
            row = jnp.exp(s - log_item[t : t + 1, :] - row_max)
            row_exp[span, t * LANES : (t + 1) * LANES] = row
            total = total + row
            col = jnp.exp(s - lu - col_max[t, 0:1, :])
            col_exp[span, t * LANES : (t + 1) * LANES] = col
            col_sum[t] += jnp.sum(fold(col), axis=0)
        lse = row_max + jnp.log(jnp.sum(total, axis=1, keepdims=True))
        z_stats[ring, pl.ds(b, 1), :] = jnp.transpose(lse)[0:1, :]
        return carry

    lax.fori_loop(0, blocks, sweep_two, 0)
    col_lse_rows = []
    hits_rows = []
    for t in range(tiles):
        total = jnp.sum(col_sum[t], axis=0, keepdims=True)
        col_lse_rows.append(col_max[t, 0:1, :] + jnp.log(total))
        hits_rows.append(jnp.sum(hits_acc[t], axis=0, keepdims=True))
    p_stats[mine] = jnp.concatenate(col_lse_rows + hits_rows, axis=0)

    pl.semaphore_wait(barrier, rings - 1 + 2 * chips - 1)
    for step in z_steps:
        remote(
            z_stats.at[ring], z_stats.at[ring], z_sems.at[0], z_sems.at[1], z_peer(step)
        ).start()
    for step in row_steps:
        remote(
            p_stats.at[mine], p_stats.at[mine], p_sems.at[0], p_sems.at[1], row_peer(step)
        ).start()
    wait_bytes(z_stats.at[pl.ds(0, rings - 1)], z_sems.at[1])
    row_lse = merged_lse(z_stats[...])
    for k in range(row_tiles):
        span = pl.ds(k * LANES, LANES)
        row_col[span, :] = jnp.exp(row_col[span, :] - columns_of(row_lse[k : k + 1, :]))
    user_loss = jnp.sum(row_lse + log_user, axis=0, keepdims=True)
    match_loss = jnp.sum(z_part, axis=0, keepdims=True)
    loss_rows = jnp.concatenate([user_loss, match_loss, jnp.zeros((6, LANES), F32)], axis=0)
    wait_bytes(p_stats.at[pl.ds(0, 2 * chips - 1)], p_sems.at[1])
    item_stats = p_stats[...]
    col_lse = merged_lse(item_stats[:, :tiles])
    pos_hits = jnp.sum(item_stats[:, tiles:], axis=0)
    item_loss = jnp.sum(pos_hits * col_lse, axis=0, keepdims=True)
    col_top = jnp.concatenate([col_max[t, 0:1, :] for t in range(tiles)], axis=0)
    col_scale = pos_hits * jnp.exp(col_top - col_lse)

    strip = rows_here // rings
    sub = strip // PARTS
    per_block = BLOCK // sub
    direct = rings // 8
    hub = 2 * direct + 1
    covers = [c for c in range(-direct, direct + 1) if c != 0 and hub + c < rings // 2]
    far = rings // 2 - hub
    order = [(direct + 1 + j) % rings for j in range(rings)]
    signs = (1, -1)

    def sub_at(offset, h, start=0, size=None):
        size = sub if size is None else size
        first = (ring + offset + rings) % rings * strip + h * sub + start
        return pl.ds(pl.multiple_of(first, 8 if size < 16 else size), size)

    def part_at(offset, h):
        return pl.ds(h * (rows_here // PARTS) + order.index(offset % rings) * sub, sub)

    def z_at(offset):
        return z_peer(offset % rings)

    sub_lane = lane[:sub, :]

    def user_block(b):
        for k in range(b * per_block, (b + 1) * per_block):
            h, j = k // rings, k % rings
            source = sub_at(order[j], h)
            target = pl.ds(k * sub, sub)
            users[target, :] = user_ref[source, :]
            pos = pos_col[source, :]
            row = row_col[source, :]
            for t in range(tiles):
                here = slice(t * LANES, (t + 1) * LANES)
                value = row_exp[source, here] * row + col_exp[source, here] * col_scale[t : t + 1, :]
                match = pos == sub_lane + float(t * LANES)
                value = value - jnp.where(match, 2.0, 0.0)
                at = (t % half_tiles) * LANES
                coupling[t // half_tiles, target, at : at + LANES] = value.astype(jnp.bfloat16)
        span = pl.ds(b * BLOCK, BLOCK)
        part[span, :] = 2.0 * (
            jnp.dot(coupling[0, span, :], item_ref[:half_cols, :], preferred_element_type=F32)
            + jnp.dot(coupling[1, span, :], item_ref[half_cols:, :], preferred_element_type=F32)
        )

    leaving = {}
    hub_half = pl.ds(len(covers) * sub, sub // 2)
    for h in range(PARTS):
        for index, sign in enumerate(signs):
            for slot, c in enumerate(covers):
                leaving.setdefault((h, -sign * (hub + c) % rings), []).append(
                    (
                        part.at[part_at(-sign * (hub + c), h), :],
                        hub_in.at[h, index, pl.ds(slot * sub, sub), :],
                        w_sems.at[0],
                        h_sems.at[h, index],
                        z_at(-sign * c),
                    )
                )
            first = part_at(rings // 2, h).start + index * (sub // 2)
            leaving.setdefault((h, rings // 2), []).append(
                (
                    part.at[pl.ds(first, sub // 2), :],
                    hub_in.at[h, index, hub_half, :],
                    w_sems.at[0],
                    h_sems.at[h, index],
                    z_at(-sign * far),
                )
            )
            for step in range(1, direct + 1):
                leaving.setdefault((h, -sign * step % rings), []).append(
                    (
                        part.at[part_at(-sign * step, h), :],
                        near_in.at[h, index * direct + step - 1],
                        w_sems.at[1],
                        n_sems.at[h],
                        z_at(-sign * step),
                    )
                )

    for b in range(blocks):
        user_block(b)
        for k in range(b * per_block, (b + 1) * per_block):
            for copy in leaving.get((k // rings, order[k % rings]), ()):
                remote(*copy).start()

    def hub_sum(h):
        for index, sign in enumerate(signs):
            wait_bytes(hub_in.at[h, index], h_sems.at[h, index])
            span = part_at(-sign * hub, h)
            total = part[span, :]
            for slot in range(len(covers)):
                total = total + hub_in[h, index, slot * sub : (slot + 1) * sub, :]
            part[span, :] = total
            half = pl.ds(span.start + index * (sub // 2), sub // 2)
            part[half, :] += hub_in[h, index, hub_half, :]
            remote(
                part.at[span, :],
                near_in.at[h, 2 * direct + index],
                w_sems.at[1],
                n_sems.at[h],
                z_at(-sign * hub),
            ).start()

    def own_sum(h):
        wait_bytes(near_in.at[h], n_sems.at[h])
        total = part[part_at(0, h), :]
        for slot in range(2 * direct + 2):
            total = total + near_in[h, slot]
        span = sub_at(0, h)
        ug_ref[span, :] = total
        here = ug_ref.at[span, :]
        for index, sign in enumerate(signs):
            remote(here, here, w_sems.at[2], g_sems.at[h, index], z_at(sign * hub)).start()
        for step in range(1, direct + 1):
            for sign in signs:
                remote(here, here, w_sems.at[2], w_sems.at[3], z_at(sign * step)).start()

    def hub_spread(h):
        for index, sign in enumerate(signs):
            here = ug_ref.at[sub_at(-sign * hub, h), :]
            wait_bytes(here, g_sems.at[h, index])
            half = ug_ref.at[sub_at(-sign * hub, h, index * (sub // 2), sub // 2), :]
            remote(half, half, w_sems.at[2], w_sems.at[3], z_at(sign * far)).start()
            for c in sorted(covers, key=lambda c: -abs(c)):
                remote(here, here, w_sems.at[2], w_sems.at[3], z_at(sign * c)).start()

    def gather_end():
        wait_bytes(ug_ref.at[pl.ds(0, (rings - 3) * strip), :], w_sems.at[3])

    def item_part(which):
        items[which, :half_cols, :] = 2.0 * lax.dot_general(
            coupling[which],
            users[...],
            (((0,), (0,)), ((), ())),
            preferred_element_type=F32,
        )

    core_rows = half_cols // CORE_PARTS

    def core_send():
        item_part(other)
        items[other, half_cols:, :LANES] = loss_rows
        items[other, half_cols:, LANES:] = jnp.zeros((8, width - LANES), F32)
        for k in range(CORE_PARTS):
            extra = 8 if k == CORE_PARTS - 1 else 0
            span = pl.ds(k * core_rows, core_rows + extra)
            remote(
                items.at[other, span, :],
                core_in.at[span, :],
                x_sems.at[0],
                x_sems.at[1],
                (twin, ring),
            ).start()

    def plane_send():
        wait_bytes(core_in, x_sems.at[1])
        pair_loss = core_in[half_cols:, :LANES] + loss_rows

        def pack(k, carry):
            span = pl.ds(pl.multiple_of(k * piece, piece), piece)
            plane_out[k, :piece, :] = items[core, span, :] + core_in[span, :]
            plane_out[k, piece:, :LANES] = pair_loss
            plane_out[k, piece:, LANES:] = jnp.zeros((8, width - LANES), F32)
            return carry

        lax.fori_loop(0, chips, pack, 0)
        for step in chip_steps:
            remote(
                plane_out.at[(chip + step) % chips],
                plane_in.at[chip],
                x_sems.at[2],
                x_sems.at[3],
                chip_peer(step),
            ).start()
        plane_in[chip] = plane_out[chip]

    def piece_at(half_index, index):
        start = half_index * half_cols + index % chips * piece
        return pl.ds(pl.multiple_of(start, piece), piece)

    def plane_sum():
        wait_bytes(plane_in.at[pl.ds(0, chips - 1)], x_sems.at[3])
        total = plane_in[0]
        for k in range(1, chips):
            total = total + plane_in[k]
        here = ig_ref.at[piece_at(core, chip), :]
        here[...] = total[:piece, :]
        for step in chip_steps:
            remote(
                here, here, x_sems.at[4], back_sems.at[step - 1], chip_peer(step)
            ).start()
        remote(here, here, x_sems.at[5], x_sems.at[6], (twin, ring)).start()
        z_loss[ring] = jnp.broadcast_to(
            item_loss - total[piece + 1 : piece + 2, :LANES], (8, LANES)
        )
        for step in z_steps:
            remote(
                z_loss.at[ring], z_loss.at[ring], l_sems.at[0], l_sems.at[1], z_peer(step)
            ).start()
        return total[piece : piece + 1, :LANES]

    def forward(step):
        here = ig_ref.at[piece_at(core, chip + chips - step), :]
        wait_bytes(here, back_sems.at[step - 1])
        remote(here, here, x_sems.at[5], x_sems.at[6], (twin, ring)).start()

    others = pl.ds(0, (chips - 1) * piece)

    def loss_end(users):
        wait_bytes(z_loss.at[pl.ds(0, rings - 1)], l_sems.at[1])
        total = users
        for k in range(rings):
            total = total + z_loss[k, 0:1, :]
        loss_ref[0, 0] = jnp.sum(total) * (1.0 / total_users)

    core_send()
    item_part(core)
    hub_sum(0)
    plane_send()
    hub_sum(1)
    own_sum(0)
    own_sum(1)
    plane_total = plane_sum()
    hub_spread(0)
    hub_spread(1)
    for step in chip_steps:
        forward(step)
    loss_end(plane_total)

    def half_out(which):
        span = pl.ds(pl.multiple_of(which * half_cols, half_cols), half_cols)
        return pltpu.make_async_copy(ig_ref.at[span, :], ig_hbm.at[span, :], out_sems.at[which])

    half_out(core).start()
    gather_end()
    user_out = pltpu.make_async_copy(ug_ref, ug_hbm, out_sems.at[2])
    user_out.start()
    wait_bytes(ig_ref.at[pl.ds(0, half_cols), :], x_sems.at[6])
    half_out(other).start()

    wait_bytes(z_stats.at[pl.ds(0, rings - 1)], z_sems.at[0])
    wait_bytes(p_stats.at[pl.ds(0, 2 * chips - 1)], p_sems.at[0])
    wait_bytes(z_loss.at[pl.ds(0, rings - 1)], l_sems.at[0])
    wait_bytes(hub_in, w_sems.at[0])
    wait_bytes(near_in, w_sems.at[1])
    wait_bytes(ug_ref.at[pl.ds(0, (rings - 1) * strip), :], w_sems.at[2])
    wait_bytes(core_in, x_sems.at[0])
    wait_bytes(plane_in.at[pl.ds(0, chips - 1)], x_sems.at[2])
    wait_bytes(ig_ref.at[others, :], x_sems.at[4])
    wait_bytes(ig_ref.at[pl.ds(0, half_cols), :], x_sems.at[5])
    half_out(core).wait()
    user_out.wait()
    half_out(other).wait()


def copy_out(ug_in, ig_in, ug_out, ig_out, ug_here, ig_here, sems):
    loads = []
    stores = []
    for source, here, target, count in (
        (ug_in, ug_here, ug_out, 2),
        (ig_in, ig_here, ig_out, 4),
    ):
        rows = source.shape[0] // count
        for k in range(count):
            span = pl.ds(k * rows, rows)
            slot = len(loads)
            loads.append(
                pltpu.make_async_copy(source.at[span, :], here.at[span, :], sems.at[0, slot])
            )
            stores.append(
                pltpu.make_async_copy(here.at[span, :], target.at[span, :], sems.at[1, slot])
            )
    for load in loads:
        load.start()
    for load, store in zip(loads, stores):
        load.wait()
        store.start()
    for store in stores:
        store.wait()


def per_device(total_users, chips, rings, user_embed, item_embed, positive, user_count, item_count):
    rows, width = user_embed.shape
    cols = item_embed.shape[0]
    tiles = cols // LANES
    strip = rows // rings
    direct = rings // 8
    sub = strip // PARTS
    hub_rows = (2 * direct if rings > 8 else 1) * sub + sub // 2
    piece = cols // 2 // chips
    vmem = pl.BlockSpec(memory_space=pltpu.VMEM)
    hbm = pl.BlockSpec(memory_space=pltpu.HBM)
    dma = pltpu.SemaphoreType.DMA
    user_grad, item_grad, loss = pl.pallas_call(
        functools.partial(kernel, total_users, chips, rings),
        out_shape=(
            jax.ShapeDtypeStruct((rows, width), F32),
            jax.ShapeDtypeStruct((cols, width), F32),
            jax.ShapeDtypeStruct((1, 1), F32),
        ),
        in_specs=[hbm] * 2 + [vmem] * 3,
        out_specs=(hbm, hbm, pl.BlockSpec(memory_space=pltpu.SMEM)),
        scratch_shapes=[
            pltpu.VMEM((rows, width), F32),
            pltpu.VMEM((cols, width), F32),
            pltpu.VMEM((rows, width), user_embed.dtype),
            pltpu.VMEM((cols, width), item_embed.dtype),
            pltpu.VMEM((rows, width), user_embed.dtype),
            pltpu.VMEM((rows, cols), F32),
            pltpu.VMEM((rows, cols), F32),
            pltpu.VMEM((rows, cols), F32),
            pltpu.VMEM((2, rows, cols // 2), jnp.bfloat16),
            pltpu.VMEM((rows, width), F32),
            pltpu.VMEM((2, cols // 2 + 8, width), F32),
            pltpu.VMEM((tiles, LANES), F32),
            pltpu.VMEM((rows, LANES), F32),
            pltpu.VMEM((rows, LANES), F32),
            pltpu.VMEM((rows, LANES), F32),
            pltpu.VMEM((tiles, 8, LANES), F32),
            pltpu.VMEM((tiles, 8, LANES), F32),
            pltpu.VMEM((tiles, 8, LANES), F32),
            pltpu.VMEM((rings, rows // LANES, LANES), F32),
            pltpu.VMEM((2 * chips, 2 * tiles, LANES), F32),
            pltpu.VMEM((rings, 8, LANES), F32),
            pltpu.VMEM((PARTS, 2, hub_rows, width), F32),
            pltpu.VMEM((PARTS, 2 * direct + 2, sub, width), F32),
            pltpu.VMEM((cols // 2 + 8, width), F32),
            pltpu.VMEM((chips, piece + 8, width), F32),
            pltpu.VMEM((chips, piece + 8, width), F32),
            dma((2,)),
            dma((2,)),
            dma((4,)),
            dma((4,)),
            dma((PARTS, 2)),
            dma((PARTS,)),
            dma((PARTS, 2)),
            dma((8,)),
            dma((chips - 1,)),
            dma((2,)),
            dma((3,)),
        ],
        compiler_params=pltpu.CompilerParams(
            collective_id=0, has_side_effects=True, vmem_limit_bytes=60 * 1024 * 1024
        ),
        name="two_sided",
    )(
        user_embed,
        item_embed,
        positive.reshape(rows // LANES, LANES),
        user_count.reshape(rows // LANES, LANES),
        item_count.reshape(tiles, LANES),
    )
    user_grad, item_grad = pl.pallas_call(
        copy_out,
        out_shape=(
            jax.ShapeDtypeStruct((rows, width), F32),
            jax.ShapeDtypeStruct((cols, width), F32),
        ),
        in_specs=[hbm] * 2,
        out_specs=(hbm, hbm),
        scratch_shapes=[
            pltpu.VMEM((rows, width), F32),
            pltpu.VMEM((cols, width), F32),
            dma((2, 6)),
        ],
        compiler_params=pltpu.CompilerParams(vmem_limit_bytes=60 * 1024 * 1024),
        name="copy_out",
    )(user_grad, item_grad)
    return user_grad, item_grad, loss.reshape(())


def solution(mesh):
    row_size, rings = mesh.shape["row"], mesh.shape["col"]

    def whole(user_embed, *others):
        body = functools.partial(per_device, user_embed.shape[0], row_size // 2, rings)
        return jax.shard_map(
            body,
            mesh=mesh,
            in_specs=(P("row", None), P("col", None), P("row"), P("row"), P("col")),
            out_specs=(P("row", None), P("col", None), P()),
            check_vma=False,
        )(user_embed, *others)

    return whole
```

```python
import functools

import jax
import jax.numpy as jnp
from jax import lax
from jax.experimental import pallas as pl
from jax.experimental.pallas import tpu as pltpu
from jax.sharding import PartitionSpec as P

MESH = pl.DeviceIdType.MESH
LANES = 128
BLOCK = 128
CORE_PARTS = 4
PARTS = 2
F32 = jnp.float32


def columns_of(row):
    return jnp.transpose(jnp.broadcast_to(row, (LANES, LANES)))


def fold(block):
    return block.reshape(block.shape[0] // 8, 8, LANES)


def merged_lse(parts):
    top = jnp.max(parts, axis=0)
    return top + jnp.log(jnp.sum(jnp.exp(parts - top[None]), axis=0))


def kernel(
    total_users,
    chips,
    rings,
    user_hbm,
    item_hbm,
    pos_ref,
    ucnt_ref,
    icnt_ref,
    ug_hbm,
    ig_hbm,
    loss_ref,
    ug_ref,
    ig_ref,
    user_ref,
    item_ref,
    users,
    scores,
    row_exp,
    col_exp,
    coupling,
    part,
    items,
    log_item,
    lu_col,
    pos_col,
    row_col,
    col_max,
    col_sum,
    hits_acc,
    z_stats,
    c_stats,
    p_stats,
    z_loss,
    hub_in,
    near_in,
    core_in,
    plane_out,
    plane_in,
    z_sems,
    s_sems,
    p_sems,
    l_sems,
    w_sems,
    h_sems,
    n_sems,
    g_sems,
    x_sems,
    back_sems,
    in_sems,
    out_sems,
):
    rows_here, width = user_ref.shape
    cols_here = item_ref.shape[0]
    tiles = cols_here // LANES
    row_tiles = rows_here // LANES
    half_cols = cols_here // 2
    half_tiles = tiles // 2
    blocks = rows_here // BLOCK
    piece = half_cols // chips

    user_in = pltpu.make_async_copy(user_hbm, user_ref, in_sems.at[0])
    item_in = pltpu.make_async_copy(item_hbm, item_ref, in_sems.at[1])
    item_in.start()
    user_in.start()

    mine = lax.axis_index("row")
    ring = lax.axis_index("col")
    chip = mine // 2
    core = mine % 2
    other = 1 - core
    twin = chip * 2 + other

    def z_peer(step):
        return (mine, (ring + step) % rings)

    def chip_peer(step):
        return (((chip + step) % chips) * 2 + core, ring)

    z_steps = sorted(range(1, rings), key=lambda k: -min(k, rings - k))
    chip_steps = list(range(1, chips))

    barrier = pltpu.get_barrier_semaphore()
    for step in z_steps:
        pl.semaphore_signal(barrier, inc=1, device_id=z_peer(step), device_id_type=MESH)
    for step in chip_steps:
        pl.semaphore_signal(barrier, inc=1, device_id=chip_peer(step), device_id_type=MESH)
    pl.semaphore_signal(barrier, inc=1, device_id=(twin, ring), device_id_type=MESH)

    def remote(src, dst, send_sem, recv_sem, device):
        return pltpu.make_async_remote_copy(
            src_ref=src,
            dst_ref=dst,
            send_sem=send_sem,
            recv_sem=recv_sem,
            device_id=device,
            device_id_type=MESH,
        )

    def wait_bytes(ref, sem):
        pltpu.make_async_copy(ref, ref, sem).wait()

    log_item[...] = jnp.log(icnt_ref[...].astype(F32))
    log_user = jnp.log(ucnt_ref[...].astype(F32))
    local_pos = pos_ref[...].astype(F32) - (ring * cols_here).astype(F32)
    for k in range(row_tiles):
        span = pl.ds(k * LANES, LANES)
        lu_col[span, :] = columns_of(log_user[k : k + 1, :])
        pos_col[span, :] = columns_of(local_pos[k : k + 1, :])
    col_max[...] = jnp.full(col_max.shape, -jnp.inf, F32)
    col_sum[...] = jnp.zeros(col_sum.shape, F32)
    hits_acc[...] = jnp.zeros(hits_acc.shape, F32)
    lane = lax.broadcasted_iota(jnp.int32, (BLOCK, LANES), 1).astype(F32)

    def sweep_one(b, z_part):
        span = pl.ds(pl.multiple_of(b * BLOCK, BLOCK), BLOCK)
        scores[span, :] = 2.0 * lax.dot_general(
            user_ref[span, :],
            item_ref[...],
            (((1,), (1,)), ((), ())),
            preferred_element_type=F32,
        )
        lu = lu_col[span, :]
        pos = pos_col[span, :]
        top = None
        for t in range(tiles):
            s = scores[span, t * LANES : (t + 1) * LANES]
            shifted = s - log_item[t : t + 1, :]
            top = shifted if top is None else jnp.maximum(top, shifted)
            col_max[t] = jnp.maximum(col_max[t], jnp.max(fold(s - lu), axis=0))
            match = pos == lane + float(t * LANES)
            hits_acc[t] += jnp.sum(fold(jnp.where(match, 1.0, 0.0)), axis=0)
            z_part = z_part + jnp.sum(fold(jnp.where(match, s + shifted, 0.0)), axis=0)
        row_col[span, :] = jnp.broadcast_to(jnp.max(top, axis=1, keepdims=True), (BLOCK, LANES))
        return z_part

    item_in.wait()
    user_in.wait()
    z_part = lax.fori_loop(0, blocks, sweep_one, jnp.zeros((8, LANES), F32))
    for t in range(tiles):
        col_max[t] = jnp.broadcast_to(jnp.max(col_max[t], axis=0, keepdims=True), (8, LANES))

    def sweep_two(b, carry):
        span = pl.ds(pl.multiple_of(b * BLOCK, BLOCK), BLOCK)
        lu = lu_col[span, :]
        row_max = row_col[span, :]
        total = jnp.zeros((BLOCK, LANES), F32)
        for t in range(tiles):
            s = scores[span, t * LANES : (t + 1) * LANES]
            row = jnp.exp(s - log_item[t : t + 1, :] - row_max)
            row_exp[span, t * LANES : (t + 1) * LANES] = row
            total = total + row
            col = jnp.exp(s - lu - col_max[t, 0:1, :])
            col_exp[span, t * LANES : (t + 1) * LANES] = col
            col_sum[t] += jnp.sum(fold(col), axis=0)
        lse = row_max + jnp.log(jnp.sum(total, axis=1, keepdims=True))
        z_stats[ring, pl.ds(b, 1), :] = jnp.transpose(lse)[0:1, :]
        return carry

    lax.fori_loop(0, blocks, sweep_two, 0)
    col_lse_rows = []
    hits_rows = []
    for t in range(tiles):
        total = jnp.sum(col_sum[t], axis=0, keepdims=True)
        col_lse_rows.append(col_max[t, 0:1, :] + jnp.log(total))
        hits_rows.append(jnp.sum(hits_acc[t], axis=0, keepdims=True))
    c_stats[0] = jnp.concatenate(col_lse_rows + hits_rows, axis=0)

    pl.semaphore_wait(barrier, rings - 1 + chips - 1 + 1)
    core_stat = remote(c_stats.at[0], c_stats.at[1], s_sems.at[0], s_sems.at[1], (twin, ring))
    core_stat.start()
    for step in z_steps:
        remote(
            z_stats.at[ring], z_stats.at[ring], z_sems.at[0], z_sems.at[1], z_peer(step)
        ).start()
    core_stat.wait()
    one, two = c_stats[0], c_stats[1]
    p_stats[chip, 0:tiles, :] = merged_lse(jnp.stack([one[:tiles], two[:tiles]]))
    p_stats[chip, tiles : 2 * tiles, :] = one[tiles:] + two[tiles:]
    for step in chip_steps:
        remote(
            p_stats.at[chip], p_stats.at[chip], p_sems.at[0], p_sems.at[1], chip_peer(step)
        ).start()
    wait_bytes(z_stats.at[pl.ds(0, rings - 1)], z_sems.at[1])
    row_lse = merged_lse(z_stats[...])
    for k in range(row_tiles):
        span = pl.ds(k * LANES, LANES)
        row_col[span, :] = jnp.exp(row_col[span, :] - columns_of(row_lse[k : k + 1, :]))
    user_loss = jnp.sum(row_lse + log_user, axis=0, keepdims=True)
    match_loss = jnp.sum(z_part, axis=0, keepdims=True)
    loss_rows = jnp.concatenate([user_loss, match_loss, jnp.zeros((6, LANES), F32)], axis=0)
    wait_bytes(p_stats.at[pl.ds(0, chips - 1)], p_sems.at[1])
    item_stats = p_stats[...]
    col_lse = merged_lse(item_stats[:, :tiles])
    pos_hits = jnp.sum(item_stats[:, tiles:], axis=0)
    item_loss = jnp.sum(pos_hits * col_lse, axis=0, keepdims=True)
    col_top = jnp.concatenate([col_max[t, 0:1, :] for t in range(tiles)], axis=0)
    col_scale = pos_hits * jnp.exp(col_top - col_lse)

    strip = rows_here // rings
    sub = strip // PARTS
    per_block = BLOCK // sub
    direct = rings // 8
    hub = 2 * direct + 1
    covers = [c for c in range(-direct, direct + 1) if c != 0 and hub + c < rings // 2]
    far = rings // 2 - hub
    order = [(direct + 1 + j) % rings for j in range(rings)]
    signs = (1, -1)

    def sub_at(offset, h, start=0, size=None):
        size = sub if size is None else size
        first = (ring + offset + rings) % rings * strip + h * sub + start
        return pl.ds(pl.multiple_of(first, 8 if size < 16 else size), size)

    def part_at(offset, h):
        return pl.ds(h * (rows_here // PARTS) + order.index(offset % rings) * sub, sub)

    def z_at(offset):
        return z_peer(offset % rings)

    sub_lane = lane[:sub, :]

    def user_block(b):
        for k in range(b * per_block, (b + 1) * per_block):
            h, j = k // rings, k % rings
            source = sub_at(order[j], h)
            target = pl.ds(k * sub, sub)
            users[target, :] = user_ref[source, :]
            pos = pos_col[source, :]
            row = row_col[source, :]
            for t in range(tiles):
                here = slice(t * LANES, (t + 1) * LANES)
                value = row_exp[source, here] * row + col_exp[source, here] * col_scale[t : t + 1, :]
                match = pos == sub_lane + float(t * LANES)
                value = value - jnp.where(match, 2.0, 0.0)
                at = (t % half_tiles) * LANES
                coupling[t // half_tiles, target, at : at + LANES] = value.astype(jnp.bfloat16)
        span = pl.ds(b * BLOCK, BLOCK)
        part[span, :] = 2.0 * (
            jnp.dot(coupling[0, span, :], item_ref[:half_cols, :], preferred_element_type=F32)
            + jnp.dot(coupling[1, span, :], item_ref[half_cols:, :], preferred_element_type=F32)
        )

    leaving = {}
    hub_half = pl.ds(len(covers) * sub, sub // 2)
    for h in range(PARTS):
        for index, sign in enumerate(signs):
            for slot, c in enumerate(covers):
                leaving.setdefault((h, -sign * (hub + c) % rings), []).append(
                    (
                        part.at[part_at(-sign * (hub + c), h), :],
                        hub_in.at[h, index, pl.ds(slot * sub, sub), :],
                        w_sems.at[0],
                        h_sems.at[h, index],
                        z_at(-sign * c),
                    )
                )
            first = part_at(rings // 2, h).start + index * (sub // 2)
            leaving.setdefault((h, rings // 2), []).append(
                (
                    part.at[pl.ds(first, sub // 2), :],
                    hub_in.at[h, index, hub_half, :],
                    w_sems.at[0],
                    h_sems.at[h, index],
                    z_at(-sign * far),
                )
            )
            for step in range(1, direct + 1):
                leaving.setdefault((h, -sign * step % rings), []).append(
                    (
                        part.at[part_at(-sign * step, h), :],
                        near_in.at[h, index * direct + step - 1],
                        w_sems.at[1],
                        n_sems.at[h],
                        z_at(-sign * step),
                    )
                )

    for b in range(blocks):
        user_block(b)
        for k in range(b * per_block, (b + 1) * per_block):
            for copy in leaving.get((k // rings, order[k % rings]), ()):
                remote(*copy).start()

    def hub_sum(h):
        for index, sign in enumerate(signs):
            wait_bytes(hub_in.at[h, index], h_sems.at[h, index])
            span = part_at(-sign * hub, h)
            total = part[span, :]
            for slot in range(len(covers)):
                total = total + hub_in[h, index, slot * sub : (slot + 1) * sub, :]
            part[span, :] = total
            half = pl.ds(span.start + index * (sub // 2), sub // 2)
            part[half, :] += hub_in[h, index, hub_half, :]
            remote(
                part.at[span, :],
                near_in.at[h, 2 * direct + index],
                w_sems.at[1],
                n_sems.at[h],
                z_at(-sign * hub),
            ).start()

    def own_sum(h):
        wait_bytes(near_in.at[h], n_sems.at[h])
        total = part[part_at(0, h), :]
        for slot in range(2 * direct + 2):
            total = total + near_in[h, slot]
        span = sub_at(0, h)
        ug_ref[span, :] = total
        here = ug_ref.at[span, :]
        for index, sign in enumerate(signs):
            remote(here, here, w_sems.at[2], g_sems.at[h, index], z_at(sign * hub)).start()
        for step in range(1, direct + 1):
            for sign in signs:
                remote(here, here, w_sems.at[2], w_sems.at[3], z_at(sign * step)).start()

    def hub_spread(h):
        for index, sign in enumerate(signs):
            here = ug_ref.at[sub_at(-sign * hub, h), :]
            wait_bytes(here, g_sems.at[h, index])
            half = ug_ref.at[sub_at(-sign * hub, h, index * (sub // 2), sub // 2), :]
            remote(half, half, w_sems.at[2], w_sems.at[3], z_at(sign * far)).start()
            for c in sorted(covers, key=lambda c: -abs(c)):
                remote(here, here, w_sems.at[2], w_sems.at[3], z_at(sign * c)).start()

    def gather_end():
        wait_bytes(ug_ref.at[pl.ds(0, (rings - 3) * strip), :], w_sems.at[3])

    def item_part(which):
        items[which, :half_cols, :] = 2.0 * lax.dot_general(
            coupling[which],
            users[...],
            (((0,), (0,)), ((), ())),
            preferred_element_type=F32,
        )

    core_rows = half_cols // CORE_PARTS

    def core_send():
        item_part(other)
        items[other, half_cols:, :LANES] = loss_rows
        items[other, half_cols:, LANES:] = jnp.zeros((8, width - LANES), F32)
        for k in range(CORE_PARTS):
            extra = 8 if k == CORE_PARTS - 1 else 0
            span = pl.ds(k * core_rows, core_rows + extra)
            remote(
                items.at[other, span, :],
                core_in.at[span, :],
                x_sems.at[0],
                x_sems.at[1],
                (twin, ring),
            ).start()

    def plane_send():
        wait_bytes(core_in, x_sems.at[1])
        pair_loss = core_in[half_cols:, :LANES] + loss_rows

        def pack(k, carry):
            span = pl.ds(pl.multiple_of(k * piece, piece), piece)
            plane_out[k, :piece, :] = items[core, span, :] + core_in[span, :]
            plane_out[k, piece:, :LANES] = pair_loss
            plane_out[k, piece:, LANES:] = jnp.zeros((8, width - LANES), F32)
            return carry

        lax.fori_loop(0, chips, pack, 0)
        for step in chip_steps:
            remote(
                plane_out.at[(chip + step) % chips],
                plane_in.at[chip],
                x_sems.at[2],
                x_sems.at[3],
                chip_peer(step),
            ).start()
        plane_in[chip] = plane_out[chip]

    def piece_at(half_index, index):
        start = half_index * half_cols + index % chips * piece
        return pl.ds(pl.multiple_of(start, piece), piece)

    def plane_sum():
        wait_bytes(plane_in.at[pl.ds(0, chips - 1)], x_sems.at[3])
        total = plane_in[0]
        for k in range(1, chips):
            total = total + plane_in[k]
        here = ig_ref.at[piece_at(core, chip), :]
        here[...] = total[:piece, :]
        for step in chip_steps:
            remote(
                here, here, x_sems.at[4], back_sems.at[step - 1], chip_peer(step)
            ).start()
        remote(here, here, x_sems.at[5], x_sems.at[6], (twin, ring)).start()
        z_loss[ring] = jnp.broadcast_to(
            item_loss - total[piece + 1 : piece + 2, :LANES], (8, LANES)
        )
        for step in z_steps:
            remote(
                z_loss.at[ring], z_loss.at[ring], l_sems.at[0], l_sems.at[1], z_peer(step)
            ).start()
        return total[piece : piece + 1, :LANES]

    def forward(step):
        here = ig_ref.at[piece_at(core, chip + chips - step), :]
        wait_bytes(here, back_sems.at[step - 1])
        remote(here, here, x_sems.at[5], x_sems.at[6], (twin, ring)).start()

    others = pl.ds(0, (chips - 1) * piece)

    def loss_end(users):
        wait_bytes(z_loss.at[pl.ds(0, rings - 1)], l_sems.at[1])
        total = users
        for k in range(rings):
            total = total + z_loss[k, 0:1, :]
        loss_ref[0, 0] = jnp.sum(total) * (1.0 / total_users)

    core_send()
    item_part(core)
    hub_sum(0)
    plane_send()
    hub_sum(1)
    own_sum(0)
    own_sum(1)
    plane_total = plane_sum()
    hub_spread(0)
    hub_spread(1)
    for step in chip_steps:
        forward(step)
    loss_end(plane_total)

    def half_out(which):
        span = pl.ds(pl.multiple_of(which * half_cols, half_cols), half_cols)
        return pltpu.make_async_copy(ig_ref.at[span, :], ig_hbm.at[span, :], out_sems.at[which])

    half_out(core).start()
    gather_end()
    user_out = pltpu.make_async_copy(ug_ref, ug_hbm, out_sems.at[2])
    user_out.start()
    wait_bytes(ig_ref.at[pl.ds(0, half_cols), :], x_sems.at[6])
    half_out(other).start()

    wait_bytes(z_stats.at[pl.ds(0, rings - 1)], z_sems.at[0])
    wait_bytes(p_stats.at[pl.ds(0, chips - 1)], p_sems.at[0])
    wait_bytes(z_loss.at[pl.ds(0, rings - 1)], l_sems.at[0])
    wait_bytes(hub_in, w_sems.at[0])
    wait_bytes(near_in, w_sems.at[1])
    wait_bytes(ug_ref.at[pl.ds(0, (rings - 1) * strip), :], w_sems.at[2])
    wait_bytes(core_in, x_sems.at[0])
    wait_bytes(plane_in.at[pl.ds(0, chips - 1)], x_sems.at[2])
    wait_bytes(ig_ref.at[others, :], x_sems.at[4])
    wait_bytes(ig_ref.at[pl.ds(0, half_cols), :], x_sems.at[5])
    half_out(core).wait()
    user_out.wait()
    half_out(other).wait()


def copy_out(ug_in, ig_in, ug_out, ig_out, ug_here, ig_here, sems):
    loads = []
    stores = []
    for source, here, target, count in (
        (ug_in, ug_here, ug_out, 2),
        (ig_in, ig_here, ig_out, 4),
    ):
        rows = source.shape[0] // count
        for k in range(count):
            span = pl.ds(k * rows, rows)
            slot = len(loads)
            loads.append(
                pltpu.make_async_copy(source.at[span, :], here.at[span, :], sems.at[0, slot])
            )
            stores.append(
                pltpu.make_async_copy(here.at[span, :], target.at[span, :], sems.at[1, slot])
            )
    for load in loads:
        load.start()
    for load, store in zip(loads, stores):
        load.wait()
        store.start()
    for store in stores:
        store.wait()


def per_device(total_users, chips, rings, user_embed, item_embed, positive, user_count, item_count):
    rows, width = user_embed.shape
    cols = item_embed.shape[0]
    tiles = cols // LANES
    strip = rows // rings
    direct = rings // 8
    sub = strip // PARTS
    hub_rows = (2 * direct if rings > 8 else 1) * sub + sub // 2
    piece = cols // 2 // chips
    vmem = pl.BlockSpec(memory_space=pltpu.VMEM)
    hbm = pl.BlockSpec(memory_space=pltpu.HBM)
    dma = pltpu.SemaphoreType.DMA
    user_grad, item_grad, loss = pl.pallas_call(
        functools.partial(kernel, total_users, chips, rings),
        out_shape=(
            jax.ShapeDtypeStruct((rows, width), F32),
            jax.ShapeDtypeStruct((cols, width), F32),
            jax.ShapeDtypeStruct((1, 1), F32),
        ),
        in_specs=[hbm] * 2 + [vmem] * 3,
        out_specs=(hbm, hbm, pl.BlockSpec(memory_space=pltpu.SMEM)),
        scratch_shapes=[
            pltpu.VMEM((rows, width), F32),
            pltpu.VMEM((cols, width), F32),
            pltpu.VMEM((rows, width), user_embed.dtype),
            pltpu.VMEM((cols, width), item_embed.dtype),
            pltpu.VMEM((rows, width), user_embed.dtype),
            pltpu.VMEM((rows, cols), F32),
            pltpu.VMEM((rows, cols), F32),
            pltpu.VMEM((rows, cols), F32),
            pltpu.VMEM((2, rows, cols // 2), jnp.bfloat16),
            pltpu.VMEM((rows, width), F32),
            pltpu.VMEM((2, cols // 2 + 8, width), F32),
            pltpu.VMEM((tiles, LANES), F32),
            pltpu.VMEM((rows, LANES), F32),
            pltpu.VMEM((rows, LANES), F32),
            pltpu.VMEM((rows, LANES), F32),
            pltpu.VMEM((tiles, 8, LANES), F32),
            pltpu.VMEM((tiles, 8, LANES), F32),
            pltpu.VMEM((tiles, 8, LANES), F32),
            pltpu.VMEM((rings, rows // LANES, LANES), F32),
            pltpu.VMEM((2, 2 * tiles, LANES), F32),
            pltpu.VMEM((chips, 2 * tiles, LANES), F32),
            pltpu.VMEM((rings, 8, LANES), F32),
            pltpu.VMEM((PARTS, 2, hub_rows, width), F32),
            pltpu.VMEM((PARTS, 2 * direct + 2, sub, width), F32),
            pltpu.VMEM((cols // 2 + 8, width), F32),
            pltpu.VMEM((chips, piece + 8, width), F32),
            pltpu.VMEM((chips, piece + 8, width), F32),
            dma((2,)),
            dma((2,)),
            dma((2,)),
            dma((4,)),
            dma((4,)),
            dma((PARTS, 2)),
            dma((PARTS,)),
            dma((PARTS, 2)),
            dma((8,)),
            dma((chips - 1,)),
            dma((2,)),
            dma((3,)),
        ],
        compiler_params=pltpu.CompilerParams(
            collective_id=0, has_side_effects=True, vmem_limit_bytes=60 * 1024 * 1024
        ),
        name="two_sided",
    )(
        user_embed,
        item_embed,
        positive.reshape(rows // LANES, LANES),
        user_count.reshape(rows // LANES, LANES),
        item_count.reshape(tiles, LANES),
    )
    user_grad, item_grad = pl.pallas_call(
        copy_out,
        out_shape=(
            jax.ShapeDtypeStruct((rows, width), F32),
            jax.ShapeDtypeStruct((cols, width), F32),
        ),
        in_specs=[hbm] * 2,
        out_specs=(hbm, hbm),
        scratch_shapes=[
            pltpu.VMEM((rows, width), F32),
            pltpu.VMEM((cols, width), F32),
            dma((2, 6)),
        ],
        compiler_params=pltpu.CompilerParams(vmem_limit_bytes=60 * 1024 * 1024),
        name="copy_out",
    )(user_grad, item_grad)
    return user_grad, item_grad, loss.reshape(())


def solution(mesh):
    row_size, rings = mesh.shape["row"], mesh.shape["col"]

    def whole(user_embed, *others):
        body = functools.partial(per_device, user_embed.shape[0], row_size // 2, rings)
        return jax.shard_map(
            body,
            mesh=mesh,
            in_specs=(P("row", None), P("col", None), P("row"), P("row"), P("col")),
            out_specs=(P("row", None), P("col", None), P()),
            check_vma=False,
        )(user_embed, *others)

    return whole
```

```python
import functools

import jax
import jax.numpy as jnp
from jax import lax
from jax.experimental import pallas as pl
from jax.experimental.pallas import tpu as pltpu
from jax.sharding import PartitionSpec as P

MESH = pl.DeviceIdType.MESH
LANES = 128
BLOCK = 128
CORE_PARTS = 4
PARTS = 2
F32 = jnp.float32


def columns_of(row):
    return jnp.transpose(jnp.broadcast_to(row, (LANES, LANES)))


def fold(block):
    return block.reshape(block.shape[0] // 8, 8, LANES)


def merged_lse(parts):
    top = jnp.max(parts, axis=0)
    return top + jnp.log(jnp.sum(jnp.exp(parts - top[None]), axis=0))


def kernel(
    total_users,
    chips,
    rings,
    user_hbm,
    item_hbm,
    pos_ref,
    ucnt_ref,
    icnt_ref,
    ug_hbm,
    ig_hbm,
    loss_ref,
    ug_ref,
    ig_ref,
    user_ref,
    item_ref,
    users,
    scores,
    row_exp,
    col_exp,
    coupling,
    part,
    items,
    log_item,
    lu_col,
    pos_col,
    row_col,
    col_max,
    col_sum,
    hits_acc,
    z_stats,
    c_stats,
    p_stats,
    z_loss,
    hub_in,
    near_in,
    core_in,
    plane_out,
    plane_in,
    z_sems,
    s_sems,
    p_sems,
    l_sems,
    w_sems,
    h_sems,
    n_sems,
    g_sems,
    x_sems,
    back_sems,
    in_sems,
    out_sems,
):
    rows_here, width = user_ref.shape
    cols_here = item_ref.shape[0]
    tiles = cols_here // LANES
    row_tiles = rows_here // LANES
    half_cols = cols_here // 2
    half_tiles = tiles // 2
    blocks = rows_here // BLOCK
    piece = half_cols // chips

    user_in = pltpu.make_async_copy(user_hbm, user_ref, in_sems.at[0])
    item_in = pltpu.make_async_copy(item_hbm, item_ref, in_sems.at[1])
    item_in.start()
    user_in.start()

    mine = lax.axis_index("row")
    ring = lax.axis_index("col")
    chip = mine // 2
    core = mine % 2
    other = 1 - core
    twin = chip * 2 + other

    def z_peer(step):
        return (mine, (ring + step) % rings)

    def chip_peer(step):
        return (((chip + step) % chips) * 2 + core, ring)

    z_steps = sorted(range(1, rings), key=lambda k: -min(k, rings - k))
    chip_steps = list(range(1, chips))

    barrier = pltpu.get_barrier_semaphore()
    for step in z_steps:
        pl.semaphore_signal(barrier, inc=1, device_id=z_peer(step), device_id_type=MESH)
    for step in chip_steps:
        pl.semaphore_signal(barrier, inc=1, device_id=chip_peer(step), device_id_type=MESH)
    pl.semaphore_signal(barrier, inc=1, device_id=(twin, ring), device_id_type=MESH)

    def remote(src, dst, send_sem, recv_sem, device):
        return pltpu.make_async_remote_copy(
            src_ref=src,
            dst_ref=dst,
            send_sem=send_sem,
            recv_sem=recv_sem,
            device_id=device,
            device_id_type=MESH,
        )

    def wait_bytes(ref, sem):
        pltpu.make_async_copy(ref, ref, sem).wait()

    log_item[...] = jnp.log(icnt_ref[...].astype(F32))
    log_user = jnp.log(ucnt_ref[...].astype(F32))
    local_pos = pos_ref[...].astype(F32) - (ring * cols_here).astype(F32)
    for k in range(row_tiles):
        span = pl.ds(k * LANES, LANES)
        lu_col[span, :] = columns_of(log_user[k : k + 1, :])
        pos_col[span, :] = columns_of(local_pos[k : k + 1, :])
    col_max[...] = jnp.full(col_max.shape, -jnp.inf, F32)
    col_sum[...] = jnp.zeros(col_sum.shape, F32)
    hits_acc[...] = jnp.zeros(hits_acc.shape, F32)
    lane = lax.broadcasted_iota(jnp.int32, (BLOCK, LANES), 1).astype(F32)

    def sweep_one(b, z_part):
        span = pl.ds(pl.multiple_of(b * BLOCK, BLOCK), BLOCK)
        scores[span, :] = 2.0 * lax.dot_general(
            user_ref[span, :],
            item_ref[...],
            (((1,), (1,)), ((), ())),
            preferred_element_type=F32,
        )
        lu = lu_col[span, :]
        pos = pos_col[span, :]
        top = None
        for t in range(tiles):
            s = scores[span, t * LANES : (t + 1) * LANES]
            shifted = s - log_item[t : t + 1, :]
            top = shifted if top is None else jnp.maximum(top, shifted)
            col_max[t] = jnp.maximum(col_max[t], jnp.max(fold(s - lu), axis=0))
            match = pos == lane + float(t * LANES)
            hits_acc[t] += jnp.sum(fold(jnp.where(match, 1.0, 0.0)), axis=0)
            z_part = z_part + jnp.sum(fold(jnp.where(match, s + shifted, 0.0)), axis=0)
        row_col[span, :] = jnp.broadcast_to(jnp.max(top, axis=1, keepdims=True), (BLOCK, LANES))
        return z_part

    item_in.wait()
    user_in.wait()
    z_part = lax.fori_loop(0, blocks, sweep_one, jnp.zeros((8, LANES), F32))
    for t in range(tiles):
        col_max[t] = jnp.broadcast_to(jnp.max(col_max[t], axis=0, keepdims=True), (8, LANES))

    def sweep_two(b, carry):
        span = pl.ds(pl.multiple_of(b * BLOCK, BLOCK), BLOCK)
        lu = lu_col[span, :]
        row_max = row_col[span, :]
        total = jnp.zeros((BLOCK, LANES), F32)
        for t in range(tiles):
            s = scores[span, t * LANES : (t + 1) * LANES]
            row = jnp.exp(s - log_item[t : t + 1, :] - row_max)
            row_exp[span, t * LANES : (t + 1) * LANES] = row
            total = total + row
            col = jnp.exp(s - lu - col_max[t, 0:1, :])
            col_exp[span, t * LANES : (t + 1) * LANES] = col
            col_sum[t] += jnp.sum(fold(col), axis=0)
        lse = row_max + jnp.log(jnp.sum(total, axis=1, keepdims=True))
        z_stats[ring, pl.ds(b, 1), :] = jnp.transpose(lse)[0:1, :]
        return carry

    lax.fori_loop(0, blocks, sweep_two, 0)
    col_lse_rows = []
    hits_rows = []
    for t in range(tiles):
        total = jnp.sum(col_sum[t], axis=0, keepdims=True)
        col_lse_rows.append(col_max[t, 0:1, :] + jnp.log(total))
        hits_rows.append(jnp.sum(hits_acc[t], axis=0, keepdims=True))
    c_stats[0] = jnp.concatenate(col_lse_rows + hits_rows, axis=0)

    pl.semaphore_wait(barrier, rings - 1 + chips - 1 + 1)
    core_stat = remote(c_stats.at[0], c_stats.at[1], s_sems.at[0], s_sems.at[1], (twin, ring))
    core_stat.start()
    for step in z_steps:
        remote(
            z_stats.at[ring], z_stats.at[ring], z_sems.at[0], z_sems.at[1], z_peer(step)
        ).start()
    core_stat.wait()
    one, two = c_stats[0], c_stats[1]
    p_stats[chip, 0:tiles, :] = merged_lse(jnp.stack([one[:tiles], two[:tiles]]))
    p_stats[chip, tiles : 2 * tiles, :] = one[tiles:] + two[tiles:]
    for step in chip_steps:
        remote(
            p_stats.at[chip], p_stats.at[chip], p_sems.at[0], p_sems.at[1], chip_peer(step)
        ).start()
    wait_bytes(z_stats.at[pl.ds(0, rings - 1)], z_sems.at[1])
    row_lse = merged_lse(z_stats[...])
    for k in range(row_tiles):
        span = pl.ds(k * LANES, LANES)
        row_col[span, :] = jnp.exp(row_col[span, :] - columns_of(row_lse[k : k + 1, :]))
    user_loss = jnp.sum(row_lse + log_user, axis=0, keepdims=True)
    match_loss = jnp.sum(z_part, axis=0, keepdims=True)
    loss_rows = jnp.concatenate([user_loss, match_loss, jnp.zeros((6, LANES), F32)], axis=0)
    wait_bytes(p_stats.at[pl.ds(0, chips - 1)], p_sems.at[1])
    item_stats = p_stats[...]
    col_lse = merged_lse(item_stats[:, :tiles])
    pos_hits = jnp.sum(item_stats[:, tiles:], axis=0)
    item_loss = jnp.sum(pos_hits * col_lse, axis=0, keepdims=True)
    col_top = jnp.concatenate([col_max[t, 0:1, :] for t in range(tiles)], axis=0)
    col_scale = pos_hits * jnp.exp(col_top - col_lse)

    strip = rows_here // rings
    sub = strip // PARTS
    per_block = BLOCK // sub
    direct = rings // 8
    hub = 2 * direct + 1
    covers = [c for c in range(-direct, direct + 1) if c != 0 and hub + c < rings // 2]
    far = rings // 2 - hub
    order = [(direct + 1 + j) % rings for j in range(rings)]
    signs = (1, -1)

    def sub_at(offset, h, start=0, size=None):
        size = sub if size is None else size
        first = (ring + offset + rings) % rings * strip + h * sub + start
        return pl.ds(pl.multiple_of(first, 8 if size < 16 else size), size)

    def part_at(offset, h):
        return pl.ds(h * (rows_here // PARTS) + order.index(offset % rings) * sub, sub)

    def z_at(offset):
        return z_peer(offset % rings)

    sub_lane = lane[:sub, :]

    def user_block(b):
        for k in range(b * per_block, (b + 1) * per_block):
            h, j = k // rings, k % rings
            source = sub_at(order[j], h)
            target = pl.ds(k * sub, sub)
            users[target, :] = user_ref[source, :]
            pos = pos_col[source, :]
            row = row_col[source, :]
            for t in range(tiles):
                here = slice(t * LANES, (t + 1) * LANES)
                value = row_exp[source, here] * row + col_exp[source, here] * col_scale[t : t + 1, :]
                match = pos == sub_lane + float(t * LANES)
                value = value - jnp.where(match, 2.0, 0.0)
                at = (t % half_tiles) * LANES
                coupling[t // half_tiles, target, at : at + LANES] = value.astype(jnp.bfloat16)
        span = pl.ds(b * BLOCK, BLOCK)
        part[span, :] = 2.0 * (
            jnp.dot(coupling[0, span, :], item_ref[:half_cols, :], preferred_element_type=F32)
            + jnp.dot(coupling[1, span, :], item_ref[half_cols:, :], preferred_element_type=F32)
        )

    leaving = {}
    hub_half = pl.ds(len(covers) * sub, sub // 2)
    for h in range(PARTS):
        for index, sign in enumerate(signs):
            for slot, c in enumerate(covers):
                leaving.setdefault((h, -sign * (hub + c) % rings), []).append(
                    (
                        part.at[part_at(-sign * (hub + c), h), :],
                        hub_in.at[h, index, pl.ds(slot * sub, sub), :],
                        w_sems.at[0],
                        h_sems.at[h, index],
                        z_at(-sign * c),
                    )
                )
            first = part_at(rings // 2, h).start + index * (sub // 2)
            leaving.setdefault((h, rings // 2), []).append(
                (
                    part.at[pl.ds(first, sub // 2), :],
                    hub_in.at[h, index, hub_half, :],
                    w_sems.at[0],
                    h_sems.at[h, index],
                    z_at(-sign * far),
                )
            )
            for step in range(1, direct + 1):
                leaving.setdefault((h, -sign * step % rings), []).append(
                    (
                        part.at[part_at(-sign * step, h), :],
                        near_in.at[h, index * direct + step - 1],
                        w_sems.at[1],
                        n_sems.at[h],
                        z_at(-sign * step),
                    )
                )

    for b in range(blocks):
        user_block(b)
        for k in range(b * per_block, (b + 1) * per_block):
            for copy in leaving.get((k // rings, order[k % rings]), ()):
                remote(*copy).start()

    def hub_sum(h):
        for index, sign in enumerate(signs):
            wait_bytes(hub_in.at[h, index], h_sems.at[h, index])
            span = part_at(-sign * hub, h)
            total = part[span, :]
            for slot in range(len(covers)):
                total = total + hub_in[h, index, slot * sub : (slot + 1) * sub, :]
            part[span, :] = total
            half = pl.ds(span.start + index * (sub // 2), sub // 2)
            part[half, :] += hub_in[h, index, hub_half, :]
            remote(
                part.at[span, :],
                near_in.at[h, 2 * direct + index],
                w_sems.at[1],
                n_sems.at[h],
                z_at(-sign * hub),
            ).start()

    def own_sum(h):
        wait_bytes(near_in.at[h], n_sems.at[h])
        total = part[part_at(0, h), :]
        for slot in range(2 * direct + 2):
            total = total + near_in[h, slot]
        span = sub_at(0, h)
        ug_ref[span, :] = total
        here = ug_ref.at[span, :]
        for index, sign in enumerate(signs):
            remote(here, here, w_sems.at[2], g_sems.at[h, index], z_at(sign * hub)).start()
        for step in range(1, direct + 1):
            for sign in signs:
                remote(here, here, w_sems.at[2], w_sems.at[3], z_at(sign * step)).start()

    def hub_spread(h):
        for index, sign in enumerate(signs):
            here = ug_ref.at[sub_at(-sign * hub, h), :]
            wait_bytes(here, g_sems.at[h, index])
            half = ug_ref.at[sub_at(-sign * hub, h, index * (sub // 2), sub // 2), :]
            remote(half, half, w_sems.at[2], w_sems.at[3], z_at(sign * far)).start()
            for c in sorted(covers, key=lambda c: -abs(c)):
                remote(here, here, w_sems.at[2], w_sems.at[3], z_at(sign * c)).start()

    def gather_end():
        wait_bytes(ug_ref.at[pl.ds(0, (rings - 3) * strip), :], w_sems.at[3])

    def item_part(which):
        items[which, :half_cols, :] = 2.0 * lax.dot_general(
            coupling[which],
            users[...],
            (((0,), (0,)), ((), ())),
            preferred_element_type=F32,
        )

    core_rows = half_cols // CORE_PARTS

    def core_send():
        item_part(other)
        items[other, half_cols:, :LANES] = loss_rows
        items[other, half_cols:, LANES:] = jnp.zeros((8, width - LANES), F32)
        for k in range(CORE_PARTS):
            extra = 8 if k == CORE_PARTS - 1 else 0
            span = pl.ds(k * core_rows, core_rows + extra)
            remote(
                items.at[other, span, :],
                core_in.at[span, :],
                x_sems.at[0],
                x_sems.at[1],
                (twin, ring),
            ).start()

    def plane_send():
        wait_bytes(core_in, x_sems.at[1])
        pair_loss = core_in[half_cols:, :LANES] + loss_rows

        def pack(k, carry):
            span = pl.ds(pl.multiple_of(k * piece, piece), piece)
            plane_out[k, :piece, :] = items[core, span, :] + core_in[span, :]
            plane_out[k, piece:, :LANES] = pair_loss
            plane_out[k, piece:, LANES:] = jnp.zeros((8, width - LANES), F32)
            return carry

        lax.fori_loop(0, chips, pack, 0)
        for step in chip_steps:
            remote(
                plane_out.at[(chip + step) % chips],
                plane_in.at[chip],
                x_sems.at[2],
                x_sems.at[3],
                chip_peer(step),
            ).start()
        plane_in[chip] = plane_out[chip]

    def piece_at(half_index, index):
        start = half_index * half_cols + index % chips * piece
        return pl.ds(pl.multiple_of(start, piece), piece)

    def plane_sum():
        wait_bytes(plane_in.at[pl.ds(0, chips - 1)], x_sems.at[3])
        total = plane_in[0]
        for k in range(1, chips):
            total = total + plane_in[k]
        here = ig_ref.at[piece_at(core, chip), :]
        here[...] = total[:piece, :]
        for step in chip_steps:
            remote(
                here, here, x_sems.at[4], back_sems.at[step - 1], chip_peer(step)
            ).start()
        remote(here, here, x_sems.at[5], x_sems.at[6], (twin, ring)).start()
        return total[piece : piece + 8, :LANES]

    def loss_send(total):
        z_loss[ring] = jnp.broadcast_to(item_loss - total[1:2, :], (8, LANES))
        for step in z_steps:
            remote(
                z_loss.at[ring], z_loss.at[ring], l_sems.at[0], l_sems.at[1], z_peer(step)
            ).start()

    def forward(step):
        here = ig_ref.at[piece_at(core, chip + chips - step), :]
        wait_bytes(here, back_sems.at[step - 1])
        remote(here, here, x_sems.at[5], x_sems.at[6], (twin, ring)).start()

    others = pl.ds(0, (chips - 1) * piece)

    def loss_end(users):
        wait_bytes(z_loss.at[pl.ds(0, rings - 1)], l_sems.at[1])
        total = users
        for k in range(rings):
            total = total + z_loss[k, 0:1, :]
        loss_ref[0, 0] = jnp.sum(total) * (1.0 / total_users)

    core_send()
    item_part(core)
    hub_sum(0)
    plane_send()
    hub_sum(1)
    own_sum(0)
    own_sum(1)
    plane_total = plane_sum()
    hub_spread(0)
    loss_send(plane_total)
    hub_spread(1)
    for step in chip_steps:
        forward(step)
    loss_end(plane_total[0:1, :])

    def half_out(which):
        span = pl.ds(pl.multiple_of(which * half_cols, half_cols), half_cols)
        return pltpu.make_async_copy(ig_ref.at[span, :], ig_hbm.at[span, :], out_sems.at[which])

    half_out(core).start()
    gather_end()
    user_out = pltpu.make_async_copy(ug_ref, ug_hbm, out_sems.at[2])
    user_out.start()
    wait_bytes(ig_ref.at[pl.ds(0, half_cols), :], x_sems.at[6])
    half_out(other).start()

    wait_bytes(z_stats.at[pl.ds(0, rings - 1)], z_sems.at[0])
    wait_bytes(p_stats.at[pl.ds(0, chips - 1)], p_sems.at[0])
    wait_bytes(z_loss.at[pl.ds(0, rings - 1)], l_sems.at[0])
    wait_bytes(hub_in, w_sems.at[0])
    wait_bytes(near_in, w_sems.at[1])
    wait_bytes(ug_ref.at[pl.ds(0, (rings - 1) * strip), :], w_sems.at[2])
    wait_bytes(core_in, x_sems.at[0])
    wait_bytes(plane_in.at[pl.ds(0, chips - 1)], x_sems.at[2])
    wait_bytes(ig_ref.at[others, :], x_sems.at[4])
    wait_bytes(ig_ref.at[pl.ds(0, half_cols), :], x_sems.at[5])
    half_out(core).wait()
    user_out.wait()
    half_out(other).wait()


def copy_out(ug_in, ig_in, ug_out, ig_out, ug_here, ig_here, sems):
    loads = []
    stores = []
    for source, here, target, count in (
        (ug_in, ug_here, ug_out, 2),
        (ig_in, ig_here, ig_out, 4),
    ):
        rows = source.shape[0] // count
        for k in range(count):
            span = pl.ds(k * rows, rows)
            slot = len(loads)
            loads.append(
                pltpu.make_async_copy(source.at[span, :], here.at[span, :], sems.at[0, slot])
            )
            stores.append(
                pltpu.make_async_copy(here.at[span, :], target.at[span, :], sems.at[1, slot])
            )
    for load in loads:
        load.start()
    for load, store in zip(loads, stores):
        load.wait()
        store.start()
    for store in stores:
        store.wait()


def per_device(total_users, chips, rings, user_embed, item_embed, positive, user_count, item_count):
    rows, width = user_embed.shape
    cols = item_embed.shape[0]
    tiles = cols // LANES
    strip = rows // rings
    direct = rings // 8
    sub = strip // PARTS
    hub_rows = (2 * direct if rings > 8 else 1) * sub + sub // 2
    piece = cols // 2 // chips
    vmem = pl.BlockSpec(memory_space=pltpu.VMEM)
    hbm = pl.BlockSpec(memory_space=pltpu.HBM)
    dma = pltpu.SemaphoreType.DMA
    user_grad, item_grad, loss = pl.pallas_call(
        functools.partial(kernel, total_users, chips, rings),
        out_shape=(
            jax.ShapeDtypeStruct((rows, width), F32),
            jax.ShapeDtypeStruct((cols, width), F32),
            jax.ShapeDtypeStruct((1, 1), F32),
        ),
        in_specs=[hbm] * 2 + [vmem] * 3,
        out_specs=(hbm, hbm, pl.BlockSpec(memory_space=pltpu.SMEM)),
        scratch_shapes=[
            pltpu.VMEM((rows, width), F32),
            pltpu.VMEM((cols, width), F32),
            pltpu.VMEM((rows, width), user_embed.dtype),
            pltpu.VMEM((cols, width), item_embed.dtype),
            pltpu.VMEM((rows, width), user_embed.dtype),
            pltpu.VMEM((rows, cols), F32),
            pltpu.VMEM((rows, cols), F32),
            pltpu.VMEM((rows, cols), F32),
            pltpu.VMEM((2, rows, cols // 2), jnp.bfloat16),
            pltpu.VMEM((rows, width), F32),
            pltpu.VMEM((2, cols // 2 + 8, width), F32),
            pltpu.VMEM((tiles, LANES), F32),
            pltpu.VMEM((rows, LANES), F32),
            pltpu.VMEM((rows, LANES), F32),
            pltpu.VMEM((rows, LANES), F32),
            pltpu.VMEM((tiles, 8, LANES), F32),
            pltpu.VMEM((tiles, 8, LANES), F32),
            pltpu.VMEM((tiles, 8, LANES), F32),
            pltpu.VMEM((rings, rows // LANES, LANES), F32),
            pltpu.VMEM((2, 2 * tiles, LANES), F32),
            pltpu.VMEM((chips, 2 * tiles, LANES), F32),
            pltpu.VMEM((rings, 8, LANES), F32),
            pltpu.VMEM((PARTS, 2, hub_rows, width), F32),
            pltpu.VMEM((PARTS, 2 * direct + 2, sub, width), F32),
            pltpu.VMEM((cols // 2 + 8, width), F32),
            pltpu.VMEM((chips, piece + 8, width), F32),
            pltpu.VMEM((chips, piece + 8, width), F32),
            dma((2,)),
            dma((2,)),
            dma((2,)),
            dma((4,)),
            dma((4,)),
            dma((PARTS, 2)),
            dma((PARTS,)),
            dma((PARTS, 2)),
            dma((8,)),
            dma((chips - 1,)),
            dma((2,)),
            dma((3,)),
        ],
        compiler_params=pltpu.CompilerParams(
            collective_id=0, has_side_effects=True, vmem_limit_bytes=60 * 1024 * 1024
        ),
        name="two_sided",
    )(
        user_embed,
        item_embed,
        positive.reshape(rows // LANES, LANES),
        user_count.reshape(rows // LANES, LANES),
        item_count.reshape(tiles, LANES),
    )
    user_grad, item_grad = pl.pallas_call(
        copy_out,
        out_shape=(
            jax.ShapeDtypeStruct((rows, width), F32),
            jax.ShapeDtypeStruct((cols, width), F32),
        ),
        in_specs=[hbm] * 2,
        out_specs=(hbm, hbm),
        scratch_shapes=[
            pltpu.VMEM((rows, width), F32),
            pltpu.VMEM((cols, width), F32),
            dma((2, 6)),
        ],
        compiler_params=pltpu.CompilerParams(vmem_limit_bytes=60 * 1024 * 1024),
        name="copy_out",
    )(user_grad, item_grad)
    return user_grad, item_grad, loss.reshape(())


def solution(mesh):
    row_size, rings = mesh.shape["row"], mesh.shape["col"]

    def whole(user_embed, *others):
        body = functools.partial(per_device, user_embed.shape[0], row_size // 2, rings)
        return jax.shard_map(
            body,
            mesh=mesh,
            in_specs=(P("row", None), P("col", None), P("row"), P("row"), P("col")),
            out_specs=(P("row", None), P("col", None), P()),
            check_vma=False,
        )(user_embed, *others)

    return whole
```
